32 devices in a mesh: head: 4 (over x, core), blk: 8 (over z, y).
Axes of the slice: x: 2, y: 2, z: 4, core: 2. Of those that a mesh axis runs over, the one named last changes fastest.
Arguments:
- inputs: bfloat16 [2, 2048, 768], P(None, ('head', 'blk')), may hold values from -6 to 6
- doc_lengths: int32 [2, 32], replicated, may hold values from 1 to 1024, 2048 in all within a row
- grad_out: bfloat16 [2, 2048, 768], P(None, ('head', 'blk')), may hold values from -6 to 6
- qkv_weight: bfloat16 [3, 768, 768], P(None, ('head', 'blk')), may hold values from -0.21875 to 0.21875
- out_weight: bfloat16 [768, 768], P(('head', 'blk')), may hold values from -1.75 to 1.75
- inner_weight: bfloat16 [768, 3072], P(('head', 'blk')), may hold values from -0.21875 to 0.21875
- outer_weight: bfloat16 [3072, 768], P(('head', 'blk')), may hold values from -0.109375 to 0.109375
- bias_rows: bfloat16 [4, 768], P(None, ('head', 'blk')), may hold values from -3 to 3
- inner_bias: bfloat16 [3072], P(('head', 'blk')), may hold values from -3 to 3
- norm_gains: bfloat16 [2, 768], P(None, ('head', 'blk')), may hold values from 0.5 to 1.5
- norm_shifts: bfloat16 [2, 768], P(None, ('head', 'blk')), may hold values from -3 to 3
Outputs:
- output: bfloat16 [2, 2048, 768], P(None, ('head', 'blk'))
- grad_inputs: bfloat16 [2, 2048, 768], P(None, ('head', 'blk'))
- grad_qkv_weight: float32 [3, 768, 768], P(None, ('head', 'blk'))
- grad_out_weight: float32 [768, 768], P(('head', 'blk'))
- grad_inner_weight: float32 [768, 3072], P(('head', 'blk'))
- grad_outer_weight: float32 [3072, 768], P(('head', 'blk'))
- grad_bias_rows: float32 [4, 768], P(None, ('head', 'blk'))
- grad_inner_bias: float32 [3072], P(('head', 'blk'))
- grad_norm_gains: float32 [2, 768], P(None, ('head', 'blk'))
- grad_norm_shifts: float32 [2, 768], P(None, ('head', 'blk'))
The draws below stay inside these ranges and needn't reach their ends.
Inputs may be any that keep to these rules, and one draw needn't show every extreme that they name: `doc_lengths`: each row lists, in order, the lengths of the 32 documents packed into one micro-batch's sequence; a row sums to 2048, and its longest document has exactly half of 2048 tokens.
All inputs are finite; a program needn't handle non-finite values.
Results may differ from the reference program's by a relative error of at most 0.017.
Values may be sent and summed in bfloat16 or wider, within the bound.
No kernel may reach another device: no remote copies, remote signals or barrier semaphores. Data moves between devices by JAX's collectives and lax.ppermute only.
A program may use at most 256 MiB of HBM per device.

```python
import math
from functools import partial
import jax
import jax.numpy as jnp
import numpy as np
from jax import lax

D = 768
HEADS = 12
FF = 3072
MB = 2
NDOC = 32
SEQ = 2048


def block_levels(rng, shape, shards, least, largest):
    factor_of, own = 1.0, jax.random.fold_in(rng, 6)
    for dim, blocks in shards:
        steps = jnp.exp(jax.random.uniform(jax.random.fold_in(own, dim), (blocks,), jnp.float32, least / len(shards), largest / len(shards)))
        factor_of = factor_of * jnp.repeat(steps, shape[dim] // blocks).reshape([-1 if axis == dim else 1 for axis in range(len(shape))])
    return factor_of


def profile(amount, total, reach, lean):
    loads = [(1 << 20) // math.isqrt(grade ** lean) + 1 for grade in range(2, amount + 1)]
    rest, given = total - reach - (amount - 1), [1] * (amount - 1)
    while rest > 0:
        movable = [i for i in range(amount - 1) if given[i] < reach]
        mass, remaining = sum([loads[i] for i in movable]), rest
        for i in movable:
            extra = min(reach - given[i], max(1, remaining * loads[i] // mass), rest)
            given[i] = given[i] + extra
            rest = rest - extra
    return np.array([reach] + given)


def uneven(key, amount, total, limit, slope):
    if amount == 2:
        one = jax.random.randint(key, (), max(1, total - limit), min(limit, total - 1) + 1)
        return jnp.stack([one, total - one])
    tallies = jnp.asarray(profile(amount, total, limit, slope), jnp.int32)
    pairs = (amount - 1) // 2
    donor, sink = tallies[1:1 + 2 * pairs:2], tallies[2:2 + 2 * pairs:2]
    margin = jnp.minimum(donor - 1, limit - sink)
    shifted = jax.random.randint(jax.random.fold_in(key, 1), (pairs,), 0, 1 << 20) % (margin + 1)
    tallies = tallies.at[1:1 + 2 * pairs:2].set(donor - shifted).at[2:2 + 2 * pairs:2].set(sink + shifted)
    return tallies[jax.random.permutation(jax.random.fold_in(key, 2), amount)]


def bell_draw(rng, extent, scale, reach, split=(), kind=jnp.bfloat16):
    array = scale * jax.random.normal(rng, extent, jnp.float32)
    if split:
        array = array * block_levels(rng, extent, split, -0.22, 0.18)
    return jnp.clip(array, -reach, reach).astype(kind)


def setup_inputs(seed: int = 0) -> dict:
    streams_of = jax.random.split(jax.random.key(seed), 12)
    inputs = bell_draw(streams_of[0], (MB, SEQ, D), 1.0, 6.0, ((1, 32),))
    doc_lengths = jax.vmap(lambda own: uneven(own, NDOC, SEQ, SEQ // 2, 2))(jax.random.split(streams_of[1], MB)).reshape((MB, NDOC)).astype(jnp.int32)
    grad_out = bell_draw(streams_of[2], (MB, SEQ, D), 1.0, 6.0, ((1, 32),))
    qkv_weight = bell_draw(streams_of[3], (3, D, D), D ** -0.5, 0.21875, ((1, 32),))
    out_weight = bell_draw(streams_of[4], (D, D), (D // 64) ** -0.5, 1.75, ((0, 32),))
    inner_weight = bell_draw(streams_of[5], (D, FF), D ** -0.5, 0.21875, ((0, 32),))
    outer_weight = bell_draw(streams_of[6], (FF, D), FF ** -0.5, 0.109375, ((0, 32),))
    bias_rows = bell_draw(streams_of[7], (4, D), 0.5, 3.0, ((1, 32),))
    inner_bias = bell_draw(streams_of[8], (FF,), 0.5, 3.0, ((0, 32),))
    norm_gains = jnp.clip(1.0 + 0.1 * jax.random.normal(streams_of[9], (2, D), jnp.float32), 0.5, 1.5).astype(jnp.bfloat16)
    norm_shifts = bell_draw(streams_of[10], (2, D), 0.5, 3.0, ((1, 32),))
    return {"inputs": inputs, "doc_lengths": doc_lengths, "grad_out": grad_out, "qkv_weight": qkv_weight, "out_weight": out_weight, "inner_weight": inner_weight, "outer_weight": outer_weight, "bias_rows": bias_rows, "inner_bias": inner_bias, "norm_gains": norm_gains, "norm_shifts": norm_shifts}


norm_eps = 1e-12
masked_score = -1e+30
highest = lax.Precision.HIGHEST

@jax.custom_vjp
def low(v):
    return lax.optimization_barrier(v.astype(jnp.bfloat16)).astype(jnp.float32)

@jax.custom_vjp
def low_back(v):
    return v

def low_keep(v):
    return (low(v), None)

def low_pass(kept, grad):
    return (grad,)

def back_keep(v):
    return (v, None)

def back_low(kept, grad):
    return (low(grad),)
low.defvjp(low_keep, low_pass)
low_back.defvjp(back_keep, back_low)

def layer_norm(hidden, norm_gain, norm_shift):
    center = hidden - lax.optimization_barrier(jnp.mean(hidden, axis=-1, keepdims=True))
    spread = lax.optimization_barrier(jnp.mean(center * center, axis=-1, keepdims=True))
    return center * lax.rsqrt(spread + norm_eps) * norm_gain + norm_shift

def doc_index(positions, lengths):
    bounds = jnp.cumsum(lengths).astype(jnp.int32)
    return lax.optimization_barrier(jnp.sum((positions[:, None] >= bounds[None, :]).astype(jnp.int32), axis=1)).astype(jnp.int32)

def matmul(left_side, right_side):
    return jnp.dot(left_side, right_side, precision=highest, preferred_element_type=jnp.float32)

def attend_rows(batch_item, key_rows, values, key_docs, score_scale):
    queries, query_docs = batch_item
    scores = jnp.einsum('qhd,khd->hqk', queries, key_rows, precision=highest) * score_scale
    scores = low_back(scores)
    same_doc = (query_docs[:, None] == key_docs[None, :])[None]
    scores = jnp.where(same_doc, scores, masked_score)
    attn_prob = jax.nn.softmax(scores, axis=-1)
    return jnp.einsum('hqk,khd->qhd', low(attn_prob), values, precision=highest)

def forward(params, inputs, doc_ids):
    qkv_weight, out_weight, inner_weight, outer_weight, bias_rows, inner_bias, norm_gains, norm_shifts = params
    length = inputs.shape[0]
    head_dim = D // HEADS
    score_scale = 1.0 / math.sqrt(head_dim)
    zero_row = jnp.zeros((D,), jnp.float32)
    qkv_bias = jnp.stack([bias_rows[0], zero_row, bias_rows[1]])
    projected = jnp.einsum('td,cde->tce', inputs, qkv_weight, precision=highest) + qkv_bias[None]
    projected = low_back(low(projected))
    queries = projected[:, 0].reshape(length, HEADS, head_dim)
    key_rows = projected[:, 1].reshape(length, HEADS, head_dim)
    values = projected[:, 2].reshape(length, HEADS, head_dim)
    block_rows = 512 if length % 512 == 0 else length
    block_count = length // block_rows
    attend = jax.checkpoint(partial(attend_rows, key_rows=key_rows, values=values, key_docs=doc_ids, score_scale=score_scale))
    attended = lax.map(attend, (queries.reshape(block_count, block_rows, HEADS, head_dim), doc_ids.reshape(block_count, block_rows)))
    attended = low_back(low(attended.reshape(length, D)))
    branch = low_back(matmul(attended, out_weight) + bias_rows[2])
    first_sum = inputs + branch
    first_normed = layer_norm(first_sum, norm_gains[0], norm_shifts[0])
    inner_pre = low_back(matmul(low(first_normed), inner_weight) + inner_bias)
    activated = low(jax.nn.gelu(inner_pre, approximate=False))
    ffn_branch = low_back(matmul(activated, outer_weight) + bias_rows[3])
    return layer_norm(first_normed + ffn_branch, norm_gains[1], norm_shifts[1])

def reference(inputs, doc_lengths, grad_out, qkv_weight, out_weight, inner_weight, outer_weight, bias_rows, inner_bias, norm_gains, norm_shifts):
    params = tuple((weight.astype(jnp.float32) for weight in (qkv_weight, out_weight, inner_weight, outer_weight, bias_rows, inner_bias, norm_gains, norm_shifts)))
    length = inputs.shape[1]
    positions = jnp.arange(length, dtype=jnp.int32)

    def micro_step(totals, batch_item):
        tokens, lengths, cotangent = batch_item
        doc_ids = doc_index(positions, lengths)
        result, pullback = jax.vjp(lambda weights, token_rows: forward(weights, token_rows, doc_ids), params, tokens.astype(jnp.float32))
        weight_grads, input_grad = pullback(cotangent.astype(jnp.float32))
        totals = jax.tree.map(lambda first_term, second_term: first_term + second_term, totals, weight_grads)
        return (totals, (result.astype(jnp.bfloat16), input_grad.astype(jnp.bfloat16)))
    zero_grads = jax.tree.map(jnp.zeros_like, params)
    totals, (output, grad_inputs) = lax.scan(micro_step, zero_grads, (inputs, doc_lengths, grad_out))
    return (output, grad_inputs, totals[0], totals[1], totals[2], totals[3], totals[4], totals[5], totals[6], totals[7])
```

```python
import math

import jax
import jax.numpy as jnp
from jax import lax
from jax.sharding import PartitionSpec as P

D = 768
HEADS = 12
FF = 3072
MB = 2


norm_eps = 1e-12
masked_score = -1e30


def layer_norm(hidden, norm_gain, norm_shift):
    center = hidden - jnp.mean(hidden, axis=-1, keepdims=True)
    spread = jnp.mean(center * center, axis=-1, keepdims=True)
    return center * lax.rsqrt(spread + norm_eps) * norm_gain + norm_shift


def exact_gelu(pre_act):
    return jax.nn.gelu(pre_act, approximate=False)


def doc_index(positions, lengths):
    order = jnp.arange(lengths.shape[0], dtype=jnp.int32)
    bounds = jnp.sum(jnp.where(order[None, :] <= order[:, None], lengths[None, :], 0), axis=1)
    return jnp.sum((positions[:, None] >= bounds[None, :]).astype(jnp.int32), axis=1)


def row_positions(indices, width, quarter, tokens_dev):
    block_index = indices // width
    inner_row = indices % width
    return inner_row // tokens_dev * quarter + block_index * tokens_dev + inner_row % tokens_dev


def collect(
    qkv_weight,
    out_weight,
    inner_weight,
    outer_weight,
    bias_rows,
    inner_bias,
    norm_gains,
    norm_shifts,
):
    return (
        lax.all_gather(qkv_weight, ("head", "blk"), axis=1, tiled=True),
        lax.all_gather(out_weight, ("head", "blk"), axis=0, tiled=True),
        lax.all_gather(inner_weight, ("head", "blk"), axis=0, tiled=True),
        lax.all_gather(outer_weight, ("head", "blk"), axis=0, tiled=True),
        lax.all_gather(bias_rows, ("head", "blk"), axis=1, tiled=True),
        lax.all_gather(inner_bias, ("head", "blk"), axis=0, tiled=True),
        lax.all_gather(norm_gains, ("head", "blk"), axis=1, tiled=True),
        lax.all_gather(norm_shifts, ("head", "blk"), axis=1, tiled=True),
    )


def fold_block(state, query_rows, query_docs, key_rows, value_rows, key_docs, score_scale):
    running_max, running_sum, running_out = state
    scores = (
        jnp.einsum("qhd,khd->hqk", query_rows, key_rows, preferred_element_type=jnp.float32)
        * score_scale
    )
    same_doc = (query_docs[:, None] == key_docs[None, :])[None]
    scores = jnp.where(same_doc, scores, masked_score)
    new_max = jnp.maximum(running_max, jnp.max(scores, axis=-1))
    attn_prob = jnp.where(same_doc, jnp.exp(scores - new_max[:, :, None]), 0.0)
    factor = jnp.exp(running_max - new_max)
    running_sum = running_sum * factor + jnp.sum(attn_prob, axis=-1)
    update = jnp.einsum(
        "hqk,khd->qhd",
        attn_prob.astype(jnp.bfloat16),
        value_rows,
        preferred_element_type=jnp.float32,
    )
    running_out = running_out * factor.T[:, :, None] + update
    return (new_max, running_sum, running_out)


def grad_block(
    query_rows,
    grad_rows,
    lse_rows,
    delta_rows,
    query_docs,
    key_rows,
    value_rows,
    key_docs,
    score_scale,
):
    scores = (
        jnp.einsum("qhd,khd->hqk", query_rows, key_rows, preferred_element_type=jnp.float32)
        * score_scale
    )
    same_doc = (query_docs[:, None] == key_docs[None, :])[None]
    attn_prob = jnp.where(
        same_doc, jnp.exp(jnp.where(same_doc, scores, masked_score) - lse_rows[:, :, None]), 0.0
    )
    grad_values = jnp.einsum(
        "hqk,qhd->khd",
        attn_prob.astype(jnp.bfloat16),
        grad_rows,
        preferred_element_type=jnp.float32,
    )
    grad_prob = jnp.einsum(
        "qhd,khd->hqk", grad_rows, value_rows, preferred_element_type=jnp.float32
    )
    grad_scores = (attn_prob * (grad_prob - delta_rows[:, :, None])).astype(jnp.bfloat16)
    grad_queries = (
        jnp.einsum("hqk,khd->qhd", grad_scores, key_rows, preferred_element_type=jnp.float32)
        * score_scale
    )
    grad_keys = (
        jnp.einsum("hqk,qhd->khd", grad_scores, query_rows, preferred_element_type=jnp.float32)
        * score_scale
    )
    return (grad_queries, grad_keys, grad_values)


def local(
    inputs,
    doc_lengths,
    grad_out,
    qkv_weight,
    out_weight,
    inner_weight,
    outer_weight,
    bias_rows,
    inner_bias,
    norm_gains,
    norm_shifts,
):
    tokens_dev = inputs.shape[1]
    groups = lax.axis_size("head")
    cycle_size = lax.axis_size("blk")
    width = groups * tokens_dev
    quarter = cycle_size * tokens_dev
    heads_dev = HEADS // groups
    head_dim = D // HEADS
    group_width = heads_dev * head_dim
    score_scale = 1.0 / math.sqrt(head_dim)
    own_index = lax.axis_index("blk") * width + jnp.arange(width, dtype=jnp.int32)
    own_positions = row_positions(own_index, width, quarter, tokens_dev)
    step_rows = 2 * width
    step_count = cycle_size * width // step_rows
    all_positions = row_positions(
        jnp.arange(cycle_size * width, dtype=jnp.int32), width, quarter, tokens_dev
    )
    totals = [
        jnp.zeros((3, D, D), jnp.float32),
        jnp.zeros((D, D), jnp.float32),
        jnp.zeros((D, FF), jnp.float32),
        jnp.zeros((FF, D), jnp.float32),
        jnp.zeros((4, D), jnp.float32),
        jnp.zeros((FF,), jnp.float32),
        jnp.zeros((2, D), jnp.float32),
        jnp.zeros((2, D), jnp.float32),
    ]
    outputs_list = []
    grads_list = []
    for micro in range(MB):
        forward_weights = collect(
            qkv_weight,
            out_weight,
            inner_weight,
            outer_weight,
            bias_rows,
            inner_bias,
            norm_gains,
            norm_shifts,
        )
        fwd_qkv, fwd_out, fwd_inner, fwd_outer, fwd_bias, fwd_ibias, fwd_gains, fwd_shifts = (
            forward_weights
        )
        lengths = doc_lengths[micro]
        own_docs = doc_index(own_positions, lengths)
        all_docs = doc_index(all_positions, lengths).reshape(step_count, step_rows)
        token_rows = inputs[micro]
        bias_float = fwd_bias.astype(jnp.float32)
        zero_row = jnp.zeros((D,), jnp.float32)
        qkv_bias = (
            jnp.stack([bias_float[0], zero_row, bias_float[1]])
            .reshape(3, groups, group_width)
            .transpose(1, 0, 2)
        )
        projected = (
            jnp.einsum(
                "td,cdgf->tgcf",
                token_rows,
                fwd_qkv.reshape(3, D, groups, group_width),
                preferred_element_type=jnp.float32,
            )
            + qkv_bias[None]
        )
        projected = projected.astype(jnp.bfloat16).reshape(tokens_dev, groups, 3 * group_width)
        by_heads = lax.all_to_all(
            projected, "head", split_axis=1, concat_axis=0, tiled=True
        ).reshape(width, 3 * group_width)
        query_flat = by_heads[:, :group_width]
        query_rows = query_flat.reshape(width, heads_dev, head_dim)
        kv_rows = by_heads[:, group_width:]
        start_state = (
            jnp.full((heads_dev, width), masked_score, jnp.float32),
            jnp.zeros((heads_dev, width), jnp.float32),
            jnp.zeros((width, heads_dev, head_dim), jnp.float32),
        )
        state = start_state
        piece = lax.all_gather(kv_rows, "blk", axis=0, tiled=True)
        piece_rows = piece.shape[0]
        part_count = piece_rows // width
        parts = piece.reshape(part_count, width, 2, heads_dev, head_dim)
        part_index = jnp.arange(piece_rows, dtype=jnp.int32).reshape(part_count, width)

        def one_part(carry, part_item):
            part_kv, index_rows = part_item
            key_docs = doc_index(row_positions(index_rows, width, quarter, tokens_dev), lengths)
            return (
                fold_block(
                    carry, query_rows, own_docs, part_kv[:, 0], part_kv[:, 1], key_docs, score_scale
                ),
                None,
            )

        state, unused = lax.scan(one_part, state, (parts, part_index))
        run_max, run_sum, run_out = state
        log_sum = run_max + jnp.log(run_sum)
        attn_full = run_out / run_sum.T[:, :, None]
        attn_low = attn_full.astype(jnp.bfloat16).reshape(width, 1, group_width)
        attn_tokens = lax.all_to_all(
            attn_low, "head", split_axis=0, concat_axis=1, tiled=True
        ).reshape(tokens_dev, D)
        gains_fwd = fwd_gains.astype(jnp.float32)
        shifts_fwd = fwd_shifts.astype(jnp.float32)
        branch = jnp.dot(attn_tokens, fwd_out, preferred_element_type=jnp.float32) + bias_float[2]
        first_sum = token_rows.astype(jnp.float32) + branch
        first_normed, pull_first = jax.vjp(layer_norm, first_sum, gains_fwd[0], shifts_fwd[0])
        normed_low = first_normed.astype(jnp.bfloat16)
        inner_pre = jnp.dot(
            normed_low, fwd_inner, preferred_element_type=jnp.float32
        ) + fwd_ibias.astype(jnp.float32)
        activated, pull_gelu = jax.vjp(exact_gelu, inner_pre)
        act_low = activated.astype(jnp.bfloat16)
        second_sum = (
            first_normed
            + jnp.dot(act_low, fwd_outer, preferred_element_type=jnp.float32)
            + bias_float[3]
        )
        layer_out, pull_second = jax.vjp(layer_norm, second_sum, gains_fwd[1], shifts_fwd[1])
        outputs_list.append(layer_out.astype(jnp.bfloat16))
        back_weights = collect(
            qkv_weight,
            out_weight,
            inner_weight,
            outer_weight,
            bias_rows,
            inner_bias,
            norm_gains,
            norm_shifts,
        )
        (
            back_qkv,
            back_out,
            back_inner,
            back_outer,
            back_bias,
            back_ibias,
            back_gains,
            back_shifts,
        ) = back_weights
        d_second, d_gain_two, d_shift_two = pull_second(grad_out[micro].astype(jnp.float32))
        d_ffn = d_second.astype(jnp.bfloat16)
        outer_grad = jnp.einsum("tf,td->fd", act_low, d_ffn, preferred_element_type=jnp.float32)
        ffn_bias_grad = jnp.sum(d_ffn.astype(jnp.float32), axis=0)
        d_hidden = jnp.einsum("td,fd->tf", d_ffn, back_outer, preferred_element_type=jnp.float32)
        d_inner = pull_gelu(d_hidden)[0].astype(jnp.bfloat16)
        inner_grad = jnp.einsum(
            "td,tf->df", normed_low, d_inner, preferred_element_type=jnp.float32
        )
        inner_bias_grad = jnp.sum(d_inner.astype(jnp.float32), axis=0)
        d_first_normed = d_second + jnp.einsum(
            "tf,df->td", d_inner, back_inner, preferred_element_type=jnp.float32
        )
        d_first, d_gain_one, d_shift_one = pull_first(d_first_normed)
        d_branch = d_first.astype(jnp.bfloat16)
        out_grad = jnp.einsum(
            "te,td->ed", attn_tokens, d_branch, preferred_element_type=jnp.float32
        )
        branch_bias_grad = jnp.sum(d_branch.astype(jnp.float32), axis=0)
        d_attn = jnp.einsum(
            "td,ed->te", d_branch, back_out, preferred_element_type=jnp.float32
        ).astype(jnp.bfloat16)
        grad_heads = lax.all_to_all(
            d_attn.reshape(tokens_dev, groups, group_width),
            "head",
            split_axis=1,
            concat_axis=0,
            tiled=True,
        ).reshape(width, heads_dev, head_dim)
        delta_rows = jnp.sum(grad_heads.astype(jnp.float32) * attn_full, axis=-1).T
        kv_all = lax.all_gather(kv_rows, "blk", axis=0, tiled=True).reshape(
            step_count, step_rows, 2, heads_dev, head_dim
        )

        def key_step(grad_query, key_item):
            part_kv, part_docs = key_item
            grad_queries, grad_keys, grad_values = grad_block(
                query_rows,
                grad_heads,
                log_sum,
                delta_rows,
                own_docs,
                part_kv[:, 0],
                part_kv[:, 1],
                part_docs,
                score_scale,
            )
            return (grad_query + grad_queries, jnp.stack([grad_keys, grad_values], axis=1))

        grad_query, kv_terms = lax.scan(
            key_step, jnp.zeros((width, heads_dev, head_dim), jnp.float32), (kv_all, all_docs)
        )
        kv_home = lax.psum_scatter(
            kv_terms.reshape(cycle_size * width, 2 * group_width),
            "blk",
            scatter_dimension=0,
            tiled=True,
        )
        grad_q_low = grad_query.reshape(width, group_width).astype(jnp.bfloat16)
        grad_kv_low = kv_home.astype(jnp.bfloat16)
        back_rows = jnp.concatenate([grad_q_low, grad_kv_low], axis=1).reshape(
            width, 1, 3 * group_width
        )
        home_grads = lax.all_to_all(
            back_rows, "head", split_axis=0, concat_axis=1, tiled=True
        ).reshape(tokens_dev, groups, 3, group_width)
        qkv_grad = jnp.einsum(
            "td,tgcf->cdgf", token_rows, home_grads, preferred_element_type=jnp.float32
        ).reshape(3, D, D)
        column_sums = jnp.sum(home_grads.astype(jnp.float32), axis=0)
        query_bias_grad = column_sums[:, 0].reshape(D)
        value_bias_grad = column_sums[:, 2].reshape(D)
        grad_tokens = d_first + jnp.einsum(
            "tgcf,cdgf->td",
            home_grads,
            back_qkv.reshape(3, D, groups, group_width),
            preferred_element_type=jnp.float32,
        )
        grads_list.append(grad_tokens.astype(jnp.bfloat16))
        totals[0] = totals[0] + qkv_grad
        totals[1] = totals[1] + out_grad
        totals[2] = totals[2] + inner_grad
        totals[3] = totals[3] + outer_grad
        totals[4] = totals[4] + jnp.stack(
            [query_bias_grad, value_bias_grad, branch_bias_grad, ffn_bias_grad]
        )
        totals[5] = totals[5] + inner_bias_grad
        totals[6] = totals[6] + jnp.stack([d_gain_one, d_gain_two])
        totals[7] = totals[7] + jnp.stack([d_shift_one, d_shift_two])
    summed = (
        lax.psum_scatter(totals[0], ("head", "blk"), scatter_dimension=1, tiled=True),
        lax.psum_scatter(totals[1], ("head", "blk"), scatter_dimension=0, tiled=True),
        lax.psum_scatter(totals[2], ("head", "blk"), scatter_dimension=0, tiled=True),
        lax.psum_scatter(totals[3], ("head", "blk"), scatter_dimension=0, tiled=True),
        lax.psum_scatter(totals[4], ("head", "blk"), scatter_dimension=1, tiled=True),
        lax.psum_scatter(totals[5], ("head", "blk"), scatter_dimension=0, tiled=True),
        lax.psum_scatter(totals[6], ("head", "blk"), scatter_dimension=1, tiled=True),
        lax.psum_scatter(totals[7], ("head", "blk"), scatter_dimension=1, tiled=True),
    )
    return (
        jnp.stack(outputs_list),
        jnp.stack(grads_list),
        summed[0],
        summed[1],
        summed[2],
        summed[3],
        summed[4],
        summed[5],
        summed[6],
        summed[7],
    )


def solution(mesh):
    placed = (
        P(None, ("head", "blk"), None),
        P(),
        P(None, ("head", "blk"), None),
        P(None, ("head", "blk"), None),
        P(("head", "blk"), None),
        P(("head", "blk"), None),
        P(("head", "blk"), None),
        P(None, ("head", "blk")),
        P(("head", "blk")),
        P(None, ("head", "blk")),
        P(None, ("head", "blk")),
    )
    return jax.shard_map(
        local,
        mesh=mesh,
        in_specs=placed,
        out_specs=(
            P(None, ("head", "blk"), None),
            P(None, ("head", "blk"), None),
            P(None, ("head", "blk"), None),
            P(("head", "blk"), None),
            P(("head", "blk"), None),
            P(("head", "blk"), None),
            P(None, ("head", "blk")),
            P(("head", "blk")),
            P(None, ("head", "blk")),
            P(None, ("head", "blk")),
        ),
        check_vma=False,
    )
```

```python
import functools
import math

import jax
import jax.numpy as jnp
from jax import lax
from jax.experimental import pallas as pl
from jax.experimental.pallas import tpu as pltpu
from jax.sharding import PartitionSpec as P

HEADS = 12
F32 = jnp.float32
BF = jnp.bfloat16
NT = (((1,), (1,)), ((), ()))
NN = (((1,), (0,)), ((), ()))
TN = (((0,), (0,)), ((), ()))
LOG2E = math.log2(math.e)
BOTH = ("head", "blk")
norm_eps = 1e-12
masked_score = -1e30
VMEM = pl.BlockSpec(memory_space=pltpu.VMEM)
SMEM = pl.BlockSpec(memory_space=pltpu.SMEM)
PARAMS = pltpu.CompilerParams(vmem_limit_bytes=56 << 20)


def dot(a, b, dims):
    return lax.dot_general(a, b, dims, preferred_element_type=F32)


def cdiv(a, b):
    return -(-a // b)


def chunk_walk(place_ref, blocks, halves, per, tokens, visit):
    core, half = place_ref[0], place_ref[1]
    runs = halves // per
    for source in range(2):

        def one(n, carry, source=source):
            xh = n // (2 * runs)
            rel = n // runs % 2
            run = n % runs
            head = xh * 2 + (core if source == 0 else 1 - core)
            position = ((head * 2 + (rel ^ half)) * halves + run * per) * tokens
            rows = pl.ds(pl.multiple_of(rel * tokens, tokens), tokens)

            def load(ref):
                return jnp.concatenate(
                    [ref[xh * halves + run * per + k, rows, :] for k in range(per)], axis=0
                )

            visit(source, load, pl.multiple_of(position, per * tokens))
            return carry

        lax.fori_loop(0, 4 * runs, one, 0, unroll=4 * runs <= 4)


def project_kernel(
    place_ref, a_ref, b_ref, w_ref, bias_ref, q_ref, k_ref, v_ref, kt_ref, vt_ref, *, halves, per
):
    tokens = a_ref.shape[1] // 2

    def visit(source, load, position):
        x = load((a_ref, b_ref)[source])
        rows = pl.ds(position, per * tokens)
        for n, ref in enumerate((q_ref, k_ref, v_ref)):
            y = dot(x, w_ref[n], NN) + bias_ref[n]
            ref[rows, :] = y.astype(BF)
            if n:
                (kt_ref, vt_ref)[n - 1][:, rows] = y.T.astype(BF)

    chunk_walk(place_ref, a_ref.shape[0], halves, per, tokens, visit)


def project(place, a, b, w, bias, halves, per):
    length = 2 * a.shape[0] * a.shape[1]
    hd = w.shape[2]
    rows = jax.ShapeDtypeStruct((length, hd), BF)
    columns = jax.ShapeDtypeStruct((hd, length), BF)
    return pl.pallas_call(
        functools.partial(project_kernel, halves=halves, per=per),
        out_shape=(rows, rows, rows, columns, columns),
        in_specs=[SMEM] + [VMEM] * 4,
        out_specs=(VMEM,) * 5,
        compiler_params=PARAMS,
        name="project",
    )(place, a, b, w, bias)


def weight_grad_kernel(place_ref, a_ref, b_ref, gt_ref, out_ref, acc_ref, *, halves, per):
    tokens = a_ref.shape[1] // 2
    acc_ref[...] = jnp.zeros_like(acc_ref)

    def visit(source, load, position):
        x = load((a_ref, b_ref)[source])
        acc_ref[...] += dot(gt_ref[:, pl.ds(position, per * tokens)], x, NN)

    chunk_walk(place_ref, a_ref.shape[0], halves, per, tokens, visit)
    out_ref[...] = acc_ref[...].T.astype(BF)


def weight_grad(place, a, b, gt, halves, per):
    depth = a.shape[2]
    return pl.pallas_call(
        functools.partial(weight_grad_kernel, halves=halves, per=per),
        out_shape=jax.ShapeDtypeStruct((depth, gt.shape[0]), BF),
        in_specs=[SMEM] + [VMEM] * 3,
        out_specs=VMEM,
        scratch_shapes=[pltpu.VMEM((gt.shape[0], depth), F32)],
        compiler_params=PARAMS,
        name="weight_grad",
    )(place, a, b, gt)


def inside(first, start, stop, bk):
    key = first + lax.broadcasted_iota(jnp.int32, (bk, start.shape[1]), 0)
    return (key >= start) & (key < stop)


def attend_kernel(
    lo_ref, hi_ref, q_ref, k_ref, vt_ref, span_ref, out_ref, ot_ref, lse_ref, s_ref,
    *, bq, bk, pack
):
    length, hd = q_ref.shape
    factor = LOG2E / math.sqrt(hd)
    half = pack // 2

    def q_step(i, carry):
        qs = pl.ds(pl.multiple_of(i * bq, bq), bq)
        q = q_ref[qs, :]
        start, stop = span_ref[0:1, qs], span_ref[1:2, qs]
        lo, hi = lo_ref[i], hi_ref[i]

        def first(j, top):
            ks = pl.ds(pl.multiple_of(j * bk, bk), bk)
            s = dot(k_ref[ks, :], q, NT) * factor
            s = jnp.where(inside(j * bk, start, stop, bk), s, masked_score)
            s_ref[ks, :] = s
            return jnp.maximum(top, jnp.max(s.reshape(bk // 8, 8, bq), axis=0))

        top = lax.fori_loop(lo, hi, first, jnp.full((8, bq), masked_score, F32))
        peak = jnp.max(top, axis=0, keepdims=True)

        def second(j, state):
            total, acc = state
            ks = pl.ds(pl.multiple_of(j * bk, bk), bk)
            p = jnp.exp2(s_ref[ks, :] - peak)
            total = total + jnp.sum(p.reshape(bk // 8, 8, bq), axis=0)
            return total, acc + dot(vt_ref[:, ks], p.astype(BF), NN)

        total, acc = lax.fori_loop(
            lo, hi, second, (jnp.zeros((8, bq), F32), jnp.zeros((hd, bq), F32))
        )
        total = jnp.sum(total, axis=0, keepdims=True)
        out = acc / total
        ot_ref[:, qs] = out
        lse_ref[:, qs] = peak + jnp.log2(total)
        rows = out.T.astype(BF)
        for c in range(bq // pack):
            piece = rows[c * pack : (c + 1) * pack]
            out_ref[i * (bq // pack) + c] = jnp.concatenate([piece[:half], piece[half:]], axis=1)
        return carry

    lax.fori_loop(0, length // bq, q_step, 0)


def attend(lo, hi, q, k, vt, spans, pack, bq, bk):
    length, hd = q.shape
    return pl.pallas_call(
        functools.partial(attend_kernel, bq=bq, bk=bk, pack=pack),
        out_shape=(
            jax.ShapeDtypeStruct((length // pack, pack // 2, 2 * hd), BF),
            jax.ShapeDtypeStruct((hd, length), F32),
            jax.ShapeDtypeStruct((1, length), F32),
        ),
        in_specs=[SMEM, SMEM] + [VMEM] * 4,
        out_specs=(VMEM,) * 3,
        scratch_shapes=[pltpu.VMEM((length, bq), F32)],
        compiler_params=PARAMS,
        name="attend",
    )(lo, hi, q, k, vt, spans)


def attend_back_kernel(
    lo_ref, hi_ref, q_ref, k_ref, v_ref, kt_ref, ot_ref, lse_ref, do_ref, span_ref,
    out_ref, gt_ref, sums_ref, dq_ref, dk_ref, dv_ref, *, bq, bk, pack
):
    length, hd = q_ref.shape
    scale = 1.0 / math.sqrt(hd)
    factor = LOG2E * scale
    half = pack // 2
    dk_ref[...] = jnp.zeros_like(dk_ref)
    dv_ref[...] = jnp.zeros_like(dv_ref)

    def q_step(i, carry):
        qs = pl.ds(pl.multiple_of(i * bq, bq), bq)
        q = q_ref[qs, :]
        start, stop = span_ref[0:1, qs], span_ref[1:2, qs]
        pieces = []
        for c in range(bq // pack):
            piece = do_ref[i * (bq // pack) + c]
            pieces += [piece[:, :hd], piece[:, hd:]]
        do = jnp.concatenate(pieces, axis=0)
        delta = jnp.sum(do.astype(F32).T * ot_ref[:, qs], axis=0, keepdims=True)
        lse = lse_ref[:, qs]

        def step(j, acc):
            ks = pl.ds(pl.multiple_of(j * bk, bk), bk)
            s = dot(k_ref[ks, :], q, NT) * factor - lse
            p = jnp.where(inside(j * bk, start, stop, bk), jnp.exp2(s), 0.0)
            dp = dot(v_ref[ks, :], do, NT)
            ds = (p * (dp - delta)).astype(BF)
            dv_ref[ks, :] += dot(p.astype(BF), do, NN)
            dk_ref[ks, :] += dot(ds, q, NN)
            return acc + dot(kt_ref[:, ks], ds, NN)

        acc = lax.fori_loop(lo_ref[i], hi_ref[i], step, jnp.zeros((hd, bq), F32))
        dq_ref[:, qs] = acc
        return carry

    lax.fori_loop(0, length // bq, q_step, 0)

    def emit(i, sums):
        rows = pl.ds(pl.multiple_of(i * bq, bq), bq)
        dqt = (dq_ref[:, rows] * scale).astype(BF)
        dk = (dk_ref[rows, :] * scale).astype(BF)
        dv = dv_ref[rows, :].astype(BF)
        dq = dqt.astype(F32).T.astype(BF)
        gt_ref[0:hd, rows] = dqt
        gt_ref[hd : 2 * hd, rows] = dk.astype(F32).T.astype(BF)
        gt_ref[2 * hd : 3 * hd, rows] = dv.astype(F32).T.astype(BF)
        for c in range(bq // pack):
            for n, value in enumerate((dq, dk, dv)):
                piece = value[c * pack : (c + 1) * pack]
                out_ref[i * (bq // pack) + c, n * half : (n + 1) * half, :] = jnp.concatenate(
                    [piece[:half], piece[half:]], axis=1
                )
        both = jnp.concatenate([dq.astype(F32), dv.astype(F32)], axis=1)
        return sums + jnp.sum(both, axis=0, keepdims=True)

    sums_ref[...] = lax.fori_loop(0, length // bq, emit, jnp.zeros((1, 2 * hd), F32))


def attend_back(lo, hi, q, k, v, kt, ot, lse, do, spans, pack, bq, bk):
    length, hd = q.shape
    return pl.pallas_call(
        functools.partial(attend_back_kernel, bq=bq, bk=bk, pack=pack),
        out_shape=(
            jax.ShapeDtypeStruct((length // pack, 3 * pack // 2, 2 * hd), BF),
            jax.ShapeDtypeStruct((3 * hd, length), BF),
            jax.ShapeDtypeStruct((1, 2 * hd), F32),
        ),
        in_specs=[SMEM, SMEM] + [VMEM] * 8,
        out_specs=(VMEM,) * 3,
        scratch_shapes=[
            pltpu.VMEM((hd, length), F32),
            pltpu.VMEM((length, hd), F32),
            pltpu.VMEM((length, hd), F32),
        ],
        compiler_params=PARAMS,
        name="attend_back",
    )(lo, hi, q, k, v, kt, ot, lse, do, spans)


def normalise(hidden):
    center = hidden - jnp.mean(hidden, axis=-1, keepdims=True)
    spread = jnp.mean(center * center, axis=-1, keepdims=True)
    inverse = lax.rsqrt(spread + norm_eps)
    return center * inverse, inverse


def norm_back(grad, normed, inverse, gain):
    e = grad * gain
    dh = inverse * (
        e
        - jnp.mean(e, axis=-1, keepdims=True)
        - normed * jnp.mean(e * normed, axis=-1, keepdims=True)
    )
    return dh, jnp.sum(grad * normed, axis=0), jnp.sum(grad, axis=0)


def by_core(value):
    return lax.ppermute(value, "head", [(0, 1), (1, 0), (2, 3), (3, 2)])


def by_x(value):
    return lax.ppermute(value, "head", [(0, 2), (2, 0), (1, 3), (3, 1)])


def swap(value, axes, groups=None):
    return lax.all_to_all(
        value, axes, split_axis=0, concat_axis=0, tiled=True, axis_index_groups=groups
    )


def spread_over(value, axes, count, groups=None):
    return swap(jnp.broadcast_to(value[None], (count, *value.shape)), axes, groups)


def gather_group(rows):
    pair = jnp.concatenate([rows[None], by_x(rows)[None]])
    return jnp.concatenate([pair, by_core(pair)]).reshape(4 * rows.shape[0], rows.shape[1])


def reduce_group(partial, count):
    parts = partial.reshape(4, count, -1)
    kept = parts[:2] + by_core(parts[2:].astype(BF)).astype(F32)
    return kept[0] + by_x(kept[1].astype(BF)).astype(F32)


def key_ranges(spans, bq, bk):
    return spans[0, ::bq] // bk, cdiv(spans[1, bq - 1 :: bq], bk)


def local(
    inputs,
    doc_lengths,
    grad_out,
    qkv_weight,
    out_weight,
    inner_weight,
    outer_weight,
    bias_rows,
    inner_bias,
    norm_gains,
    norm_shifts,
):
    micro, tokens, depth = inputs.shape
    groups, cycle = lax.axis_size("head"), lax.axis_size("blk")
    halves = cycle // 2
    devices = groups * cycle
    length = devices * tokens
    hd = depth // HEADS
    heads_dev = HEADS // groups
    rows_dev = qkv_weight.shape[1]
    ff_dev = outer_weight.shape[0]
    ff_part = cycle * ff_dev
    half_tokens = tokens // 2
    head_index = lax.axis_index("head")
    blk_index = lax.axis_index("blk")
    half = blk_index // halves
    unit_head = head_index * heads_dev + jnp.minimum(blk_index % halves, heads_dev - 1)
    unit_of = [min(i, heads_dev - 1) for i in range(halves)]

    own_x = lax.dynamic_index_in_dim(inputs, half, 0, keepdims=False)
    other_x = lax.dynamic_index_in_dim(inputs, 1 - half, 0, keepdims=False)
    got_x = lax.ppermute(other_x, "blk", [(i, (i + halves) % cycle) for i in range(cycle)])
    pair_x = jnp.concatenate([own_x, got_x], axis=0)
    cube = [
        [h * cycle + b for h in (c, c + 2) for b in range(s * halves, (s + 1) * halves)]
        for c in range(2)
        for s in range(2)
    ]
    tokens_a = spread_over(pair_x, BOTH, cycle, cube)
    tokens_b = by_core(tokens_a)

    weights = qkv_weight.reshape(3, rows_dev, groups, heads_dev, hd).transpose(2, 3, 1, 0, 4)
    weights = weights.reshape(groups, heads_dev, rows_dev * 3 * hd)
    small = jnp.concatenate(
        [bias_rows.reshape(-1), norm_gains.reshape(-1), norm_shifts.reshape(-1), inner_bias]
    )
    weight_size = weights.shape[2]
    pad = -(weight_size + small.shape[0]) % (2 * hd)
    small = jnp.pad(small, (0, pad))
    slots = jnp.stack([weights[:, u] for u in unit_of * 2], axis=1)
    slots = jnp.concatenate(
        [slots, jnp.broadcast_to(small, (groups, cycle, small.shape[0]))], axis=2
    ).reshape(devices, -1, 2 * hd)
    slots = swap(slots, BOTH).reshape(devices, -1)
    unit_weight = (
        slots[:, :weight_size].reshape(depth, 3, hd).transpose(1, 0, 2)
    )
    small = slots[:, weight_size:].astype(F32)

    def column(first, count):
        part = small[:, first * rows_dev : (first + count) * rows_dev]
        return part.reshape(devices, count, rows_dev).transpose(1, 0, 2).reshape(count, depth)

    bias, gains, shifts = column(0, 4), column(4, 2), column(6, 2)
    inner_bias_all = small[:, 8 * rows_dev : 8 * rows_dev + ff_dev].reshape(groups, ff_part)
    inner_bias_part = lax.dynamic_index_in_dim(inner_bias_all, head_index, 0, keepdims=False)
    unit_bias = jnp.stack([bias[0], jnp.zeros_like(bias[0]), bias[1]]).reshape(3, HEADS, hd)
    unit_bias = lax.dynamic_index_in_dim(unit_bias, unit_head, 1, keepdims=True)

    inner_slots = inner_weight.reshape(rows_dev, groups, 1, ff_part).transpose(1, 2, 0, 3)
    inner_part = swap(
        jnp.broadcast_to(inner_slots, (groups, cycle, rows_dev, ff_part)).reshape(
            devices, rows_dev, ff_part
        ),
        BOTH,
    ).reshape(depth, ff_part)
    outer_part = spread_over(outer_weight, "blk", cycle).reshape(ff_part, depth)
    out_all = spread_over(
        spread_over(out_weight, "blk", cycle).reshape(depth // groups, depth), "head", groups
    ).reshape(depth, depth)
    qkv_all = spread_over(spread_over(qkv_weight, "blk", cycle), "head", groups)

    lengths = lax.dynamic_index_in_dim(doc_lengths, half, 0, keepdims=False)
    order = jnp.arange(lengths.shape[0], dtype=jnp.int32)
    bounds = jnp.sum(jnp.where(order[None, :] <= order[:, None], lengths[None, :], 0), axis=1)
    positions = jnp.arange(length, dtype=jnp.int32)[None, :]
    starts = (bounds - lengths)[:, None]
    own = (positions >= starts) & (positions < bounds[:, None])
    spans = jnp.stack(
        [
            jnp.sum(jnp.where(own, starts, 0), axis=0),
            jnp.sum(jnp.where(own, bounds[:, None], 0), axis=0),
        ]
    )

    place = jnp.stack([head_index % 2, half]).astype(jnp.int32)
    per = max(1, 256 // tokens)
    q, k, v, kt, vt = project(place, tokens_a, tokens_b, unit_weight, unit_bias, halves, per)
    block = 512 if length <= 4096 else 256
    lo, hi = key_ranges(spans, block, 512)
    attn_out, attn_t, lse = attend(lo, hi, q, k, vt, spans, tokens, block, 512)

    rows = micro * tokens
    attn = (
        swap(attn_out, BOTH)
        .reshape(groups, micro, halves, half_tokens, 2, hd)[:, :, :heads_dev]
        .transpose(1, 4, 3, 0, 2, 5)
        .reshape(rows, depth)
    )
    first_sum = (
        inputs.reshape(rows, depth).astype(F32)
        + dot(attn, out_all, NN)
        + bias[2]
    )
    normed_one, inverse_one = normalise(first_sum)
    first_normed = normed_one * gains[0] + shifts[0]
    normed_low = gather_group(first_normed.astype(BF))
    inner_pre = dot(normed_low, inner_part, NN) + inner_bias_part
    cdf = 0.5 * (1.0 + lax.erf(inner_pre * (1.0 / math.sqrt(2.0))))
    slope = cdf + inner_pre * jnp.exp(-0.5 * inner_pre * inner_pre) * (1.0 / math.sqrt(2.0 * math.pi))
    act_low = (inner_pre * cdf).astype(BF)
    second_sum = first_normed + reduce_group(dot(act_low, outer_part, NN), rows) + bias[3]
    normed_two, inverse_two = normalise(second_sum)
    output = (normed_two * gains[1] + shifts[1]).astype(BF).reshape(inputs.shape)

    d_second, gain_two, shift_two = norm_back(
        grad_out.reshape(rows, depth).astype(F32), normed_two, inverse_two, gains[1]
    )
    d_ffn = d_second.astype(BF)
    d_ffn_group = gather_group(d_ffn)
    d_inner = (dot(d_ffn_group, outer_part, NT) * slope).astype(BF)
    d_first_normed = d_second + reduce_group(dot(d_inner, inner_part, NT), rows)
    d_first, gain_one, shift_one = norm_back(d_first_normed, normed_one, inverse_one, gains[0])
    d_branch = d_first.astype(BF)
    d_attn = dot(d_branch, out_all, NT).astype(BF)
    d_heads = d_attn.reshape(micro, 2, half_tokens, groups, heads_dev, hd).transpose(3, 0, 4, 2, 1, 5)
    d_heads = d_heads.reshape(groups, micro, heads_dev, half_tokens, 2 * hd)
    d_heads = jnp.stack([d_heads[:, :, u] for u in unit_of], axis=2)
    d_heads = swap(d_heads.reshape(devices, half_tokens, 2 * hd), BOTH)

    outer_grad = dot(act_low, d_ffn_group, TN).astype(BF)
    outer_grad = jnp.sum(
        swap(outer_grad.reshape(cycle, ff_dev, depth), "blk").astype(F32), axis=0
    )
    inner_grad = dot(normed_low, d_inner, TN).astype(BF)
    inner_grad = swap(inner_grad.reshape(devices, rows_dev, ff_part), BOTH)
    inner_grad = (
        jnp.sum(inner_grad.reshape(groups, cycle, rows_dev, ff_part).astype(F32), axis=1)
        .transpose(1, 0, 2)
        .reshape(rows_dev, groups * ff_part)
    )
    out_grad = dot(attn, d_branch, TN).reshape(groups, depth // groups, depth)

    def out_block(offset):
        return lax.dynamic_index_in_dim(out_grad, head_index ^ offset, 0, keepdims=False)

    from_core = by_core(jnp.stack([out_block(1), out_block(3)]).astype(BF)).astype(F32)
    from_x = by_x((out_block(2) + from_core[1]).astype(BF)).astype(F32)
    out_grad = (out_block(0) + from_core[0] + from_x).astype(BF)
    out_grad = jnp.sum(
        swap(out_grad.reshape(cycle, rows_dev, depth), "blk").astype(F32), axis=0
    )

    lo, hi = key_ranges(spans, 512, 256)
    qkv_out, qkv_t, qv_sums = attend_back(
        lo, hi, q, k, v, kt, attn_t, lse, d_heads, spans, tokens, 512, 256
    )
    d_qkv = (
        swap(qkv_out, BOTH)
        .reshape(groups, micro, halves, 3, half_tokens, 2, hd)[:, :, :heads_dev]
        .transpose(3, 1, 5, 4, 0, 2, 6)
        .reshape(3, rows, depth)
    )
    qkv_all = qkv_all.reshape(devices, 3, rows_dev, depth).transpose(1, 0, 2, 3).reshape(3, depth, depth)
    d_tokens = d_first
    for c in range(3):
        d_tokens = d_tokens + dot(d_qkv[c], qkv_all[c], NT)
    grad_inputs = d_tokens.astype(BF).reshape(inputs.shape)

    unit_grad = weight_grad(place, tokens_a, tokens_b, qkv_t, halves, per)
    ones = [gain_one, gain_two, shift_one, shift_two]
    ones += [jnp.sum(d.astype(F32), axis=0) for d in (d_branch, d_ffn)]
    wide = jnp.zeros((2, HEADS, hd), F32)
    wide = lax.dynamic_update_slice(wide, qv_sums.reshape(2, 1, hd), (0, unit_head, 0))
    wide = jnp.where((blk_index % halves < heads_dev), wide, 0.0)
    sums = jnp.concatenate([jnp.stack(ones), wide.reshape(2, depth)]).T
    inner_sums = jnp.sum(d_inner.astype(F32), axis=0).reshape(1, cycle, rows_dev, ff_dev // rows_dev)
    inner_sums = jnp.broadcast_to(inner_sums, (groups, *inner_sums.shape[1:]))
    extra = jnp.concatenate(
        [
            sums.reshape(devices, rows_dev, 8),
            inner_sums.reshape(devices, rows_dev, -1),
        ],
        axis=2,
    ).astype(BF)
    extra = jnp.pad(extra, ((0, 0), (0, 0), (0, hd - extra.shape[2])))
    final = swap(
        jnp.concatenate([unit_grad.reshape(devices, rows_dev, 3 * hd), extra], axis=2), BOTH
    ).astype(F32)
    qkv_grad = jnp.sum(
        final[:, :, : 3 * hd].reshape(groups, micro, halves, rows_dev, 3, hd)[:, :, :heads_dev], axis=1
    )
    qkv_grad = qkv_grad.transpose(3, 2, 0, 1, 4).reshape(3, rows_dev, depth)
    sums = jnp.sum(final[:, :, 3 * hd : 3 * hd + 8], axis=0).T
    inner_sums = final[:, :, 3 * hd + 8 : 3 * hd + 8 + ff_dev // rows_dev]
    inner_sums = lax.dynamic_index_in_dim(
        inner_sums.reshape(groups, cycle, rows_dev, -1), head_index, 0, keepdims=False
    )
    inner_bias_grad = jnp.sum(inner_sums, axis=0).reshape(ff_dev)
    return (
        output,
        grad_inputs,
        qkv_grad,
        out_grad,
        inner_grad,
        outer_grad,
        jnp.stack([sums[6], sums[7], sums[4], sums[5]]),
        inner_bias_grad,
        sums[0:2],
        sums[2:4],
    )


def solution(mesh):
    tokens = P(None, BOTH, None)
    rows = P(BOTH, None)
    columns = P(None, BOTH)
    return jax.shard_map(
        local,
        mesh=mesh,
        in_specs=(tokens, P(), tokens, tokens, rows, rows, rows, columns, P(BOTH), columns, columns),
        out_specs=(tokens, tokens, tokens, rows, rows, rows, columns, P(BOTH), columns, columns),
        check_vma=False,
    )
```

```python
import functools
import math

import jax
import jax.numpy as jnp
from jax import lax
from jax.experimental import pallas as pl
from jax.experimental.pallas import tpu as pltpu
from jax.sharding import PartitionSpec as P

HEADS = 12
F32 = jnp.float32
BF = jnp.bfloat16
NT = (((1,), (1,)), ((), ()))
NN = (((1,), (0,)), ((), ()))
TN = (((0,), (0,)), ((), ()))
LOG2E = math.log2(math.e)
BOTH = ("head", "blk")
norm_eps = 1e-12
masked_score = -1e30
VMEM = pl.BlockSpec(memory_space=pltpu.VMEM)
SMEM = pl.BlockSpec(memory_space=pltpu.SMEM)
PARAMS = pltpu.CompilerParams(vmem_limit_bytes=56 << 20)


def dot(a, b, dims):
    return lax.dot_general(a, b, dims, preferred_element_type=F32)


def cdiv(a, b):
    return -(-a // b)


def chunk_walk(place_ref, blocks, halves, per, tokens, visit):
    core, half = place_ref[0], place_ref[1]
    runs = halves // per
    for source in range(2):

        def one(n, carry, source=source):
            xh = n // (2 * runs)
            rel = n // runs % 2
            run = n % runs
            head = xh * 2 + (core if source == 0 else 1 - core)
            position = ((head * 2 + (rel ^ half)) * halves + run * per) * tokens
            rows = pl.ds(pl.multiple_of(rel * tokens, tokens), tokens)

            def load(ref):
                return jnp.concatenate(
                    [ref[xh * halves + run * per + k, rows, :] for k in range(per)], axis=0
                )

            visit(source, load, pl.multiple_of(position, per * tokens))
            return carry

        lax.fori_loop(0, 4 * runs, one, 0, unroll=4 * runs <= 4)


def project_kernel(
    place_ref, a_ref, b_ref, w_ref, bias_ref, q_ref, k_ref, v_ref, kt_ref, vt_ref, *, halves, per
):
    tokens = a_ref.shape[1] // 2

    def visit(source, load, position):
        x = load((a_ref, b_ref)[source])
        rows = pl.ds(position, per * tokens)
        for n, ref in enumerate((q_ref, k_ref, v_ref)):
            y = dot(x, w_ref[n], NN) + bias_ref[n]
            ref[rows, :] = y.astype(BF)
            if n:
                (kt_ref, vt_ref)[n - 1][:, rows] = y.T.astype(BF)

    chunk_walk(place_ref, a_ref.shape[0], halves, per, tokens, visit)


def project(place, a, b, w, bias, halves, per):
    length = 2 * a.shape[0] * a.shape[1]
    hd = w.shape[2]
    rows = jax.ShapeDtypeStruct((length, hd), BF)
    columns = jax.ShapeDtypeStruct((hd, length), BF)
    return pl.pallas_call(
        functools.partial(project_kernel, halves=halves, per=per),
        out_shape=(rows, rows, rows, columns, columns),
        in_specs=[SMEM] + [VMEM] * 4,
        out_specs=(VMEM,) * 5,
        compiler_params=PARAMS,
        name="project",
    )(place, a, b, w, bias)


def weight_grad_kernel(place_ref, a_ref, b_ref, gt_ref, out_ref, acc_ref, *, halves, per):
    tokens = a_ref.shape[1] // 2
    acc_ref[...] = jnp.zeros_like(acc_ref)

    def visit(source, load, position):
        x = load((a_ref, b_ref)[source])
        acc_ref[...] += dot(gt_ref[:, pl.ds(position, per * tokens)], x, NN)

    chunk_walk(place_ref, a_ref.shape[0], halves, per, tokens, visit)
    out_ref[...] = acc_ref[...].T.astype(BF)


def weight_grad(place, a, b, gt, halves, per):
    depth = a.shape[2]
    return pl.pallas_call(
        functools.partial(weight_grad_kernel, halves=halves, per=per),
        out_shape=jax.ShapeDtypeStruct((depth, gt.shape[0]), BF),
        in_specs=[SMEM] + [VMEM] * 3,
        out_specs=VMEM,
        scratch_shapes=[pltpu.VMEM((gt.shape[0], depth), F32)],
        compiler_params=PARAMS,
        name="weight_grad",
    )(place, a, b, gt)


def inside(first, start, stop, bk):
    key = first + lax.broadcasted_iota(jnp.int32, (bk, start.shape[1]), 0)
    return (key >= start) & (key < stop)


def attend_kernel(
    lo_ref, hi_ref, q_ref, k_ref, vt_ref, span_ref, out_ref, ot_ref, lse_ref, s_ref,
    *, bq, bk, pack
):
    length, hd = q_ref.shape
    factor = LOG2E / math.sqrt(hd)
    half = pack // 2

    def q_step(i, carry):
        qs = pl.ds(pl.multiple_of(i * bq, bq), bq)
        q = q_ref[qs, :]
        start, stop = span_ref[0:1, qs], span_ref[1:2, qs]
        lo, hi = lo_ref[i], hi_ref[i]

        def first(j, top):
            ks = pl.ds(pl.multiple_of(j * bk, bk), bk)
            s = dot(k_ref[ks, :], q, NT) * factor
            s = jnp.where(inside(j * bk, start, stop, bk), s, masked_score)
            s_ref[ks, :] = s
            return jnp.maximum(top, jnp.max(s.reshape(bk // 8, 8, bq), axis=0))

        top = lax.fori_loop(lo, hi, first, jnp.full((8, bq), masked_score, F32))
        peak = jnp.max(top, axis=0, keepdims=True)

        def second(j, state):
            total, acc = state
            ks = pl.ds(pl.multiple_of(j * bk, bk), bk)
            p = jnp.exp2(s_ref[ks, :] - peak)
            total = total + jnp.sum(p.reshape(bk // 8, 8, bq), axis=0)
            return total, acc + dot(vt_ref[:, ks], p.astype(BF), NN)

        total, acc = lax.fori_loop(
            lo, hi, second, (jnp.zeros((8, bq), F32), jnp.zeros((hd, bq), F32))
        )
        total = jnp.sum(total, axis=0, keepdims=True)
        out = acc / total
        ot_ref[:, qs] = out
        lse_ref[:, qs] = peak + jnp.log2(total)
        rows = out.T.astype(BF)
        for c in range(bq // pack):
            piece = rows[c * pack : (c + 1) * pack]
            out_ref[i * (bq // pack) + c] = jnp.concatenate([piece[:half], piece[half:]], axis=1)
        return carry

    lax.fori_loop(0, length // bq, q_step, 0)


def attend(lo, hi, q, k, vt, spans, pack, bq, bk):
    length, hd = q.shape
    return pl.pallas_call(
        functools.partial(attend_kernel, bq=bq, bk=bk, pack=pack),
        out_shape=(
            jax.ShapeDtypeStruct((length // pack, pack // 2, 2 * hd), BF),
            jax.ShapeDtypeStruct((hd, length), F32),
            jax.ShapeDtypeStruct((1, length), F32),
        ),
        in_specs=[SMEM, SMEM] + [VMEM] * 4,
        out_specs=(VMEM,) * 3,
        scratch_shapes=[pltpu.VMEM((length, bq), F32)],
        compiler_params=PARAMS,
        name="attend",
    )(lo, hi, q, k, vt, spans)


def attend_back_kernel(
    lo_ref, hi_ref, q_ref, k_ref, v_ref, kt_ref, ot_ref, lse_ref, do_ref, span_ref,
    out_ref, gt_ref, sums_ref, dq_ref, dk_ref, dv_ref, *, bq, bk, pack
):
    length, hd = q_ref.shape
    scale = 1.0 / math.sqrt(hd)
    factor = LOG2E * scale
    half = pack // 2
    dk_ref[...] = jnp.zeros_like(dk_ref)
    dv_ref[...] = jnp.zeros_like(dv_ref)

    def q_step(i, carry):
        qs = pl.ds(pl.multiple_of(i * bq, bq), bq)
        q = q_ref[qs, :]
        start, stop = span_ref[0:1, qs], span_ref[1:2, qs]
        pieces = []
        for c in range(bq // pack):
            piece = do_ref[i * (bq // pack) + c]
            pieces += [piece[:, :hd], piece[:, hd:]]
        do = jnp.concatenate(pieces, axis=0)
        delta = jnp.sum(do.astype(F32).T * ot_ref[:, qs], axis=0, keepdims=True)
        lse = lse_ref[:, qs]

        def step(j, acc):
            ks = pl.ds(pl.multiple_of(j * bk, bk), bk)
            s = dot(k_ref[ks, :], q, NT) * factor - lse
            p = jnp.where(inside(j * bk, start, stop, bk), jnp.exp2(s), 0.0)
            dp = dot(v_ref[ks, :], do, NT)
            ds = (p * (dp - delta)).astype(BF)
            dv_ref[ks, :] += dot(p.astype(BF), do, NN)
            dk_ref[ks, :] += dot(ds, q, NN)
            return acc + dot(kt_ref[:, ks], ds, NN)

        acc = lax.fori_loop(lo_ref[i], hi_ref[i], step, jnp.zeros((hd, bq), F32))
        dq_ref[:, qs] = acc
        return carry

    lax.fori_loop(0, length // bq, q_step, 0)

    def emit(i, sums):
        rows = pl.ds(pl.multiple_of(i * bq, bq), bq)
        dqt = (dq_ref[:, rows] * scale).astype(BF)
        dk = (dk_ref[rows, :] * scale).astype(BF)
        dv = dv_ref[rows, :].astype(BF)
        dq = dqt.astype(F32).T.astype(BF)
        gt_ref[0:hd, rows] = dqt
        gt_ref[hd : 2 * hd, rows] = dk.astype(F32).T.astype(BF)
        gt_ref[2 * hd : 3 * hd, rows] = dv.astype(F32).T.astype(BF)
        for c in range(bq // pack):
            for n, value in enumerate((dq, dk, dv)):
                piece = value[c * pack : (c + 1) * pack]
                out_ref[i * (bq // pack) + c, n * half : (n + 1) * half, :] = jnp.concatenate(
                    [piece[:half], piece[half:]], axis=1
                )
        both = jnp.concatenate([dq.astype(F32), dv.astype(F32)], axis=1)
        return sums + jnp.sum(both, axis=0, keepdims=True)

    sums_ref[...] = lax.fori_loop(0, length // bq, emit, jnp.zeros((1, 2 * hd), F32))


def attend_back(lo, hi, q, k, v, kt, ot, lse, do, spans, pack, bq, bk):
    length, hd = q.shape
    return pl.pallas_call(
        functools.partial(attend_back_kernel, bq=bq, bk=bk, pack=pack),
        out_shape=(
            jax.ShapeDtypeStruct((length // pack, 3 * pack // 2, 2 * hd), BF),
            jax.ShapeDtypeStruct((3 * hd, length), BF),
            jax.ShapeDtypeStruct((1, 2 * hd), F32),
        ),
        in_specs=[SMEM, SMEM] + [VMEM] * 8,
        out_specs=(VMEM,) * 3,
        scratch_shapes=[
            pltpu.VMEM((hd, length), F32),
            pltpu.VMEM((length, hd), F32),
            pltpu.VMEM((length, hd), F32),
        ],
        compiler_params=PARAMS,
        name="attend_back",
    )(lo, hi, q, k, v, kt, ot, lse, do, spans)


def normalise(hidden):
    center = hidden - jnp.mean(hidden, axis=-1, keepdims=True)
    spread = jnp.mean(center * center, axis=-1, keepdims=True)
    inverse = lax.rsqrt(spread + norm_eps)
    return center * inverse, inverse


def norm_back(grad, normed, inverse, gain):
    e = grad * gain
    dh = inverse * (
        e
        - jnp.mean(e, axis=-1, keepdims=True)
        - normed * jnp.mean(e * normed, axis=-1, keepdims=True)
    )
    return dh, jnp.sum(grad * normed, axis=0), jnp.sum(grad, axis=0)


def by_core(value):
    return lax.ppermute(value, "head", [(0, 1), (1, 0), (2, 3), (3, 2)])


def by_x(value):
    return lax.ppermute(value, "head", [(0, 2), (2, 0), (1, 3), (3, 1)])


def swap(value, axes, groups=None):
    return lax.all_to_all(
        value, axes, split_axis=0, concat_axis=0, tiled=True, axis_index_groups=groups
    )


def spread_over(value, axes, count, groups=None):
    return swap(jnp.broadcast_to(value[None], (count, *value.shape)), axes, groups)


def gather_group(rows):
    pair = jnp.concatenate([rows[None], by_x(rows)[None]])
    return jnp.concatenate([pair, by_core(pair)]).reshape(4 * rows.shape[0], rows.shape[1])


def reduce_group(partial, count):
    parts = partial.reshape(4, count, -1)
    kept = parts[:2] + by_core(parts[2:].astype(BF)).astype(F32)
    return kept[0] + by_x(kept[1].astype(BF)).astype(F32)


def in_order(blocks):
    index = lax.axis_index("head")
    own, across_x, across_core, across = [blocks[i] for i in range(4)]
    odd, far = index % 2 == 1, index // 2 == 1
    near = [jnp.where(odd, q, p) for p, q in ((own, across_core), (across_core, own))]
    wide = [jnp.where(odd, q, p) for p, q in ((across_x, across), (across, across_x))]
    return jnp.stack(
        [jnp.where(far, q, p) for p, q in zip(near + wide, wide + near)]
    )


def to_group(blocks):
    index = lax.axis_index("head")

    def block(offset):
        return lax.dynamic_index_in_dim(blocks, index ^ offset, 0, keepdims=False)

    across = lax.ppermute(block(3), "head", [(i, i ^ 3) for i in range(4)])
    return in_order(jnp.stack([block(0), by_x(block(2)), by_core(block(1)), across]))


def key_ranges(spans, bq, bk):
    return spans[0, ::bq] // bk, cdiv(spans[1, bq - 1 :: bq], bk)


def local(
    inputs,
    doc_lengths,
    grad_out,
    qkv_weight,
    out_weight,
    inner_weight,
    outer_weight,
    bias_rows,
    inner_bias,
    norm_gains,
    norm_shifts,
):
    micro, tokens, depth = inputs.shape
    groups, cycle = lax.axis_size("head"), lax.axis_size("blk")
    halves = cycle // 2
    devices = groups * cycle
    length = devices * tokens
    hd = depth // HEADS
    heads_dev = HEADS // groups
    rows_dev = qkv_weight.shape[1]
    ff_dev = outer_weight.shape[0]
    ff_part = cycle * ff_dev
    half_tokens = tokens // 2
    head_index = lax.axis_index("head")
    blk_index = lax.axis_index("blk")
    half = blk_index // halves
    unit_head = head_index * heads_dev + jnp.minimum(blk_index % halves, heads_dev - 1)
    unit_of = [min(i, heads_dev - 1) for i in range(halves)]

    own_x = lax.dynamic_index_in_dim(inputs, half, 0, keepdims=False)
    other_x = lax.dynamic_index_in_dim(inputs, 1 - half, 0, keepdims=False)
    got_x = lax.ppermute(other_x, "blk", [(i, (i + halves) % cycle) for i in range(cycle)])
    pair_x = jnp.concatenate([own_x, got_x], axis=0)
    cube = [
        [h * cycle + b for h in (c, c + 2) for b in range(s * halves, (s + 1) * halves)]
        for c in range(2)
        for s in range(2)
    ]
    tokens_a = spread_over(pair_x, BOTH, cycle, cube)
    tokens_b = by_core(tokens_a)

    weights = qkv_weight.reshape(3, rows_dev, groups, heads_dev, hd).transpose(2, 3, 1, 0, 4)
    weights = weights.reshape(groups, heads_dev, rows_dev * 3 * hd)
    small = jnp.concatenate(
        [bias_rows.reshape(-1), norm_gains.reshape(-1), norm_shifts.reshape(-1), inner_bias]
    )
    weight_size = weights.shape[2]
    pad = -(weight_size + small.shape[0]) % (2 * hd)
    small = jnp.pad(small, (0, pad))
    slots = jnp.stack([weights[:, u] for u in unit_of * 2], axis=1)
    slots = jnp.concatenate(
        [slots, jnp.broadcast_to(small, (groups, cycle, small.shape[0]))], axis=2
    ).reshape(devices, -1, 2 * hd)
    slots = swap(slots, BOTH).reshape(devices, -1)
    unit_weight = (
        slots[:, :weight_size].reshape(depth, 3, hd).transpose(1, 0, 2)
    )
    small = slots[:, weight_size:].astype(F32)

    def column(first, count):
        part = small[:, first * rows_dev : (first + count) * rows_dev]
        return part.reshape(devices, count, rows_dev).transpose(1, 0, 2).reshape(count, depth)

    bias, gains, shifts = column(0, 4), column(4, 2), column(6, 2)
    inner_bias_all = small[:, 8 * rows_dev : 8 * rows_dev + ff_dev].reshape(groups, ff_part)
    inner_bias_part = lax.dynamic_index_in_dim(inner_bias_all, head_index, 0, keepdims=False)
    unit_bias = jnp.stack([bias[0], jnp.zeros_like(bias[0]), bias[1]]).reshape(3, HEADS, hd)
    unit_bias = lax.dynamic_index_in_dim(unit_bias, unit_head, 1, keepdims=True)

    inner_own = to_group(inner_weight.reshape(rows_dev, groups, ff_part).transpose(1, 0, 2))
    ffn = lax.all_gather(
        jnp.concatenate([inner_own.reshape(groups * rows_dev, ff_part), outer_weight]),
        "blk",
        axis=0,
        tiled=False,
    )
    inner_part = (
        ffn[:, : groups * rows_dev]
        .reshape(cycle, groups, rows_dev, ff_part)
        .transpose(1, 0, 2, 3)
        .reshape(depth, ff_part)
    )
    outer_part = ffn[:, groups * rows_dev :].reshape(ff_part, depth)
    out_part = spread_over(out_weight, "blk", cycle).reshape(depth // groups, depth)
    out_all = in_order(gather_group(out_part).reshape(groups, depth // groups, depth)).reshape(
        depth, depth
    )
    qkv_all = lax.all_gather(qkv_weight, BOTH, axis=0, tiled=False)

    lengths = lax.dynamic_index_in_dim(doc_lengths, half, 0, keepdims=False)
    order = jnp.arange(lengths.shape[0], dtype=jnp.int32)
    bounds = jnp.sum(jnp.where(order[None, :] <= order[:, None], lengths[None, :], 0), axis=1)
    positions = jnp.arange(length, dtype=jnp.int32)[None, :]
    starts = (bounds - lengths)[:, None]
    own = (positions >= starts) & (positions < bounds[:, None])
    spans = jnp.stack(
        [
            jnp.sum(jnp.where(own, starts, 0), axis=0),
            jnp.sum(jnp.where(own, bounds[:, None], 0), axis=0),
        ]
    )

    place = jnp.stack([head_index % 2, half]).astype(jnp.int32)
    per = max(1, 256 // tokens)
    q, k, v, kt, vt = project(place, tokens_a, tokens_b, unit_weight, unit_bias, halves, per)
    block = 512 if length <= 4096 else 256
    lo, hi = key_ranges(spans, block, 512)
    attn_out, attn_t, lse = attend(lo, hi, q, k, vt, spans, tokens, block, 512)

    rows = micro * tokens
    attn = (
        swap(attn_out, BOTH)
        .reshape(groups, micro, halves, half_tokens, 2, hd)[:, :, :heads_dev]
        .transpose(1, 4, 3, 0, 2, 5)
        .reshape(rows, depth)
    )
    first_sum = (
        inputs.reshape(rows, depth).astype(F32)
        + dot(attn, out_all, NN)
        + bias[2]
    )
    normed_one, inverse_one = normalise(first_sum)
    first_normed = normed_one * gains[0] + shifts[0]
    normed_low = gather_group(first_normed.astype(BF))
    inner_pre = dot(normed_low, inner_part, NN) + inner_bias_part
    cdf = 0.5 * (1.0 + lax.erf(inner_pre * (1.0 / math.sqrt(2.0))))
    slope = cdf + inner_pre * jnp.exp(-0.5 * inner_pre * inner_pre) * (1.0 / math.sqrt(2.0 * math.pi))
    act_low = (inner_pre * cdf).astype(BF)
    second_sum = first_normed + reduce_group(dot(act_low, outer_part, NN), rows) + bias[3]
    normed_two, inverse_two = normalise(second_sum)
    output = (normed_two * gains[1] + shifts[1]).astype(BF).reshape(inputs.shape)

    d_second, gain_two, shift_two = norm_back(
        grad_out.reshape(rows, depth).astype(F32), normed_two, inverse_two, gains[1]
    )
    d_ffn = d_second.astype(BF)
    d_ffn_group = gather_group(d_ffn)
    d_inner = (dot(d_ffn_group, outer_part, NT) * slope).astype(BF)
    d_first_normed = d_second + reduce_group(dot(d_inner, inner_part, NT), rows)
    d_first, gain_one, shift_one = norm_back(d_first_normed, normed_one, inverse_one, gains[0])
    d_branch = d_first.astype(BF)
    d_attn = dot(d_branch, out_all, NT).astype(BF)
    d_heads = d_attn.reshape(micro, 2, half_tokens, groups, heads_dev, hd).transpose(3, 0, 4, 2, 1, 5)
    d_heads = d_heads.reshape(groups, micro, heads_dev, half_tokens, 2 * hd)
    d_heads = jnp.stack([d_heads[:, :, u] for u in unit_of], axis=2)
    d_heads = swap(d_heads.reshape(devices, half_tokens, 2 * hd), BOTH)

    outer_grad = dot(act_low, d_ffn_group, TN).astype(BF).reshape(cycle, ff_dev, depth)
    inner_grad = (
        dot(normed_low, d_inner, TN)
        .astype(BF)
        .reshape(groups, cycle, rows_dev, ff_part)
        .transpose(1, 0, 2, 3)
        .reshape(cycle, groups * rows_dev, ff_part)
    )
    ffn_grad = lax.psum_scatter(
        jnp.concatenate([inner_grad, outer_grad], axis=1), "blk", scatter_dimension=0, tiled=False
    )
    outer_grad = ffn_grad[groups * rows_dev :].astype(F32)
    inner_grad = to_group(ffn_grad[: groups * rows_dev].reshape(groups, rows_dev, ff_part))
    inner_grad = inner_grad.transpose(1, 0, 2).reshape(rows_dev, groups * ff_part).astype(F32)
    out_grad = dot(attn, d_branch, TN).reshape(groups, depth // groups, depth)

    def out_block(offset):
        return lax.dynamic_index_in_dim(out_grad, head_index ^ offset, 0, keepdims=False)

    from_core = by_core(jnp.stack([out_block(1), out_block(3)]).astype(BF)).astype(F32)
    from_x = by_x((out_block(2) + from_core[1]).astype(BF)).astype(F32)
    out_grad = (out_block(0) + from_core[0] + from_x).astype(BF)
    out_grad = jnp.sum(
        swap(out_grad.reshape(cycle, rows_dev, depth), "blk").astype(F32), axis=0
    )

    lo, hi = key_ranges(spans, 512, 256)
    qkv_out, qkv_t, qv_sums = attend_back(
        lo, hi, q, k, v, kt, attn_t, lse, d_heads, spans, tokens, 512, 256
    )
    d_qkv = (
        swap(qkv_out, BOTH)
        .reshape(groups, micro, halves, 3, half_tokens, 2, hd)[:, :, :heads_dev]
        .transpose(3, 1, 5, 4, 0, 2, 6)
        .reshape(3, rows, depth)
    )
    qkv_all = qkv_all.transpose(1, 0, 2, 3).reshape(3, depth, depth)
    d_tokens = d_first
    for c in range(3):
        d_tokens = d_tokens + dot(d_qkv[c], qkv_all[c], NT)
    grad_inputs = d_tokens.astype(BF).reshape(inputs.shape)

    unit_grad = weight_grad(place, tokens_a, tokens_b, qkv_t, halves, per)
    ones = [gain_one, gain_two, shift_one, shift_two]
    ones += [jnp.sum(d.astype(F32), axis=0) for d in (d_branch, d_ffn)]
    wide = jnp.zeros((2, HEADS, hd), F32)
    wide = lax.dynamic_update_slice(wide, qv_sums.reshape(2, 1, hd), (0, unit_head, 0))
    wide = jnp.where((blk_index % halves < heads_dev), wide, 0.0)
    sums = jnp.concatenate([jnp.stack(ones), wide.reshape(2, depth)]).T
    inner_sums = jnp.sum(d_inner.astype(F32), axis=0).reshape(1, cycle, rows_dev, ff_dev // rows_dev)
    inner_sums = jnp.broadcast_to(inner_sums, (groups, *inner_sums.shape[1:]))
    extra = jnp.concatenate(
        [
            sums.reshape(devices, rows_dev, 8),
            inner_sums.reshape(devices, rows_dev, -1),
        ],
        axis=2,
    ).astype(BF)
    extra = jnp.pad(extra, ((0, 0), (0, 0), (0, hd - extra.shape[2])))
    final = swap(
        jnp.concatenate([unit_grad.reshape(devices, rows_dev, 3 * hd), extra], axis=2), BOTH
    ).astype(F32)
    qkv_grad = jnp.sum(
        final[:, :, : 3 * hd].reshape(groups, micro, halves, rows_dev, 3, hd)[:, :, :heads_dev], axis=1
    )
    qkv_grad = qkv_grad.transpose(3, 2, 0, 1, 4).reshape(3, rows_dev, depth)
    sums = jnp.sum(final[:, :, 3 * hd : 3 * hd + 8], axis=0).T
    inner_sums = final[:, :, 3 * hd + 8 : 3 * hd + 8 + ff_dev // rows_dev]
    inner_sums = lax.dynamic_index_in_dim(
        inner_sums.reshape(groups, cycle, rows_dev, -1), head_index, 0, keepdims=False
    )
    inner_bias_grad = jnp.sum(inner_sums, axis=0).reshape(ff_dev)
    return (
        output,
        grad_inputs,
        qkv_grad,
        out_grad,
        inner_grad,
        outer_grad,
        jnp.stack([sums[6], sums[7], sums[4], sums[5]]),
        inner_bias_grad,
        sums[0:2],
        sums[2:4],
    )


def solution(mesh):
    tokens = P(None, BOTH, None)
    rows = P(BOTH, None)
    columns = P(None, BOTH)
    return jax.shard_map(
        local,
        mesh=mesh,
        in_specs=(tokens, P(), tokens, tokens, rows, rows, rows, columns, P(BOTH), columns, columns),
        out_specs=(tokens, tokens, tokens, rows, rows, rows, columns, P(BOTH), columns, columns),
        check_vma=False,
    )
```

```python
import functools
import math

import jax
import jax.numpy as jnp
from jax import lax
from jax.experimental import pallas as pl
from jax.experimental.pallas import tpu as pltpu
from jax.sharding import PartitionSpec as P

HEADS = 12
F32 = jnp.float32
BF = jnp.bfloat16
NT = (((1,), (1,)), ((), ()))
NN = (((1,), (0,)), ((), ()))
TN = (((0,), (0,)), ((), ()))
LOG2E = math.log2(math.e)
BOTH = ("head", "blk")
norm_eps = 1e-12
masked_score = -1e30
VMEM = pl.BlockSpec(memory_space=pltpu.VMEM)
SMEM = pl.BlockSpec(memory_space=pltpu.SMEM)
PARAMS = pltpu.CompilerParams(vmem_limit_bytes=56 << 20)


def dot(a, b, dims):
    return lax.dot_general(a, b, dims, preferred_element_type=F32)


def cdiv(a, b):
    return -(-a // b)


def chunk_walk(place_ref, blocks, halves, per, tokens, visit):
    core, half = place_ref[0], place_ref[1]
    runs = halves // per
    for source in range(2):

        def one(n, carry, source=source):
            xh = n // (2 * runs)
            rel = n // runs % 2
            run = n % runs
            head = xh * 2 + (core if source == 0 else 1 - core)
            position = ((head * 2 + (rel ^ half)) * halves + run * per) * tokens
            rows = pl.ds(pl.multiple_of(rel * tokens, tokens), tokens)

            def load(ref):
                return jnp.concatenate(
                    [ref[xh * halves + run * per + k, rows, :] for k in range(per)], axis=0
                )

            visit(source, load, pl.multiple_of(position, per * tokens))
            return carry

        lax.fori_loop(0, 4 * runs, one, 0, unroll=4 * runs <= 4)


def project_kernel(
    place_ref, a_ref, b_ref, qk_ref, v_w_ref, bias_ref, q_ref, k_ref, v_ref, kt_ref, vt_ref, *, halves, per
):
    tokens = a_ref.shape[1] // 2
    hd = q_ref.shape[1]

    def visit(source, load, position):
        x = load((a_ref, b_ref)[source])
        rows = pl.ds(position, per * tokens)
        qk = dot(x, qk_ref[...], NN) + bias_ref[0:1]
        v = (dot(x, v_w_ref[...], NN) + bias_ref[1:2])[:, :hd]
        k = qk[:, hd:]
        q_ref[rows, :] = qk[:, :hd].astype(BF)
        k_ref[rows, :] = k.astype(BF)
        v_ref[rows, :] = v.astype(BF)
        kt_ref[:, rows] = k.T.astype(BF)
        vt_ref[:, rows] = v.T.astype(BF)

    chunk_walk(place_ref, a_ref.shape[0], halves, per, tokens, visit)


def project(place, a, b, qk, v, bias, halves, per):
    length = 2 * a.shape[0] * a.shape[1]
    hd = qk.shape[1] // 2
    rows = jax.ShapeDtypeStruct((length, hd), BF)
    columns = jax.ShapeDtypeStruct((hd, length), BF)
    return pl.pallas_call(
        functools.partial(project_kernel, halves=halves, per=per),
        out_shape=(rows, rows, rows, columns, columns),
        in_specs=[SMEM] + [VMEM] * 5,
        out_specs=(VMEM,) * 5,
        compiler_params=PARAMS,
        cost_estimate=pl.CostEstimate(flops=5000000000, bytes_accessed=4 << 20, transcendentals=0),
        name="project",
    )(place, a, b, qk, v, bias)


def head_slots_kernel(w_ref, small_ref, out_ref, *, units):
    hd = small_ref.shape[1]
    small = small_ref[...]
    done = {}
    for d, j in enumerate(units):
        if j not in done:
            part = [w_ref[c][:, j * hd : (j + 1) * hd] for c in range(3)]
            done[j] = [
                jnp.concatenate(part[:2], axis=1),
                jnp.concatenate([part[2], small], axis=1),
            ]
        out_ref[d, 0] = done[j][0]
        out_ref[d, 1] = done[j][1]


def weight_grad_kernel(place_ref, a_ref, b_ref, gt_ref, out_ref, acc_ref, *, halves, per):
    tokens = a_ref.shape[1] // 2
    acc_ref[...] = jnp.zeros_like(acc_ref)

    def visit(source, load, position):
        x = load((a_ref, b_ref)[source])
        acc_ref[...] += dot(gt_ref[:, pl.ds(position, per * tokens)], x, NN)

    chunk_walk(place_ref, a_ref.shape[0], halves, per, tokens, visit)
    out_ref[...] = acc_ref[...].T.astype(BF)


def weight_grad(place, a, b, gt, halves, per):
    depth = a.shape[2]
    return pl.pallas_call(
        functools.partial(weight_grad_kernel, halves=halves, per=per),
        out_shape=jax.ShapeDtypeStruct((depth, gt.shape[0]), BF),
        in_specs=[SMEM] + [VMEM] * 3,
        out_specs=VMEM,
        scratch_shapes=[pltpu.VMEM((gt.shape[0], depth), F32)],
        compiler_params=PARAMS,
        cost_estimate=pl.CostEstimate(flops=3000000000, bytes_accessed=4 << 20, transcendentals=0),
        name="weight_grad",
    )(place, a, b, gt)


def inside(first, start, stop, bk):
    key = first + lax.broadcasted_iota(jnp.int32, (bk, start.shape[1]), 0)
    return (key >= start) & (key < stop)


def attend_kernel(
    lo_ref, hi_ref, q_ref, k_ref, vt_ref, span_ref, out_ref, ot_ref, lse_ref, s_ref,
    *, bq, bk, pack
):
    length, hd = q_ref.shape
    factor = LOG2E / math.sqrt(hd)
    half = pack // 2

    def q_step(i, carry):
        qs = pl.ds(pl.multiple_of(i * bq, bq), bq)
        q = q_ref[qs, :]
        start, stop = span_ref[0:1, qs], span_ref[1:2, qs]
        lo, hi = lo_ref[i], hi_ref[i]

        def first(j, top):
            ks = pl.ds(pl.multiple_of(j * bk, bk), bk)
            s = dot(k_ref[ks, :], q, NT) * factor
            s = jnp.where(inside(j * bk, start, stop, bk), s, masked_score)
            s_ref[ks, :] = s
            return jnp.maximum(top, jnp.max(s.reshape(bk // 8, 8, bq), axis=0))

        top = lax.fori_loop(lo, hi, first, jnp.full((8, bq), masked_score, F32))
        peak = jnp.max(top, axis=0, keepdims=True)

        def second(j, state):
            total, acc = state
            ks = pl.ds(pl.multiple_of(j * bk, bk), bk)
            p = jnp.exp2(s_ref[ks, :] - peak)
            total = total + jnp.sum(p.reshape(bk // 8, 8, bq), axis=0)
            return total, acc + dot(vt_ref[:, ks], p.astype(BF), NN)

        total, acc = lax.fori_loop(
            lo, hi, second, (jnp.zeros((8, bq), F32), jnp.zeros((hd, bq), F32))
        )
        total = jnp.sum(total, axis=0, keepdims=True)
        out = acc / total
        ot_ref[:, qs] = out
        lse_ref[:, qs] = peak + jnp.log2(total)
        rows = out.T.astype(BF)
        for c in range(bq // pack):
            piece = rows[c * pack : (c + 1) * pack]
            out_ref[i * (bq // pack) + c] = jnp.concatenate([piece[:half], piece[half:]], axis=1)
        return carry

    lax.fori_loop(0, length // bq, q_step, 0)


def attend(lo, hi, q, k, vt, spans, pack, bq, bk):
    length, hd = q.shape
    return pl.pallas_call(
        functools.partial(attend_kernel, bq=bq, bk=bk, pack=pack),
        out_shape=(
            jax.ShapeDtypeStruct((length // pack, pack // 2, 2 * hd), BF),
            jax.ShapeDtypeStruct((hd, length), F32),
            jax.ShapeDtypeStruct((1, length), F32),
        ),
        in_specs=[SMEM, SMEM] + [VMEM] * 4,
        out_specs=(VMEM,) * 3,
        scratch_shapes=[pltpu.VMEM((length, bq), F32)],
        compiler_params=PARAMS,
        cost_estimate=pl.CostEstimate(flops=10000000000, bytes_accessed=4 << 20, transcendentals=0),
        name="attend",
    )(lo, hi, q, k, vt, spans)


def attend_back_kernel(
    lo_ref, hi_ref, q_ref, k_ref, v_ref, kt_ref, ot_ref, lse_ref, do_ref, span_ref,
    out_ref, gt_ref, sums_ref, dq_ref, dk_ref, dv_ref, *, bq, bk, pack
):
    length, hd = q_ref.shape
    scale = 1.0 / math.sqrt(hd)
    factor = LOG2E * scale
    half = pack // 2
    dk_ref[...] = jnp.zeros_like(dk_ref)
    dv_ref[...] = jnp.zeros_like(dv_ref)

    def q_step(i, carry):
        qs = pl.ds(pl.multiple_of(i * bq, bq), bq)
        q = q_ref[qs, :]
        start, stop = span_ref[0:1, qs], span_ref[1:2, qs]
        pieces = []
        for c in range(bq // pack):
            piece = do_ref[i * (bq // pack) + c]
            pieces += [piece[:, :hd], piece[:, hd:]]
        do = jnp.concatenate(pieces, axis=0)
        delta = jnp.sum(do.astype(F32).T * ot_ref[:, qs], axis=0, keepdims=True)
        lse = lse_ref[:, qs]

        def step(j, acc):
            ks = pl.ds(pl.multiple_of(j * bk, bk), bk)
            s = dot(k_ref[ks, :], q, NT) * factor - lse
            p = jnp.where(inside(j * bk, start, stop, bk), jnp.exp2(s), 0.0)
            dp = dot(v_ref[ks, :], do, NT)
            ds = (p * (dp - delta)).astype(BF)
            dv_ref[ks, :] += dot(p.astype(BF), do, NN)
            dk_ref[ks, :] += dot(ds, q, NN)
            return acc + dot(kt_ref[:, ks], ds, NN)

        acc = lax.fori_loop(lo_ref[i], hi_ref[i], step, jnp.zeros((hd, bq), F32))
        dq_ref[:, qs] = acc
        return carry

    lax.fori_loop(0, length // bq, q_step, 0)

    def emit(i, sums):
        rows = pl.ds(pl.multiple_of(i * bq, bq), bq)
        dqt = (dq_ref[:, rows] * scale).astype(BF)
        dk = (dk_ref[rows, :] * scale).astype(BF)
        dv = dv_ref[rows, :].astype(BF)
        dq = dqt.astype(F32).T.astype(BF)
        gt_ref[0:hd, rows] = dqt
        gt_ref[hd : 2 * hd, rows] = dk.astype(F32).T.astype(BF)
        gt_ref[2 * hd : 3 * hd, rows] = dv.astype(F32).T.astype(BF)
        for c in range(bq // pack):
            for n, value in enumerate((dq, dk, dv)):
                piece = value[c * pack : (c + 1) * pack]
                out_ref[i * (bq // pack) + c, n * half : (n + 1) * half, :] = jnp.concatenate(
                    [piece[:half], piece[half:]], axis=1
                )
        both = jnp.concatenate([dq.astype(F32), dv.astype(F32)], axis=1)
        return sums + jnp.sum(both, axis=0, keepdims=True)

    sums_ref[...] = lax.fori_loop(0, length // bq, emit, jnp.zeros((1, 2 * hd), F32))


def attend_back(lo, hi, q, k, v, kt, ot, lse, do, spans, pack, bq, bk):
    length, hd = q.shape
    return pl.pallas_call(
        functools.partial(attend_back_kernel, bq=bq, bk=bk, pack=pack),
        out_shape=(
            jax.ShapeDtypeStruct((length // pack, 3 * pack // 2, 2 * hd), BF),
            jax.ShapeDtypeStruct((3 * hd, length), BF),
            jax.ShapeDtypeStruct((1, 2 * hd), F32),
        ),
        in_specs=[SMEM, SMEM] + [VMEM] * 8,
        out_specs=(VMEM,) * 3,
        scratch_shapes=[
            pltpu.VMEM((hd, length), F32),
            pltpu.VMEM((length, hd), F32),
            pltpu.VMEM((length, hd), F32),
        ],
        compiler_params=PARAMS,
        cost_estimate=pl.CostEstimate(flops=14000000000, bytes_accessed=4 << 20, transcendentals=0),
        name="attend_back",
    )(lo, hi, q, k, v, kt, ot, lse, do, spans)


def call(kernel, outs, ins, name, flops, scratch=()):
    return pl.pallas_call(
        kernel,
        out_shape=tuple(jax.ShapeDtypeStruct(shape, kind) for shape, kind in outs),
        in_specs=[SMEM if v.dtype == jnp.int32 else VMEM for v in ins],
        out_specs=(VMEM,) * len(outs),
        scratch_shapes=list(scratch),
        compiler_params=PARAMS,
        cost_estimate=pl.CostEstimate(
            flops=int(flops), bytes_accessed=2 << 20, transcendentals=0
        ),
        name=name,
    )(*ins)


def column_sums(*values):
    sums = [jnp.sum(v, axis=0, keepdims=True) for v in values]
    return jnp.concatenate(sums + [jnp.zeros_like(sums[0])] * (8 - len(sums)), axis=0)


def unpack_heads(slots_ref, out_ref, layout, piece_rows, which):
    groups, micro, halves, heads_dev = layout
    hd = slots_ref.shape[2] // 2
    part = slice(which * piece_rows, (which + 1) * piece_rows)
    for m in range(micro):
        rows = slice(m * 2 * piece_rows, (m + 1) * 2 * piece_rows)
        pieces = []
        for j in range(groups * heads_dev):
            piece = slots_ref[((j // heads_dev) * micro + m) * halves + j % heads_dev, part, :]
            pieces.append(jnp.concatenate([piece[:, :hd], piece[:, hd:]], axis=0))
        for j in range(0, groups * heads_dev, 2):
            out_ref[rows, j * hd : (j + 2) * hd] = jnp.concatenate(pieces[j : j + 2], axis=1)


def branch_kernel(slots_ref, x_ref, w_ref, vec_ref, attn_ref, low_ref, normed_ref, inv_ref, *, layout):
    unpack_heads(slots_ref, attn_ref, layout, slots_ref.shape[1], 0)
    first_sum = x_ref[...].astype(F32) + dot(attn_ref[...], w_ref[...], NN) + vec_ref[0:1]
    normed, inverse = normalise(first_sum)
    normed_ref[...] = normed
    inv_ref[...] = inverse
    low_ref[...] = (normed * vec_ref[1:2] + vec_ref[2:3]).astype(BF)


def normal_cdf(v):
    bell = jnp.exp(-0.5 * v * v)
    t = 1.0 / (1.0 + (0.3275911 * math.sqrt(0.5)) * jnp.abs(v))
    tail = 0.5 * 1.061405429
    for c in (-1.453152027, 1.421413741, -0.284496736, 0.254829592):
        tail = tail * t + 0.5 * c
    tail = tail * t * bell
    return jnp.where(v < 0.0, tail, 1.0 - tail), bell * (1.0 / math.sqrt(2.0 * math.pi))


def inner_kernel(a_ref, b_ref, c_ref, d_ref, wi_ref, wo_ref, bias_ref, act_ref, slope_ref, low_ref, keep_ref, send_ref):
    count = a_ref.shape[0]
    for n, ref in enumerate((a_ref, b_ref, c_ref, d_ref)):
        rows = slice(n * count, (n + 1) * count)
        x = ref[...]
        low_ref[rows, :] = x
        pre = dot(x, wi_ref[...], NN) + bias_ref[...]
        cdf, bell = normal_cdf(pre)
        slope_ref[rows, :] = cdf + pre * bell
        act = (pre * cdf).astype(BF)
        act_ref[rows, :] = act
        partial = dot(act, wo_ref[...], NN)
        if n < 2:
            keep_ref[rows, :] = partial
        else:
            send_ref[(n - 2) * count : (n - 1) * count, :] = partial.astype(BF)


def inner_back_kernel(a_ref, b_ref, c_ref, d_ref, wi_ref, wo_ref, slope_ref, inner_ref, low_ref, sums_ref, keep_ref, send_ref):
    count = a_ref.shape[0]
    sums = 0.0
    for n, ref in enumerate((a_ref, b_ref, c_ref, d_ref)):
        rows = slice(n * count, (n + 1) * count)
        x = ref[...]
        low_ref[rows, :] = x
        inner = (dot(x, wo_ref[...], NT) * slope_ref[rows, :]).astype(BF)
        inner_ref[rows, :] = inner
        sums = sums + jnp.sum(inner.astype(F32), axis=0, keepdims=True)
        partial = dot(inner, wi_ref[...], NT)
        if n < 2:
            keep_ref[rows, :] = partial
        else:
            send_ref[(n - 2) * count : (n - 1) * count, :] = partial.astype(BF)
    sums_ref[...] = sums


def feed_grad_kernel(low_ref, inner_ref, act_ref, ffn_ref, out_ref, acc_ref):
    cycle, blocks, rows = out_ref.shape[:3]
    half = blocks // 2
    acc_ref[...] = dot(low_ref[...], inner_ref[...], TN)
    for b in range(cycle):
        for h in range(half):
            first = (h * cycle + b) * rows
            out_ref[b, h] = acc_ref[first : first + rows, :].astype(BF)
    acc_ref[...] = dot(act_ref[...], ffn_ref[...], TN)
    for b in range(cycle):
        for h in range(half):
            first = (b * half + h) * rows
            out_ref[b, half + h] = acc_ref[first : first + rows, :].astype(BF)


def add_kernel(keep_ref, got_ref, own_ref, send_ref):
    count = own_ref.shape[0]
    own_ref[...] = keep_ref[:count] + got_ref[:count].astype(F32)
    send_ref[...] = (keep_ref[count:] + got_ref[count:].astype(F32)).astype(BF)


def output_kernel(own_ref, got_ref, normed_ref, grad_ref, vec_ref, out_ref, second_ref, low_ref, sums_ref):
    first_normed = normed_ref[...] * vec_ref[0:1] + vec_ref[1:2]
    second_sum = first_normed + own_ref[...] + got_ref[...].astype(F32) + vec_ref[2:3]
    normed, inverse = normalise(second_sum)
    out_ref[...] = (normed * vec_ref[3:4] + vec_ref[4:5]).astype(BF)
    grad = grad_ref[...].astype(F32)
    d_second = norm_back(grad, normed, inverse, vec_ref[3:4])
    low = d_second.astype(BF)
    second_ref[...] = d_second
    low_ref[...] = low
    sums_ref[...] = column_sums(grad * normed, grad, low.astype(F32))


def branch_back_kernel(own_ref, got_ref, second_ref, normed_ref, inv_ref, w_ref, vec_ref, first_ref, low_ref, sums_ref, slots_ref, *, layout):
    groups, micro, halves, heads_dev = layout
    grad = own_ref[...] + got_ref[...].astype(F32) + second_ref[...]
    normed = normed_ref[...]
    d_first = norm_back(grad, normed, inv_ref[...], vec_ref[0:1])
    low = d_first.astype(BF)
    first_ref[...] = d_first
    low_ref[...] = low
    sums_ref[...] = column_sums(grad * normed, grad, low.astype(F32))
    d_attn = dot(low, w_ref[...], NT).astype(BF)
    half = slots_ref.shape[1]
    hd = slots_ref.shape[2] // 2
    for m in range(micro):
        for j in range(groups * heads_dev):
            piece = d_attn[m * 2 * half : (m + 1) * 2 * half, j * hd : (j + 1) * hd]
            piece = jnp.concatenate([piece[:half], piece[half:]], axis=1)
            first = ((j // heads_dev) * micro + m) * halves
            slots_ref[first + j % heads_dev] = piece
            if j % heads_dev == heads_dev - 1:
                for b in range(heads_dev, halves):
                    slots_ref[first + b] = piece


def tokens_kernel(slots_ref, w_ref, first_ref, out_ref, d_ref, *, layout):
    piece_rows = slots_ref.shape[1] // 3
    total = first_ref[...]
    for c in range(3):
        unpack_heads(slots_ref, d_ref.at[c], layout, piece_rows, c)
        total = total + dot(d_ref[c], w_ref[c], NT)
    out_ref[...] = total.astype(BF)


def normalise(hidden):
    center = hidden - jnp.mean(hidden, axis=-1, keepdims=True)
    spread = jnp.mean(center * center, axis=-1, keepdims=True)
    inverse = lax.rsqrt(spread + norm_eps)
    return center * inverse, inverse


def norm_back(grad, normed, inverse, gain):
    e = grad * gain
    return inverse * (
        e
        - jnp.mean(e, axis=-1, keepdims=True)
        - normed * jnp.mean(e * normed, axis=-1, keepdims=True)
    )


def after(value, *others):
    return lax.optimization_barrier((value, *others))[0]


def by_core(value):
    return lax.ppermute(value, "head", [(0, 1), (1, 0), (2, 3), (3, 2)])


def by_x(value):
    return lax.ppermute(value, "head", [(0, 2), (2, 0), (1, 3), (3, 1)])


def swap(value, axes, groups=None):
    return lax.all_to_all(
        value, axes, split_axis=0, concat_axis=0, tiled=True, axis_index_groups=groups
    )


def spread_over(value, axes, count, groups=None):
    return swap(jnp.broadcast_to(value[None], (count, *value.shape)), axes, groups)


def gather_group(rows):
    across_x = by_x(rows)
    return rows, across_x, by_core(rows), by_core(across_x)


def reduce_group(keep, send):
    count, depth = keep.shape[0] // 2, keep.shape[1]
    shape = (count, depth)
    own, send = call(add_kernel, ((shape, F32), (shape, BF)), (keep, by_core(send)), "add", 1e9)
    return own, by_x(send)


def stack_rows(*values):
    blank = jnp.zeros_like(values[0])
    return jnp.stack([*values, *[blank] * (8 - len(values))])


def in_order(blocks):
    index = lax.axis_index("head")
    own, across_x, across_core, across = blocks
    odd, far = index % 2 == 1, index // 2 == 1
    near = [jnp.where(odd, q, p) for p, q in ((own, across_core), (across_core, own))]
    wide = [jnp.where(odd, q, p) for p, q in ((across_x, across), (across, across_x))]
    return jnp.stack(
        [jnp.where(far, q, p) for p, q in zip(near + wide, wide + near)]
    )


def to_group(blocks):
    index = lax.axis_index("head")

    def block(offset):
        return lax.dynamic_index_in_dim(blocks, index ^ offset, 0, keepdims=False)

    across = lax.ppermute(block(3), "head", [(i, i ^ 3) for i in range(4)])
    return in_order((block(0), by_x(block(2)), by_core(block(1)), across))


def key_ranges(spans, bq, bk):
    return spans[0, ::bq] // bk, cdiv(spans[1, bq - 1 :: bq], bk)


def local(
    inputs,
    doc_lengths,
    grad_out,
    qkv_weight,
    out_weight,
    inner_weight,
    outer_weight,
    bias_rows,
    inner_bias,
    norm_gains,
    norm_shifts,
):
    micro, tokens, depth = inputs.shape
    groups, cycle = lax.axis_size("head"), lax.axis_size("blk")
    halves = cycle // 2
    devices = groups * cycle
    length = devices * tokens
    hd = depth // HEADS
    heads_dev = HEADS // groups
    rows_dev = qkv_weight.shape[1]
    ff_dev = outer_weight.shape[0]
    ff_part = cycle * ff_dev
    half_tokens = tokens // 2
    head_index = lax.axis_index("head")
    blk_index = lax.axis_index("blk")
    half = blk_index // halves
    unit_head = head_index * heads_dev + jnp.minimum(blk_index % halves, heads_dev - 1)
    unit_of = [min(i, heads_dev - 1) for i in range(halves)]

    own_x = lax.dynamic_index_in_dim(inputs, half, 0, keepdims=False)
    other_x = lax.dynamic_index_in_dim(inputs, 1 - half, 0, keepdims=False)
    got_x = lax.ppermute(other_x, "blk", [(i, (i + halves) % cycle) for i in range(cycle)])
    pair_x = jnp.concatenate([own_x, got_x], axis=0)
    cube = [
        [h * cycle + b for h in (c, c + 2) for b in range(s * halves, (s + 1) * halves)]
        for c in range(2)
        for s in range(2)
    ]
    vectors = [bias_rows.T, norm_gains.T, norm_shifts.T, inner_bias.reshape(rows_dev, -1)]
    small = jnp.concatenate(vectors, axis=1)
    small = jnp.pad(small, ((0, 0), (0, hd - small.shape[1])))
    units = tuple(h * heads_dev + u for h in range(groups) for u in unit_of * 2)
    (slots,) = call(
        functools.partial(head_slots_kernel, units=units),
        (((devices, 2, rows_dev, 2 * hd), BF),),
        (qkv_weight, small),
        "head_slots",
        1e9,
    )
    slots = swap(after(slots, pair_x), BOTH)
    qk_weight = slots[:, 0].reshape(depth, 2 * hd)
    v_weight = slots[:, 1].reshape(depth, 2 * hd)
    small = slots[:, 1, :, hd : hd + 12].astype(F32).reshape(depth, 12).T

    bias, gains, shifts = small[0:4], small[4:6], small[6:8]
    inner_bias_all = small[8:12].T.reshape(groups, ff_part)
    inner_bias_part = lax.dynamic_index_in_dim(inner_bias_all, head_index, 0, keepdims=False)
    unit_bias = lax.dynamic_slice(bias[0:2], (0, unit_head * hd), (2, hd))
    unit_bias = jnp.pad(unit_bias, ((0, 0), (0, hd)))

    inner_own = inner_weight.reshape(rows_dev, groups, ff_part)
    inner_own = to_group(inner_own.transpose(1, 0, 2)).reshape(groups * rows_dev, ff_part)
    ffn = jnp.concatenate([inner_own, outer_weight, out_weight])
    qkv_weight = after(qkv_weight, ffn)
    ffn_all = lax.all_gather(ffn, "blk", axis=0, tiled=False)
    qkv_all = lax.all_gather(qkv_weight, BOTH, axis=0, tiled=False)
    tokens_a, qk_weight, v_weight, unit_bias = lax.optimization_barrier(
        (spread_over(pair_x, BOTH, cycle, cube), qk_weight, v_weight, unit_bias)
    )
    tokens_b = by_core(tokens_a)

    lengths = lax.dynamic_index_in_dim(doc_lengths, half, 0, keepdims=False)
    order = jnp.arange(lengths.shape[0], dtype=jnp.int32)
    bounds = jnp.sum(jnp.where(order[None, :] <= order[:, None], lengths[None, :], 0), axis=1)
    positions = jnp.arange(length, dtype=jnp.int32)[None, :]
    starts = (bounds - lengths)[:, None]
    own = (positions >= starts) & (positions < bounds[:, None])
    spans = jnp.stack(
        [
            jnp.sum(jnp.where(own, starts, 0), axis=0),
            jnp.sum(jnp.where(own, bounds[:, None], 0), axis=0),
        ]
    )

    place = jnp.stack([head_index % 2, half]).astype(jnp.int32)
    per = max(1, 256 // tokens)
    q, k, v, kt, vt = project(
        place, tokens_a, tokens_b, qk_weight, v_weight, unit_bias, halves, per
    )
    block = 512 if length <= 4096 else 256
    lo, hi = key_ranges(spans, block, 512)
    attn_out, attn_t, lse = attend(lo, hi, q, k, vt, spans, tokens, block, 512)

    ffn = after(ffn_all, attn_out)
    inner_part = (
        ffn[:, : groups * rows_dev]
        .reshape(cycle, groups, rows_dev, ff_part)
        .transpose(1, 0, 2, 3)
        .reshape(depth, ff_part)
    )
    first, last = groups * rows_dev, groups * rows_dev + ff_dev
    outer_part = ffn[:, first:last].reshape(ff_part, depth)
    out_part = ffn[:, last:].reshape(depth // groups, depth)
    out_all = in_order(gather_group(out_part)).reshape(depth, depth)

    rows = micro * tokens
    layout = (groups, micro, halves, heads_dev)
    flat, group = (rows, depth), (groups * rows, ff_part)
    attn, normed_low, normed_one, inverse_one = call(
        functools.partial(branch_kernel, layout=layout),
        ((flat, BF), (flat, BF), (flat, F32), ((rows, 1), F32)),
        (swap(attn_out, BOTH), inputs.reshape(flat), out_all, stack_rows(bias[2], gains[0], shifts[0])),
        "branch",
        2e9,
    )
    act_low, slope, normed_group, keep, send = call(
        inner_kernel,
        ((group, BF), (group, F32), ((groups * rows, depth), BF), ((2 * rows, depth), F32), ((2 * rows, depth), BF)),
        (*gather_group(normed_low), inner_part, outer_part, inner_bias_part[None]),
        "inner",
        4e9,
    )
    output, d_second, d_ffn, sums_two = call(
        output_kernel,
        ((flat, BF), (flat, F32), (flat, BF), ((8, depth), F32)),
        (
            *reduce_group(keep, send),
            normed_one,
            grad_out.reshape(flat),
            stack_rows(gains[0], shifts[0], bias[3], gains[1], shifts[1]),
        ),
        "output",
        2e9,
    )
    output = output.reshape(inputs.shape)
    d_inner, d_ffn_group, inner_sums, keep, send = call(
        inner_back_kernel,
        ((group, BF), ((groups * rows, depth), BF), ((1, ff_part), F32), ((2 * rows, depth), F32), ((2 * rows, depth), BF)),
        (*gather_group(d_ffn), inner_part, outer_part, slope),
        "inner_back",
        4e9,
    )
    own, got = reduce_group(keep, send)
    (ffn_grad,) = call(
        feed_grad_kernel,
        (((cycle, 2 * groups, rows_dev, depth), BF),),
        (normed_group, d_inner, act_low, d_ffn_group),
        "feed_grad",
        4e9,
        [pltpu.VMEM((depth, depth), F32)],
    )
    got, ffn_grad = lax.optimization_barrier((got, ffn_grad))
    d_first, d_branch, sums_one, d_heads = call(
        functools.partial(branch_back_kernel, layout=layout),
        ((flat, F32), (flat, BF), ((8, depth), F32), ((devices, half_tokens, 2 * hd), BF)),
        (
            own,
            got,
            d_second,
            normed_one,
            inverse_one,
            out_all,
            stack_rows(gains[0]),
        ),
        "branch_back",
        2e9,
    )
    d_heads = swap(d_heads, BOTH)

    ffn_grad = lax.psum_scatter(ffn_grad, "blk", scatter_dimension=0, tiled=False).astype(F32)
    outer_grad = ffn_grad[groups:].reshape(ff_dev, depth)
    inner_grad = to_group(ffn_grad[:groups].astype(BF))
    inner_grad = inner_grad.transpose(1, 0, 2).reshape(rows_dev, groups * ff_part).astype(F32)
    out_grad = dot(attn, d_branch, TN).reshape(groups, depth // groups, depth)

    def out_block(offset):
        return lax.dynamic_index_in_dim(out_grad, head_index ^ offset, 0, keepdims=False)

    from_core = by_core(jnp.stack([out_block(1), out_block(3)]).astype(BF)).astype(F32)
    from_x = by_x((out_block(2) + from_core[1]).astype(BF)).astype(F32)
    out_grad = (out_block(0) + from_core[0] + from_x).astype(BF)
    out_terms = swap(out_grad.reshape(cycle, rows_dev, depth), "blk")
    out_grad = jnp.sum(
        out_terms.astype(F32), axis=0
    )

    lo, hi = key_ranges(spans, 512, 256)
    qkv_out, qkv_t, qv_sums = attend_back(
        lo, hi, q, k, v, kt, attn_t, lse, d_heads, spans, tokens, 512, 256
    )
    qkv_home = swap(after(qkv_out, out_terms), BOTH)
    qkv_all = qkv_all.transpose(1, 0, 2, 3).reshape(3, depth, depth)
    (grad_inputs,) = call(
        functools.partial(tokens_kernel, layout=layout),
        ((flat, BF),),
        (qkv_home, qkv_all, d_first),
        "tokens",
        3e9,
        [pltpu.VMEM((3, rows, depth), BF)],
    )
    grad_inputs = grad_inputs.reshape(inputs.shape)

    unit_grad = weight_grad(place, tokens_a, tokens_b, qkv_t, halves, per)
    wide = jnp.zeros((2, HEADS, hd), F32)
    wide = lax.dynamic_update_slice(wide, qv_sums.reshape(2, 1, hd), (0, unit_head, 0))
    wide = jnp.where((blk_index % halves < heads_dev), wide, 0.0)
    sums = jnp.concatenate([sums_one[:3], sums_two[:3], wide.reshape(2, depth)]).T
    inner_sums = inner_sums.reshape(1, cycle, rows_dev, ff_dev // rows_dev)
    inner_sums = jnp.broadcast_to(inner_sums, (groups, *inner_sums.shape[1:]))
    extra = jnp.concatenate(
        [
            sums.reshape(devices, rows_dev, 8),
            inner_sums.reshape(devices, rows_dev, -1),
        ],
        axis=2,
    ).astype(BF)
    extra = jnp.pad(extra, ((0, 0), (0, 0), (0, hd - extra.shape[2])))
    final = jnp.concatenate([unit_grad.reshape(devices, rows_dev, 3 * hd), extra], axis=2)
    final = swap(after(final, qkv_home), BOTH).astype(F32)
    qkv_grad = jnp.sum(
        final[:, :, : 3 * hd].reshape(groups, micro, halves, rows_dev, 3, hd)[:, :, :heads_dev], axis=1
    )
    qkv_grad = qkv_grad.transpose(3, 2, 0, 1, 4).reshape(3, rows_dev, depth)
    sums = jnp.sum(final[:, :, 3 * hd : 3 * hd + 8], axis=0).T
    inner_sums = final[:, :, 3 * hd + 8 : 3 * hd + 8 + ff_dev // rows_dev]
    inner_sums = lax.dynamic_index_in_dim(
        inner_sums.reshape(groups, cycle, rows_dev, -1), head_index, 0, keepdims=False
    )
    inner_bias_grad = jnp.sum(inner_sums, axis=0).reshape(ff_dev)
    return (
        output,
        grad_inputs,
        qkv_grad,
        out_grad,
        inner_grad,
        outer_grad,
        jnp.stack([sums[6], sums[7], sums[2], sums[5]]),
        inner_bias_grad,
        jnp.stack([sums[0], sums[3]]),
        jnp.stack([sums[1], sums[4]]),
    )


def solution(mesh):
    tokens = P(None, BOTH, None)
    rows = P(BOTH, None)
    columns = P(None, BOTH)
    return jax.shard_map(
        local,
        mesh=mesh,
        in_specs=(tokens, P(), tokens, tokens, rows, rows, rows, columns, P(BOTH), columns, columns),
        out_specs=(tokens, tokens, tokens, rows, rows, rows, columns, P(BOTH), columns, columns),
        check_vma=False,
    )
```

```python
import functools
import math

import jax
import jax.numpy as jnp
from jax import lax
from jax.experimental import pallas as pl
from jax.experimental.pallas import tpu as pltpu
from jax.sharding import PartitionSpec as P

HEADS = 12
F32 = jnp.float32
BF = jnp.bfloat16
NT = (((1,), (1,)), ((), ()))
NN = (((1,), (0,)), ((), ()))
TN = (((0,), (0,)), ((), ()))
LOG2E = math.log2(math.e)
BOTH = ("head", "blk")
norm_eps = 1e-12
masked_score = -1e30
VMEM = pl.BlockSpec(memory_space=pltpu.VMEM)
SMEM = pl.BlockSpec(memory_space=pltpu.SMEM)
SMALL = pltpu.CompilerParams(vmem_limit_bytes=20 << 20)
LARGE = pltpu.CompilerParams(vmem_limit_bytes=56 << 20)


def dot(a, b, dims):
    return lax.dot_general(a, b, dims, preferred_element_type=F32)


def cdiv(a, b):
    return -(-a // b)


def chunk_walk(place_ref, blocks, halves, per, tokens, visit):
    core, half = place_ref[0], place_ref[1]
    runs = halves // per
    for source in range(2):

        def one(n, carry, source=source):
            xh = n // (2 * runs)
            rel = n // runs % 2
            run = n % runs
            head = xh * 2 + (core if source == 0 else 1 - core)
            position = ((head * 2 + (rel ^ half)) * halves + run * per) * tokens
            rows = pl.ds(pl.multiple_of(rel * tokens, tokens), tokens)

            def load(ref):
                return jnp.concatenate(
                    [ref[xh * halves + run * per + k, rows, :] for k in range(per)], axis=0
                )

            visit(source, load, pl.multiple_of(position, per * tokens))
            return carry

        lax.fori_loop(0, 4 * runs, one, 0, unroll=4 * runs <= 4)


def project_kernel(
    place_ref, a_ref, b_ref, qk_ref, v_w_ref, bias_ref, q_ref, k_ref, v_ref, kt_ref, vt_ref, *, halves, per
):
    tokens = a_ref.shape[1] // 2
    hd = q_ref.shape[1]

    def visit(source, load, position):
        x = load((a_ref, b_ref)[source])
        rows = pl.ds(position, per * tokens)
        qk = dot(x, qk_ref[...], NN) + bias_ref[0:1]
        v = (dot(x, v_w_ref[...], NN) + bias_ref[1:2])[:, :hd]
        k = qk[:, hd:]
        q_ref[rows, :] = qk[:, :hd].astype(BF)
        k_ref[rows, :] = k.astype(BF)
        v_ref[rows, :] = v.astype(BF)
        kt_ref[:, rows] = k.T.astype(BF)
        vt_ref[:, rows] = v.T.astype(BF)

    chunk_walk(place_ref, a_ref.shape[0], halves, per, tokens, visit)


def project(place, a, b, qk, v, bias, halves, per):
    length = 2 * a.shape[0] * a.shape[1]
    hd = qk.shape[1] // 2
    rows = jax.ShapeDtypeStruct((length, hd), BF)
    columns = jax.ShapeDtypeStruct((hd, length), BF)
    return pl.pallas_call(
        functools.partial(project_kernel, halves=halves, per=per),
        out_shape=(rows, rows, rows, columns, columns),
        in_specs=[SMEM] + [VMEM] * 5,
        out_specs=(VMEM,) * 5,
        compiler_params=SMALL if length <= 4096 else LARGE,
        cost_estimate=pl.CostEstimate(flops=1000000, bytes_accessed=1 << 10, transcendentals=0),
        name="project",
    )(place, a, b, qk, v, bias)


def head_slots_kernel(w_ref, small_ref, out_ref, *, units):
    hd = small_ref.shape[1]
    small = small_ref[...]
    done = {}
    for d, j in enumerate(units):
        if j not in done:
            part = [w_ref[c][:, j * hd : (j + 1) * hd] for c in range(3)]
            done[j] = [
                jnp.concatenate(part[:2], axis=1),
                jnp.concatenate([part[2], small], axis=1),
            ]
        out_ref[d, 0] = done[j][0]
        out_ref[d, 1] = done[j][1]


def weight_grad_kernel(place_ref, a_ref, b_ref, gt_ref, out_ref, acc_ref, *, halves, per):
    tokens = a_ref.shape[1] // 2
    acc_ref[...] = jnp.zeros_like(acc_ref)

    def visit(source, load, position):
        x = load((a_ref, b_ref)[source])
        acc_ref[...] += dot(gt_ref[:, pl.ds(position, per * tokens)], x, NN)

    chunk_walk(place_ref, a_ref.shape[0], halves, per, tokens, visit)
    out_ref[...] = acc_ref[...].T.astype(BF)


def weight_grad(place, a, b, gt, halves, per):
    depth = a.shape[2]
    length = gt.shape[1]
    return pl.pallas_call(
        functools.partial(weight_grad_kernel, halves=halves, per=per),
        out_shape=jax.ShapeDtypeStruct((depth, gt.shape[0]), BF),
        in_specs=[SMEM] + [VMEM] * 3,
        out_specs=VMEM,
        scratch_shapes=[pltpu.VMEM((gt.shape[0], depth), F32)],
        compiler_params=SMALL if length <= 4096 else LARGE,
        cost_estimate=pl.CostEstimate(flops=1000000, bytes_accessed=1 << 10, transcendentals=0),
        name="weight_grad",
    )(place, a, b, gt)


def inside(first, start, stop, bk):
    key = first + lax.broadcasted_iota(jnp.int32, (bk, start.shape[1]), 0)
    return (key >= start) & (key < stop)


def attend_kernel(
    lo_ref, hi_ref, q_ref, k_ref, vt_ref, span_ref, out_ref, ot_ref, lse_ref, s_ref,
    *, bq, bk, pack
):
    length, hd = q_ref.shape
    factor = LOG2E / math.sqrt(hd)
    half = pack // 2

    def q_step(i, carry):
        qs = pl.ds(pl.multiple_of(i * bq, bq), bq)
        q = q_ref[qs, :]
        start, stop = span_ref[0:1, qs], span_ref[1:2, qs]
        lo, hi = lo_ref[i], hi_ref[i]

        def first(j, top):
            ks = pl.ds(pl.multiple_of(j * bk, bk), bk)
            s = dot(k_ref[ks, :], q, NT) * factor
            s = jnp.where(inside(j * bk, start, stop, bk), s, masked_score)
            s_ref[ks, :] = s
            return jnp.maximum(top, jnp.max(s.reshape(bk // 8, 8, bq), axis=0))

        top = lax.fori_loop(lo, hi, first, jnp.full((8, bq), masked_score, F32))
        peak = jnp.max(top, axis=0, keepdims=True)

        def second(j, state):
            total, acc = state
            ks = pl.ds(pl.multiple_of(j * bk, bk), bk)
            p = jnp.exp2(s_ref[ks, :] - peak)
            total = total + jnp.sum(p.reshape(bk // 8, 8, bq), axis=0)
            return total, acc + dot(vt_ref[:, ks], p.astype(BF), NN)

        total, acc = lax.fori_loop(
            lo, hi, second, (jnp.zeros((8, bq), F32), jnp.zeros((hd, bq), F32))
        )
        total = jnp.sum(total, axis=0, keepdims=True)
        out = acc / total
        ot_ref[:, qs] = out
        lse_ref[:, qs] = peak + jnp.log2(total)
        rows = out.T.astype(BF)
        for c in range(bq // pack):
            piece = rows[c * pack : (c + 1) * pack]
            out_ref[i * (bq // pack) + c] = jnp.concatenate([piece[:half], piece[half:]], axis=1)
        return carry

    lax.fori_loop(0, length // bq, q_step, 0)


def attend(lo, hi, q, k, vt, spans, pack, bq, bk):
    length, hd = q.shape
    return pl.pallas_call(
        functools.partial(attend_kernel, bq=bq, bk=bk, pack=pack),
        out_shape=(
            jax.ShapeDtypeStruct((length // pack, pack // 2, 2 * hd), BF),
            jax.ShapeDtypeStruct((hd, length), F32),
            jax.ShapeDtypeStruct((1, length), F32),
        ),
        in_specs=[SMEM, SMEM] + [VMEM] * 4,
        out_specs=(VMEM,) * 3,
        scratch_shapes=[pltpu.VMEM((length, bq), F32)],
        compiler_params=SMALL if length <= 4096 else LARGE,
        cost_estimate=pl.CostEstimate(flops=1000000, bytes_accessed=1 << 10, transcendentals=0),
        name="attend",
    )(lo, hi, q, k, vt, spans)


def attend_back_kernel(
    lo_ref, hi_ref, q_ref, k_ref, v_ref, kt_ref, ot_ref, lse_ref, do_ref, span_ref,
    out_ref, gt_ref, sums_ref, dq_ref, dk_ref, dv_ref, *, bq, bk, pack
):
    length, hd = q_ref.shape
    scale = 1.0 / math.sqrt(hd)
    factor = LOG2E * scale
    half = pack // 2
    dk_ref[...] = jnp.zeros_like(dk_ref)
    dv_ref[...] = jnp.zeros_like(dv_ref)

    def q_step(i, carry):
        qs = pl.ds(pl.multiple_of(i * bq, bq), bq)
        q = q_ref[qs, :]
        start, stop = span_ref[0:1, qs], span_ref[1:2, qs]
        pieces = []
        for c in range(bq // pack):
            piece = do_ref[i * (bq // pack) + c]
            pieces += [piece[:, :hd], piece[:, hd:]]
        do = jnp.concatenate(pieces, axis=0)
        delta = jnp.sum(do.astype(F32).T * ot_ref[:, qs], axis=0, keepdims=True)
        lse = lse_ref[:, qs]

        def step(j, acc):
            ks = pl.ds(pl.multiple_of(j * bk, bk), bk)
            s = dot(k_ref[ks, :], q, NT) * factor - lse
            p = jnp.where(inside(j * bk, start, stop, bk), jnp.exp2(s), 0.0)
            dp = dot(v_ref[ks, :], do, NT)
            ds = (p * (dp - delta)).astype(BF)
            dv_ref[ks, :] += dot(p.astype(BF), do, NN)
            dk_ref[ks, :] += dot(ds, q, NN)
            return acc + dot(kt_ref[:, ks], ds, NN)

        acc = lax.fori_loop(lo_ref[i], hi_ref[i], step, jnp.zeros((hd, bq), F32))
        dq_ref[:, qs] = acc
        return carry

    lax.fori_loop(0, length // bq, q_step, 0)

    def emit(i, sums):
        rows = pl.ds(pl.multiple_of(i * bq, bq), bq)
        dqt = (dq_ref[:, rows] * scale).astype(BF)
        dk = (dk_ref[rows, :] * scale).astype(BF)
        dv = dv_ref[rows, :].astype(BF)
        dq = dqt.astype(F32).T.astype(BF)
        gt_ref[0:hd, rows] = dqt
        gt_ref[hd : 2 * hd, rows] = dk.astype(F32).T.astype(BF)
        gt_ref[2 * hd : 3 * hd, rows] = dv.astype(F32).T.astype(BF)
        for c in range(bq // pack):
            for n, value in enumerate((dq, dk, dv)):
                piece = value[c * pack : (c + 1) * pack]
                out_ref[i * (bq // pack) + c, n * half : (n + 1) * half, :] = jnp.concatenate(
                    [piece[:half], piece[half:]], axis=1
                )
        both = jnp.concatenate([dq.astype(F32), dv.astype(F32)], axis=1)
        return sums + jnp.sum(both, axis=0, keepdims=True)

    sums_ref[...] = lax.fori_loop(0, length // bq, emit, jnp.zeros((1, 2 * hd), F32))


def attend_back(lo, hi, q, k, v, kt, ot, lse, do, spans, pack, bq, bk):
    length, hd = q.shape
    return pl.pallas_call(
        functools.partial(attend_back_kernel, bq=bq, bk=bk, pack=pack),
        out_shape=(
            jax.ShapeDtypeStruct((length // pack, 3 * pack // 2, 2 * hd), BF),
            jax.ShapeDtypeStruct((3 * hd, length), BF),
            jax.ShapeDtypeStruct((1, 2 * hd), F32),
        ),
        in_specs=[SMEM, SMEM] + [VMEM] * 8,
        out_specs=(VMEM,) * 3,
        scratch_shapes=[
            pltpu.VMEM((hd, length), F32),
            pltpu.VMEM((length, hd), F32),
            pltpu.VMEM((length, hd), F32),
        ],
        compiler_params=SMALL if length <= 4096 else LARGE,
        cost_estimate=pl.CostEstimate(flops=1000000, bytes_accessed=1 << 10, transcendentals=0),
        name="attend_back",
    )(lo, hi, q, k, v, kt, ot, lse, do, spans)


def call(kernel, outs, ins, name, flops, scratch=()):
    return pl.pallas_call(
        kernel,
        out_shape=tuple(jax.ShapeDtypeStruct(shape, kind) for shape, kind in outs),
        in_specs=[SMEM if v.dtype == jnp.int32 else VMEM for v in ins],
        out_specs=(VMEM,) * len(outs),
        scratch_shapes=list(scratch),
        compiler_params=SMALL,
        cost_estimate=pl.CostEstimate(
            flops=int(flops), bytes_accessed=1 << 10, transcendentals=0
        ),
        name=name,
    )(*ins)


def column_sums(*values):
    sums = [jnp.sum(v, axis=0, keepdims=True) for v in values]
    return jnp.concatenate(sums + [jnp.zeros_like(sums[0])] * (8 - len(sums)), axis=0)


def unpack_heads(slots_ref, out_ref, layout, piece_rows, which):
    groups, micro, halves, heads_dev = layout
    hd = slots_ref.shape[2] // 2
    part = slice(which * piece_rows, (which + 1) * piece_rows)
    for m in range(micro):
        rows = slice(m * 2 * piece_rows, (m + 1) * 2 * piece_rows)
        pieces = []
        for j in range(groups * heads_dev):
            piece = slots_ref[((j // heads_dev) * micro + m) * halves + j % heads_dev, part, :]
            pieces.append(jnp.concatenate([piece[:, :hd], piece[:, hd:]], axis=0))
        for j in range(0, groups * heads_dev, 2):
            out_ref[rows, j * hd : (j + 2) * hd] = jnp.concatenate(pieces[j : j + 2], axis=1)


def branch_kernel(slots_ref, x_ref, w_ref, vec_ref, attn_ref, low_ref, normed_ref, inv_ref, *, layout):
    unpack_heads(slots_ref, attn_ref, layout, slots_ref.shape[1], 0)
    first_sum = x_ref[...].astype(F32) + dot(attn_ref[...], w_ref[...], NN) + vec_ref[0:1]
    normed, inverse = normalise(first_sum)
    normed_ref[...] = normed
    inv_ref[...] = inverse
    low_ref[...] = (normed * vec_ref[1:2] + vec_ref[2:3]).astype(BF)


def normal_cdf(v):
    bell = jnp.exp(-0.5 * v * v)
    t = 1.0 / (1.0 + (0.3275911 * math.sqrt(0.5)) * jnp.abs(v))
    tail = 0.5 * 1.061405429
    for c in (-1.453152027, 1.421413741, -0.284496736, 0.254829592):
        tail = tail * t + 0.5 * c
    tail = tail * t * bell
    return jnp.where(v < 0.0, tail, 1.0 - tail), bell * (1.0 / math.sqrt(2.0 * math.pi))


def inner_kernel(a_ref, b_ref, c_ref, d_ref, wi_ref, wo_ref, bias_ref, act_ref, slope_ref, low_ref, keep_ref, send_ref):
    count = a_ref.shape[0]
    for n, ref in enumerate((a_ref, b_ref, c_ref, d_ref)):
        rows = slice(n * count, (n + 1) * count)
        x = ref[...]
        low_ref[rows, :] = x
        pre = dot(x, wi_ref[...], NN) + bias_ref[...]
        cdf, bell = normal_cdf(pre)
        slope_ref[rows, :] = cdf + pre * bell
        act = (pre * cdf).astype(BF)
        act_ref[rows, :] = act
        partial = dot(act, wo_ref[...], NN)
        if n < 2:
            keep_ref[rows, :] = partial
        else:
            send_ref[(n - 2) * count : (n - 1) * count, :] = partial.astype(BF)


def inner_back_kernel(a_ref, b_ref, c_ref, d_ref, wi_ref, wo_ref, slope_ref, inner_ref, low_ref, sums_ref, keep_ref, send_ref):
    count = a_ref.shape[0]
    sums = 0.0
    for n, ref in enumerate((a_ref, b_ref, c_ref, d_ref)):
        rows = slice(n * count, (n + 1) * count)
        x = ref[...]
        low_ref[rows, :] = x
        inner = (dot(x, wo_ref[...], NT) * slope_ref[rows, :]).astype(BF)
        inner_ref[rows, :] = inner
        sums = sums + jnp.sum(inner.astype(F32), axis=0, keepdims=True)
        partial = dot(inner, wi_ref[...], NT)
        if n < 2:
            keep_ref[rows, :] = partial
        else:
            send_ref[(n - 2) * count : (n - 1) * count, :] = partial.astype(BF)
    sums_ref[...] = sums


def feed_grad_kernel(low_ref, inner_ref, act_ref, ffn_ref, out_ref, acc_ref):
    cycle, blocks, rows = out_ref.shape[:3]
    half = blocks // 2
    acc_ref[...] = dot(low_ref[...], inner_ref[...], TN)
    for b in range(cycle):
        for h in range(half):
            first = (h * cycle + b) * rows
            out_ref[b, h] = acc_ref[first : first + rows, :].astype(BF)
    acc_ref[...] = dot(act_ref[...], ffn_ref[...], TN)
    for b in range(cycle):
        for h in range(half):
            first = (b * half + h) * rows
            out_ref[b, half + h] = acc_ref[first : first + rows, :].astype(BF)


def collect_kernel(head_ref, slots_ref, qkv_ref, bias_ref, gains_ref, shifts_ref, inner_ref, *, layout):
    groups, micro, halves, heads_dev = layout
    hd = slots_ref.shape[2] // 4
    cycle = micro * halves
    pieces = []
    for j in range(groups * heads_dev):
        first = (j // heads_dev) * cycle + j % heads_dev
        piece = slots_ref[first, :, : 3 * hd].astype(F32)
        for m in range(1, micro):
            piece = piece + slots_ref[first + m * halves, :, : 3 * hd].astype(F32)
        pieces.append(piece)
    for c in range(3):
        for j in range(0, groups * heads_dev, 2):
            pair = [p[:, c * hd : (c + 1) * hd] for p in pieces[j : j + 2]]
            qkv_ref[c, :, j * hd : (j + 2) * hd] = jnp.concatenate(pair, axis=1)
    own = slots_ref[pl.ds(head_ref[0] * cycle, cycle), :, 3 * hd :].astype(F32)
    inner_ref[...] = jnp.sum(own, axis=0)
    sums = jnp.sum(slots_ref[:, :, 3 * hd :].astype(F32), axis=0).T
    bias_ref[...] = sums[0:4]
    gains_ref[...] = sums[4:6]
    shifts_ref[...] = sums[6:8]


def add_kernel(keep_ref, got_ref, own_ref, send_ref):
    count = own_ref.shape[0]
    own_ref[...] = keep_ref[:count] + got_ref[:count].astype(F32)
    send_ref[...] = (keep_ref[count:] + got_ref[count:].astype(F32)).astype(BF)


def output_kernel(own_ref, got_ref, normed_ref, grad_ref, vec_ref, out_ref, second_ref, low_ref, sums_ref):
    first_normed = normed_ref[...] * vec_ref[0:1] + vec_ref[1:2]
    second_sum = first_normed + own_ref[...] + got_ref[...].astype(F32) + vec_ref[2:3]
    normed, inverse = normalise(second_sum)
    out_ref[...] = (normed * vec_ref[3:4] + vec_ref[4:5]).astype(BF)
    grad = grad_ref[...].astype(F32)
    d_second = norm_back(grad, normed, inverse, vec_ref[3:4])
    low = d_second.astype(BF)
    second_ref[...] = d_second
    low_ref[...] = low
    sums_ref[...] = column_sums(grad * normed, grad, low.astype(F32))


def branch_back_kernel(own_ref, got_ref, second_ref, normed_ref, inv_ref, w_ref, vec_ref, first_ref, low_ref, sums_ref, slots_ref, *, layout):
    groups, micro, halves, heads_dev = layout
    grad = own_ref[...] + got_ref[...].astype(F32) + second_ref[...]
    normed = normed_ref[...]
    d_first = norm_back(grad, normed, inv_ref[...], vec_ref[0:1])
    low = d_first.astype(BF)
    first_ref[...] = d_first
    low_ref[...] = low
    sums_ref[...] = column_sums(grad * normed, grad, low.astype(F32))
    d_attn = dot(low, w_ref[...], NT).astype(BF)
    half = slots_ref.shape[1]
    hd = slots_ref.shape[2] // 2
    for m in range(micro):
        for j in range(groups * heads_dev):
            piece = d_attn[m * 2 * half : (m + 1) * 2 * half, j * hd : (j + 1) * hd]
            piece = jnp.concatenate([piece[:half], piece[half:]], axis=1)
            first = ((j // heads_dev) * micro + m) * halves
            slots_ref[first + j % heads_dev] = piece
            if j % heads_dev == heads_dev - 1:
                for b in range(heads_dev, halves):
                    slots_ref[first + b] = piece


def tokens_kernel(slots_ref, w_ref, first_ref, out_ref, d_ref, *, layout):
    piece_rows = slots_ref.shape[1] // 3
    total = first_ref[...]
    for c in range(3):
        unpack_heads(slots_ref, d_ref.at[c], layout, piece_rows, c)
        total = total + dot(d_ref[c], w_ref[c], NT)
    out_ref[...] = total.astype(BF)


def normalise(hidden):
    center = hidden - jnp.mean(hidden, axis=-1, keepdims=True)
    spread = jnp.mean(center * center, axis=-1, keepdims=True)
    inverse = lax.rsqrt(spread + norm_eps)
    return center * inverse, inverse


def norm_back(grad, normed, inverse, gain):
    e = grad * gain
    return inverse * (
        e
        - jnp.mean(e, axis=-1, keepdims=True)
        - normed * jnp.mean(e * normed, axis=-1, keepdims=True)
    )


def after(value, *others):
    return lax.optimization_barrier((value, *others))[0]


def by_core(value):
    return lax.ppermute(value, "head", [(0, 1), (1, 0), (2, 3), (3, 2)])


def by_x(value):
    return lax.ppermute(value, "head", [(0, 2), (2, 0), (1, 3), (3, 1)])


def swap(value, axes, groups=None):
    return lax.all_to_all(
        value, axes, split_axis=0, concat_axis=0, tiled=True, axis_index_groups=groups
    )


def spread_over(value, axes, count, groups=None):
    return swap(jnp.broadcast_to(value[None], (count, *value.shape)), axes, groups)


def gather_group(rows):
    across_x = by_x(rows)
    return rows, across_x, by_core(rows), by_core(across_x)


def reduce_group(keep, send):
    count, depth = keep.shape[0] // 2, keep.shape[1]
    shape = (count, depth)
    own, send = call(add_kernel, ((shape, F32), (shape, BF)), (keep, by_core(send)), "add", 1e6)
    return own, by_x(send)


def stack_rows(*values):
    blank = jnp.zeros_like(values[0])
    return jnp.stack([*values, *[blank] * (8 - len(values))])


def in_order(blocks):
    index = lax.axis_index("head")
    own, across_x, across_core, across = blocks
    odd, far = index % 2 == 1, index // 2 == 1
    near = [jnp.where(odd, q, p) for p, q in ((own, across_core), (across_core, own))]
    wide = [jnp.where(odd, q, p) for p, q in ((across_x, across), (across, across_x))]
    return jnp.stack(
        [jnp.where(far, q, p) for p, q in zip(near + wide, wide + near)]
    )


def to_group(blocks):
    index = lax.axis_index("head")

    def block(offset):
        return lax.dynamic_index_in_dim(blocks, index ^ offset, 0, keepdims=False)

    across = lax.ppermute(block(3), "head", [(i, i ^ 3) for i in range(4)])
    return in_order((block(0), by_x(block(2)), by_core(block(1)), across))


def key_ranges(spans, bq, bk):
    return spans[0, ::bq] // bk, cdiv(spans[1, bq - 1 :: bq], bk)


def local(
    inputs,
    doc_lengths,
    grad_out,
    qkv_weight,
    out_weight,
    inner_weight,
    outer_weight,
    bias_rows,
    inner_bias,
    norm_gains,
    norm_shifts,
):
    micro, tokens, depth = inputs.shape
    groups, cycle = lax.axis_size("head"), lax.axis_size("blk")
    halves = cycle // 2
    devices = groups * cycle
    length = devices * tokens
    hd = depth // HEADS
    heads_dev = HEADS // groups
    rows_dev = qkv_weight.shape[1]
    ff_dev = outer_weight.shape[0]
    ff_part = cycle * ff_dev
    half_tokens = tokens // 2
    head_index = lax.axis_index("head")
    blk_index = lax.axis_index("blk")
    half = blk_index // halves
    unit_head = head_index * heads_dev + jnp.minimum(blk_index % halves, heads_dev - 1)
    unit_of = [min(i, heads_dev - 1) for i in range(halves)]

    own_x = lax.dynamic_index_in_dim(inputs, half, 0, keepdims=False)
    other_x = lax.dynamic_index_in_dim(inputs, 1 - half, 0, keepdims=False)
    got_x = lax.ppermute(other_x, "blk", [(i, (i + halves) % cycle) for i in range(cycle)])
    pair_x = jnp.concatenate([own_x, got_x], axis=0)
    cube = [
        [h * cycle + b for h in (c, c + 2) for b in range(s * halves, (s + 1) * halves)]
        for c in range(2)
        for s in range(2)
    ]
    inner_own = inner_weight.reshape(rows_dev, groups, ff_part)
    inner_own = to_group(inner_own.transpose(1, 0, 2)).reshape(groups * rows_dev, ff_part)
    ffn = jnp.concatenate([inner_own, outer_weight])

    vectors = [bias_rows.T, norm_gains.T, norm_shifts.T, inner_bias.reshape(rows_dev, -1)]
    small = jnp.concatenate(vectors, axis=1)
    small = jnp.pad(small, ((0, 0), (0, hd - small.shape[1])))
    units = tuple(h * heads_dev + u for h in range(groups) for u in unit_of * 2)
    (slots,) = call(
        functools.partial(head_slots_kernel, units=units),
        (((devices, 2, rows_dev, 2 * hd), BF),),
        (qkv_weight, small),
        "head_slots",
        1e6,
    )
    slots = swap(after(slots, pair_x, ffn), BOTH)
    qk_weight = slots[:, 0].reshape(depth, 2 * hd)
    v_weight = slots[:, 1].reshape(depth, 2 * hd)
    small = slots[:, 1, :, hd : hd + 12].astype(F32).reshape(depth, 12).T

    bias, gains, shifts = small[0:4], small[4:6], small[6:8]
    inner_bias_all = small[8:12].T.reshape(groups, ff_part)
    inner_bias_part = lax.dynamic_index_in_dim(inner_bias_all, head_index, 0, keepdims=False)
    unit_bias = lax.dynamic_slice(bias[0:2], (0, unit_head * hd), (2, hd))
    unit_bias = jnp.pad(unit_bias, ((0, 0), (0, hd)))

    ffn_all = lax.all_gather(after(ffn, slots), "blk", axis=0, tiled=False)
    qkv_all = lax.all_gather(after(qkv_weight, ffn), BOTH, axis=0, tiled=False)
    small_rows = (
        stack_rows(bias[2], gains[0], shifts[0]),
        stack_rows(gains[0], shifts[0], bias[3], gains[1], shifts[1]),
        stack_rows(gains[0]),
        inner_bias_part[None],
    )
    tokens_a, qk_weight, v_weight, unit_bias, small_rows = lax.optimization_barrier(
        (spread_over(pair_x, BOTH, cycle, cube), qk_weight, v_weight, unit_bias, small_rows)
    )
    tokens_b = by_core(tokens_a)
    out_part = spread_over(after(out_weight, tokens_a), "blk", cycle).reshape(depth // groups, depth)

    lengths = lax.dynamic_index_in_dim(doc_lengths, half, 0, keepdims=False)
    order = jnp.arange(lengths.shape[0], dtype=jnp.int32)
    bounds = jnp.sum(jnp.where(order[None, :] <= order[:, None], lengths[None, :], 0), axis=1)
    positions = jnp.arange(length, dtype=jnp.int32)[None, :]
    starts = (bounds - lengths)[:, None]
    own = (positions >= starts) & (positions < bounds[:, None])
    spans = jnp.stack(
        [
            jnp.sum(jnp.where(own, starts, 0), axis=0),
            jnp.sum(jnp.where(own, bounds[:, None], 0), axis=0),
        ]
    )

    place = jnp.stack([head_index % 2, half]).astype(jnp.int32)
    per = max(1, 256 // tokens)
    q, k, v, kt, vt = project(
        place, tokens_a, tokens_b, qk_weight, v_weight, unit_bias, halves, per
    )
    block = 512 if length <= 4096 else 256
    lo, hi = key_ranges(spans, block, 512)
    attn_out, attn_t, lse = attend(lo, hi, q, k, vt, spans, tokens, block, 512)

    ffn = after(ffn_all, attn_out)
    inner_part = (
        ffn[:, : groups * rows_dev]
        .reshape(cycle, groups, rows_dev, ff_part)
        .transpose(1, 0, 2, 3)
        .reshape(depth, ff_part)
    )
    outer_part = ffn[:, groups * rows_dev :].reshape(ff_part, depth)
    attn_slots = swap(attn_out, BOTH)
    out_x, attn_slots, inner_part, outer_part = lax.optimization_barrier(
        (by_x(out_part), attn_slots, inner_part, outer_part)
    )
    out_all = in_order((out_part, out_x, by_core(out_part), by_core(out_x))).reshape(depth, depth)

    rows = micro * tokens
    layout = (groups, micro, halves, heads_dev)
    flat, group = (rows, depth), (groups * rows, ff_part)
    attn, normed_low, normed_one, inverse_one = call(
        functools.partial(branch_kernel, layout=layout),
        ((flat, BF), (flat, BF), (flat, F32), ((rows, 1), F32)),
        (attn_slots, inputs.reshape(flat), out_all, small_rows[0]),
        "branch",
        1e6,
    )
    act_low, slope, normed_group, keep, send = call(
        inner_kernel,
        ((group, BF), (group, F32), ((groups * rows, depth), BF), ((2 * rows, depth), F32), ((2 * rows, depth), BF)),
        (*gather_group(normed_low), inner_part, outer_part, small_rows[3]),
        "inner",
        1e6,
    )
    output, d_second, d_ffn, sums_two = call(
        output_kernel,
        ((flat, BF), (flat, F32), (flat, BF), ((8, depth), F32)),
        (
            *reduce_group(keep, send),
            normed_one,
            grad_out.reshape(flat),
            small_rows[1],
        ),
        "output",
        1e6,
    )
    output = output.reshape(inputs.shape)
    d_inner, d_ffn_group, inner_sums, keep, send = call(
        inner_back_kernel,
        ((group, BF), ((groups * rows, depth), BF), ((1, ff_part), F32), ((2 * rows, depth), F32), ((2 * rows, depth), BF)),
        (*gather_group(d_ffn), inner_part, outer_part, slope),
        "inner_back",
        1e6,
    )
    own, got = reduce_group(keep, send)
    (ffn_grad,) = call(
        feed_grad_kernel,
        (((cycle, 2 * groups, rows_dev, depth), BF),),
        (normed_group, d_inner, act_low, d_ffn_group),
        "feed_grad",
        1e6,
        [pltpu.VMEM((depth, depth), F32)],
    )
    got, ffn_grad = lax.optimization_barrier((got, ffn_grad))
    d_first, d_branch, sums_one, d_heads = call(
        functools.partial(branch_back_kernel, layout=layout),
        ((flat, F32), (flat, BF), ((8, depth), F32), ((devices, half_tokens, 2 * hd), BF)),
        (
            own,
            got,
            d_second,
            normed_one,
            inverse_one,
            out_all,
            small_rows[2],
        ),
        "branch_back",
        1e6,
    )
    d_heads = swap(d_heads, BOTH)

    ffn_grad = lax.psum_scatter(ffn_grad, "blk", scatter_dimension=0, tiled=False).astype(F32)
    outer_grad = ffn_grad[groups:].reshape(ff_dev, depth)
    inner_grad = to_group(ffn_grad[:groups].astype(BF))
    inner_grad = inner_grad.transpose(1, 0, 2).reshape(rows_dev, groups * ff_part).astype(F32)
    out_grad = dot(attn, d_branch, TN).reshape(groups, depth // groups, depth)

    def out_block(offset):
        return lax.dynamic_index_in_dim(out_grad, head_index ^ offset, 0, keepdims=False)

    from_core = by_core(jnp.stack([out_block(1), out_block(3)]).astype(BF)).astype(F32)
    from_x = by_x((out_block(2) + from_core[1]).astype(BF)).astype(F32)
    out_grad = (out_block(0) + from_core[0] + from_x).astype(BF)
    out_terms = swap(out_grad.reshape(cycle, rows_dev, depth), "blk")
    out_grad = jnp.sum(
        out_terms.astype(F32), axis=0
    )

    lo, hi = key_ranges(spans, 512, 256)
    qkv_out, qkv_t, qv_sums = attend_back(
        lo, hi, q, k, v, kt, attn_t, lse, d_heads, spans, tokens, 512, 256
    )
    qkv_home = swap(after(qkv_out, out_terms), BOTH)
    qkv_all = qkv_all.transpose(1, 0, 2, 3).reshape(3, depth, depth)
    (grad_inputs,) = call(
        functools.partial(tokens_kernel, layout=layout),
        ((flat, BF),),
        (qkv_home, qkv_all, d_first),
        "tokens",
        1e6,
        [pltpu.VMEM((3, rows, depth), BF)],
    )
    grad_inputs = grad_inputs.reshape(inputs.shape)

    unit_grad = weight_grad(place, tokens_a, tokens_b, qkv_t, halves, per)
    wide = jnp.zeros((2, HEADS, hd), F32)
    wide = lax.dynamic_update_slice(wide, qv_sums.reshape(2, 1, hd), (0, unit_head, 0))
    wide = jnp.where((blk_index % halves < heads_dev), wide, 0.0)
    sums = jnp.stack(
        [wide[0].reshape(depth), wide[1].reshape(depth), sums_one[2], sums_two[2]]
        + [sums_one[0], sums_two[0], sums_one[1], sums_two[1]]
    ).T
    inner_sums = inner_sums.reshape(1, cycle, rows_dev, ff_dev // rows_dev)
    inner_sums = jnp.broadcast_to(inner_sums, (groups, *inner_sums.shape[1:]))
    extra = jnp.concatenate(
        [
            sums.reshape(devices, rows_dev, 8),
            inner_sums.reshape(devices, rows_dev, -1),
        ],
        axis=2,
    ).astype(BF)
    extra = jnp.pad(extra, ((0, 0), (0, 0), (0, hd - extra.shape[2])))
    final = jnp.concatenate([unit_grad.reshape(devices, rows_dev, 3 * hd), extra], axis=2)
    final = swap(after(final, qkv_home), BOTH)
    final, inner_grad = lax.optimization_barrier((final, inner_grad))
    qkv_grad, bias_grad, gains_grad, shifts_grad, inner_bias_grad = call(
        functools.partial(collect_kernel, layout=layout),
        (
            ((3, rows_dev, depth), F32),
            ((4, rows_dev), F32),
            ((2, rows_dev), F32),
            ((2, rows_dev), F32),
            ((rows_dev, hd), F32),
        ),
        (head_index[None], final),
        "collect",
        1e6,
    )
    return (
        output,
        grad_inputs,
        qkv_grad,
        out_grad,
        inner_grad,
        outer_grad,
        bias_grad,
        inner_bias_grad[:, 8 : 8 + ff_dev // rows_dev].reshape(ff_dev),
        gains_grad,
        shifts_grad,
    )


def solution(mesh):
    tokens = P(None, BOTH, None)
    rows = P(BOTH, None)
    columns = P(None, BOTH)
    return jax.shard_map(
        local,
        mesh=mesh,
        in_specs=(tokens, P(), tokens, tokens, rows, rows, rows, columns, P(BOTH), columns, columns),
        out_specs=(tokens, tokens, tokens, rows, rows, rows, columns, P(BOTH), columns, columns),
        check_vma=False,
    )
```

```python
import functools
import math

import jax
import jax.numpy as jnp
from jax import lax
from jax.experimental import pallas as pl
from jax.experimental.pallas import tpu as pltpu
from jax.sharding import PartitionSpec as P

HEADS = 12
F32 = jnp.float32
BF = jnp.bfloat16
NT = (((1,), (1,)), ((), ()))
NN = (((1,), (0,)), ((), ()))
TN = (((0,), (0,)), ((), ()))
LOG2E = math.log2(math.e)
BOTH = ("head", "blk")
norm_eps = 1e-12
masked_score = -1e30
VMEM = pl.BlockSpec(memory_space=pltpu.VMEM)
SMEM = pl.BlockSpec(memory_space=pltpu.SMEM)
SMALL = pltpu.CompilerParams(vmem_limit_bytes=20 << 20)
LARGE = pltpu.CompilerParams(vmem_limit_bytes=56 << 20)


def dot(a, b, dims):
    return lax.dot_general(a, b, dims, preferred_element_type=F32)


def cdiv(a, b):
    return -(-a // b)


def chunk_walk(place_ref, blocks, halves, per, tokens, visit):
    core, half = place_ref[0], place_ref[1]
    runs = halves // per
    for source in range(2):

        def one(n, carry, source=source):
            xh = n // (2 * runs)
            rel = n // runs % 2
            run = n % runs
            head = xh * 2 + (core if source == 0 else 1 - core)
            position = ((head * 2 + (rel ^ half)) * halves + run * per) * tokens
            rows = pl.ds(pl.multiple_of(rel * tokens, tokens), tokens)

            def load(ref):
                return jnp.concatenate(
                    [ref[xh * halves + run * per + k, rows, :] for k in range(per)], axis=0
                )

            visit(source, load, pl.multiple_of(position, per * tokens))
            return carry

        lax.fori_loop(0, 4 * runs, one, 0, unroll=4 * runs <= 4)


def project_kernel(
    place_ref, a_ref, b_ref, qk_ref, v_w_ref, bias_ref, q_ref, k_ref, v_ref, kt_ref, vt_ref, *, halves, per
):
    tokens = a_ref.shape[1] // 2
    hd = q_ref.shape[1]

    def visit(source, load, position):
        x = load((a_ref, b_ref)[source])
        rows = pl.ds(position, per * tokens)
        qk = dot(x, qk_ref[...], NN) + bias_ref[0:1]
        v = (dot(x, v_w_ref[...], NN) + bias_ref[1:2])[:, :hd]
        k = qk[:, hd:]
        q_ref[rows, :] = qk[:, :hd].astype(BF)
        k_ref[rows, :] = k.astype(BF)
        v_ref[rows, :] = v.astype(BF)
        kt_ref[:, rows] = k.T.astype(BF)
        vt_ref[:, rows] = v.T.astype(BF)

    chunk_walk(place_ref, a_ref.shape[0], halves, per, tokens, visit)


def project(place, a, b, qk, v, bias, halves, per):
    length = 2 * a.shape[0] * a.shape[1]
    hd = qk.shape[1] // 2
    rows = jax.ShapeDtypeStruct((length, hd), BF)
    columns = jax.ShapeDtypeStruct((hd, length), BF)
    return pl.pallas_call(
        functools.partial(project_kernel, halves=halves, per=per),
        out_shape=(rows, rows, rows, columns, columns),
        in_specs=[SMEM] + [VMEM] * 5,
        out_specs=(VMEM,) * 5,
        compiler_params=LARGE,
        cost_estimate=pl.CostEstimate(flops=1000000, bytes_accessed=1 << 10, transcendentals=0),
        name="project",
    )(place, a, b, qk, v, bias)


def head_slots_kernel(w_ref, bias_ref, gains_ref, shifts_ref, inner_ref, out_ref, *, units):
    hd = w_ref.shape[2] // HEADS
    rows = [ref[...].astype(F32) for ref in (bias_ref, gains_ref, shifts_ref)]
    inner = inner_ref[...].astype(F32)
    blank = jnp.zeros((inner.shape[0], hd - 8 - inner.shape[1]), F32)
    small = jnp.concatenate([jnp.concatenate(rows, axis=0).T, inner, blank], axis=1).astype(BF)
    done = {}
    for d, j in enumerate(units):
        if j not in done:
            part = [w_ref[c][:, j * hd : (j + 1) * hd] for c in range(3)]
            done[j] = [
                jnp.concatenate(part[:2], axis=1),
                jnp.concatenate([part[2], small], axis=1),
            ]
        out_ref[d, 0] = done[j][0]
        out_ref[d, 1] = done[j][1]


def weight_grad_kernel(place_ref, a_ref, b_ref, gt_ref, out_ref, acc_ref, *, halves, per):
    tokens = a_ref.shape[1] // 2
    acc_ref[...] = jnp.zeros_like(acc_ref)

    def visit(source, load, position):
        x = load((a_ref, b_ref)[source])
        acc_ref[...] += dot(gt_ref[:, pl.ds(position, per * tokens)], x, NN)

    chunk_walk(place_ref, a_ref.shape[0], halves, per, tokens, visit)
    out_ref[...] = acc_ref[...].T.astype(BF)


def weight_grad(place, a, b, gt, halves, per):
    depth = a.shape[2]
    length = gt.shape[1]
    return pl.pallas_call(
        functools.partial(weight_grad_kernel, halves=halves, per=per),
        out_shape=jax.ShapeDtypeStruct((depth, gt.shape[0]), BF),
        in_specs=[SMEM] + [VMEM] * 3,
        out_specs=VMEM,
        scratch_shapes=[pltpu.VMEM((gt.shape[0], depth), F32)],
        compiler_params=SMALL if length <= 4096 else LARGE,
        cost_estimate=pl.CostEstimate(flops=1000000, bytes_accessed=1 << 10, transcendentals=0),
        name="weight_grad",
    )(place, a, b, gt)


def inside(first, start, stop, bk):
    key = first + lax.broadcasted_iota(jnp.int32, (bk, start.shape[1]), 0)
    return (key >= start) & (key < stop)


def attend_kernel(
    lo_ref, hi_ref, q_ref, k_ref, vt_ref, span_ref, out_ref, ot_ref, lse_ref, s_ref,
    *, bq, bk, pack
):
    length, hd = q_ref.shape
    factor = LOG2E / math.sqrt(hd)
    half = pack // 2

    def q_step(i, carry):
        qs = pl.ds(pl.multiple_of(i * bq, bq), bq)
        q = q_ref[qs, :]
        start, stop = span_ref[0:1, qs], span_ref[1:2, qs]
        lo, hi = lo_ref[i], hi_ref[i]

        def first(j, top):
            ks = pl.ds(pl.multiple_of(j * bk, bk), bk)
            s = dot(k_ref[ks, :], q, NT) * factor
            s = jnp.where(inside(j * bk, start, stop, bk), s, masked_score)
            s_ref[ks, :] = s
            return jnp.maximum(top, jnp.max(s.reshape(bk // 8, 8, bq), axis=0))

        top = lax.fori_loop(lo, hi, first, jnp.full((8, bq), masked_score, F32))
        peak = jnp.max(top, axis=0, keepdims=True)

        def second(j, state):
            total, acc = state
            ks = pl.ds(pl.multiple_of(j * bk, bk), bk)
            p = jnp.exp2(s_ref[ks, :] - peak)
            total = total + jnp.sum(p.reshape(bk // 8, 8, bq), axis=0)
            return total, acc + dot(vt_ref[:, ks], p.astype(BF), NN)

        total, acc = lax.fori_loop(
            lo, hi, second, (jnp.zeros((8, bq), F32), jnp.zeros((hd, bq), F32))
        )
        total = jnp.sum(total, axis=0, keepdims=True)
        out = acc / total
        ot_ref[:, qs] = out
        lse_ref[:, qs] = peak + jnp.log2(total)
        rows = out.T.astype(BF)
        for c in range(bq // pack):
            piece = rows[c * pack : (c + 1) * pack]
            out_ref[i * (bq // pack) + c] = jnp.concatenate([piece[:half], piece[half:]], axis=1)
        return carry

    lax.fori_loop(0, length // bq, q_step, 0)


def attend(lo, hi, q, k, vt, spans, pack, bq, bk):
    length, hd = q.shape
    return pl.pallas_call(
        functools.partial(attend_kernel, bq=bq, bk=bk, pack=pack),
        out_shape=(
            jax.ShapeDtypeStruct((length // pack, pack // 2, 2 * hd), BF),
            jax.ShapeDtypeStruct((hd, length), F32),
            jax.ShapeDtypeStruct((1, length), F32),
        ),
        in_specs=[SMEM, SMEM] + [VMEM] * 4,
        out_specs=(VMEM,) * 3,
        scratch_shapes=[pltpu.VMEM((length, bq), F32)],
        compiler_params=LARGE,
        cost_estimate=pl.CostEstimate(flops=1000000, bytes_accessed=1 << 10, transcendentals=0),
        name="attend",
    )(lo, hi, q, k, vt, spans)


def attend_back_kernel(
    lo_ref, hi_ref, q_ref, k_ref, v_ref, kt_ref, ot_ref, lse_ref, do_ref, span_ref,
    out_ref, gt_ref, sums_ref, dq_ref, dk_ref, dv_ref, *, bq, bk, pack
):
    length, hd = q_ref.shape
    scale = 1.0 / math.sqrt(hd)
    factor = LOG2E * scale
    half = pack // 2
    dk_ref[...] = jnp.zeros_like(dk_ref)
    dv_ref[...] = jnp.zeros_like(dv_ref)

    def q_step(i, carry):
        qs = pl.ds(pl.multiple_of(i * bq, bq), bq)
        q = q_ref[qs, :]
        start, stop = span_ref[0:1, qs], span_ref[1:2, qs]
        pieces = []
        for c in range(bq // pack):
            piece = do_ref[i * (bq // pack) + c]
            pieces += [piece[:, :hd], piece[:, hd:]]
        do = jnp.concatenate(pieces, axis=0)
        delta = jnp.sum(do.astype(F32).T * ot_ref[:, qs], axis=0, keepdims=True)
        lse = lse_ref[:, qs]

        def step(j, acc):
            ks = pl.ds(pl.multiple_of(j * bk, bk), bk)
            s = dot(k_ref[ks, :], q, NT) * factor - lse
            p = jnp.where(inside(j * bk, start, stop, bk), jnp.exp2(s), 0.0)
            dp = dot(v_ref[ks, :], do, NT)
            ds = (p * (dp - delta)).astype(BF)
            dv_ref[ks, :] += dot(p.astype(BF), do, NN)
            dk_ref[ks, :] += dot(ds, q, NN)
            return acc + dot(kt_ref[:, ks], ds, NN)

        acc = lax.fori_loop(lo_ref[i], hi_ref[i], step, jnp.zeros((hd, bq), F32))
        dq_ref[:, qs] = acc
        return carry

    lax.fori_loop(0, length // bq, q_step, 0)

    def emit(i, sums):
        rows = pl.ds(pl.multiple_of(i * bq, bq), bq)
        dqt = (dq_ref[:, rows] * scale).astype(BF)
        dk = (dk_ref[rows, :] * scale).astype(BF)
        dv = dv_ref[rows, :].astype(BF)
        dq = dqt.astype(F32).T.astype(BF)
        gt_ref[0:hd, rows] = dqt
        gt_ref[hd : 2 * hd, rows] = dk.astype(F32).T.astype(BF)
        gt_ref[2 * hd : 3 * hd, rows] = dv.astype(F32).T.astype(BF)
        for c in range(bq // pack):
            for n, value in enumerate((dq, dk, dv)):
                piece = value[c * pack : (c + 1) * pack]
                out_ref[i * (bq // pack) + c, n * half : (n + 1) * half, :] = jnp.concatenate(
                    [piece[:half], piece[half:]], axis=1
                )
        both = jnp.concatenate([dq.astype(F32), dv.astype(F32)], axis=1)
        return sums + jnp.sum(both, axis=0, keepdims=True)

    sums_ref[...] = lax.fori_loop(0, length // bq, emit, jnp.zeros((1, 2 * hd), F32))


def attend_back(lo, hi, q, k, v, kt, ot, lse, do, spans, pack, bq, bk):
    length, hd = q.shape
    return pl.pallas_call(
        functools.partial(attend_back_kernel, bq=bq, bk=bk, pack=pack),
        out_shape=(
            jax.ShapeDtypeStruct((length // pack, 3 * pack // 2, 2 * hd), BF),
            jax.ShapeDtypeStruct((3 * hd, length), BF),
            jax.ShapeDtypeStruct((1, 2 * hd), F32),
        ),
        in_specs=[SMEM, SMEM] + [VMEM] * 8,
        out_specs=(VMEM,) * 3,
        scratch_shapes=[
            pltpu.VMEM((hd, length), F32),
            pltpu.VMEM((length, hd), F32),
            pltpu.VMEM((length, hd), F32),
        ],
        compiler_params=LARGE,
        cost_estimate=pl.CostEstimate(flops=1000000, bytes_accessed=1 << 10, transcendentals=0),
        name="attend_back",
    )(lo, hi, q, k, v, kt, ot, lse, do, spans)


def call(kernel, outs, ins, name, flops, scratch=(), params=SMALL):
    return pl.pallas_call(
        kernel,
        out_shape=tuple(jax.ShapeDtypeStruct(shape, kind) for shape, kind in outs),
        in_specs=[SMEM if v.dtype == jnp.int32 else VMEM for v in ins],
        out_specs=(VMEM,) * len(outs),
        scratch_shapes=list(scratch),
        compiler_params=params,
        cost_estimate=pl.CostEstimate(
            flops=int(flops), bytes_accessed=1 << 10, transcendentals=0
        ),
        name=name,
    )(*ins)


def column_sums(*values):
    sums = [jnp.sum(v, axis=0, keepdims=True) for v in values]
    return jnp.concatenate(sums + [jnp.zeros_like(sums[0])] * (8 - len(sums)), axis=0)


def unpack_heads(slots_ref, out_ref, layout, piece_rows, which):
    groups, micro, halves, heads_dev = layout
    hd = slots_ref.shape[2] // 2
    part = slice(which * piece_rows, (which + 1) * piece_rows)
    for m in range(micro):
        rows = slice(m * 2 * piece_rows, (m + 1) * 2 * piece_rows)
        pieces = []
        for j in range(groups * heads_dev):
            piece = slots_ref[((j // heads_dev) * micro + m) * halves + j % heads_dev, part, :]
            pieces.append(jnp.concatenate([piece[:, :hd], piece[:, hd:]], axis=0))
        for j in range(0, groups * heads_dev, 2):
            out_ref[rows, j * hd : (j + 2) * hd] = jnp.concatenate(pieces[j : j + 2], axis=1)


def branch_kernel(slots_ref, x_ref, w_ref, vec_ref, attn_ref, low_ref, normed_ref, inv_ref, *, layout):
    unpack_heads(slots_ref, attn_ref, layout, slots_ref.shape[1], 0)
    first_sum = x_ref[...].astype(F32) + dot(attn_ref[...], w_ref[...], NN) + vec_ref[0:1]
    normed, inverse = normalise(first_sum)
    normed_ref[...] = normed
    inv_ref[...] = inverse
    low_ref[...] = (normed * vec_ref[1:2] + vec_ref[2:3]).astype(BF)


def normal_cdf(v):
    bell = jnp.exp(-0.5 * v * v)
    t = 1.0 / (1.0 + (0.3275911 * math.sqrt(0.5)) * jnp.abs(v))
    tail = 0.5 * 1.061405429
    for c in (-1.453152027, 1.421413741, -0.284496736, 0.254829592):
        tail = tail * t + 0.5 * c
    tail = tail * t * bell
    return jnp.where(v < 0.0, tail, 1.0 - tail), bell * (1.0 / math.sqrt(2.0 * math.pi))


def inner_kernel(a_ref, b_ref, c_ref, d_ref, wi_ref, wo_ref, bias_ref, act_ref, slope_ref, low_ref, keep_ref, send_ref):
    count = a_ref.shape[0]
    for n, ref in enumerate((a_ref, b_ref, c_ref, d_ref)):
        rows = slice(n * count, (n + 1) * count)
        x = ref[...]
        low_ref[rows, :] = x
        pre = dot(x, wi_ref[...], NN) + bias_ref[...]
        cdf, bell = normal_cdf(pre)
        slope_ref[rows, :] = cdf + pre * bell
        act = (pre * cdf).astype(BF)
        act_ref[rows, :] = act
        partial = dot(act, wo_ref[...], NN)
        if n < 2:
            keep_ref[rows, :] = partial
        else:
            send_ref[(n - 2) * count : (n - 1) * count, :] = partial.astype(BF)


def inner_back_kernel(a_ref, b_ref, c_ref, d_ref, wi_ref, wo_ref, slope_ref, inner_ref, low_ref, sums_ref, keep_ref, send_ref):
    count = a_ref.shape[0]
    sums = 0.0
    for n, ref in enumerate((a_ref, b_ref, c_ref, d_ref)):
        rows = slice(n * count, (n + 1) * count)
        x = ref[...]
        low_ref[rows, :] = x
        inner = (dot(x, wo_ref[...], NT) * slope_ref[rows, :]).astype(BF)
        inner_ref[rows, :] = inner
        sums = sums + jnp.sum(inner.astype(F32), axis=0, keepdims=True)
        partial = dot(inner, wi_ref[...], NT)
        if n < 2:
            keep_ref[rows, :] = partial
        else:
            send_ref[(n - 2) * count : (n - 1) * count, :] = partial.astype(BF)
    sums_ref[...] = sums


def feed_grad_kernel(low_ref, inner_ref, act_ref, ffn_ref, out_ref, acc_ref):
    cycle, blocks, rows = out_ref.shape[:3]
    half = blocks // 2
    acc_ref[...] = dot(low_ref[...], inner_ref[...], TN)
    for b in range(cycle):
        for h in range(half):
            first = (h * cycle + b) * rows
            out_ref[b, h] = acc_ref[first : first + rows, :].astype(BF)
    acc_ref[...] = dot(act_ref[...], ffn_ref[...], TN)
    for b in range(cycle):
        for h in range(half):
            first = (b * half + h) * rows
            out_ref[b, half + h] = acc_ref[first : first + rows, :].astype(BF)


def collect_kernel(head_ref, slots_ref, qkv_ref, bias_ref, gains_ref, shifts_ref, inner_ref, *, layout):
    groups, micro, halves, heads_dev = layout
    hd = slots_ref.shape[2] // 4
    cycle = micro * halves
    pieces = []
    for j in range(groups * heads_dev):
        first = (j // heads_dev) * cycle + j % heads_dev
        piece = slots_ref[first, :, : 3 * hd].astype(F32)
        for m in range(1, micro):
            piece = piece + slots_ref[first + m * halves, :, : 3 * hd].astype(F32)
        pieces.append(piece)
    for c in range(3):
        for j in range(0, groups * heads_dev, 2):
            pair = [p[:, c * hd : (c + 1) * hd] for p in pieces[j : j + 2]]
            qkv_ref[c, :, j * hd : (j + 2) * hd] = jnp.concatenate(pair, axis=1)
    own = slots_ref[pl.ds(head_ref[0] * cycle, cycle), :, 3 * hd :].astype(F32)
    inner_ref[...] = jnp.sum(own, axis=0)
    sums = jnp.sum(slots_ref[:, :, 3 * hd :].astype(F32), axis=0).T
    bias_ref[...] = sums[0:4]
    gains_ref[...] = sums[4:6]
    shifts_ref[...] = sums[6:8]


def add_kernel(keep_ref, got_ref, own_ref, send_ref):
    count = own_ref.shape[0]
    own_ref[...] = keep_ref[:count] + got_ref[:count].astype(F32)
    send_ref[...] = (keep_ref[count:] + got_ref[count:].astype(F32)).astype(BF)


def output_kernel(own_ref, got_ref, normed_ref, grad_ref, vec_ref, out_ref, second_ref, low_ref, sums_ref):
    first_normed = normed_ref[...] * vec_ref[0:1] + vec_ref[1:2]
    second_sum = first_normed + own_ref[...] + got_ref[...].astype(F32) + vec_ref[2:3]
    normed, inverse = normalise(second_sum)
    out_ref[...] = (normed * vec_ref[3:4] + vec_ref[4:5]).astype(BF)
    grad = grad_ref[...].astype(F32)
    d_second = norm_back(grad, normed, inverse, vec_ref[3:4])
    low = d_second.astype(BF)
    second_ref[...] = d_second
    low_ref[...] = low
    sums_ref[...] = column_sums(grad * normed, grad, low.astype(F32))


def branch_back_kernel(own_ref, got_ref, second_ref, normed_ref, inv_ref, w_ref, vec_ref, first_ref, low_ref, sums_ref, slots_ref, *, layout):
    groups, micro, halves, heads_dev = layout
    grad = own_ref[...] + got_ref[...].astype(F32) + second_ref[...]
    normed = normed_ref[...]
    d_first = norm_back(grad, normed, inv_ref[...], vec_ref[0:1])
    low = d_first.astype(BF)
    first_ref[...] = d_first
    low_ref[...] = low
    sums_ref[...] = column_sums(grad * normed, grad, low.astype(F32))
    d_attn = dot(low, w_ref[...], NT).astype(BF)
    half = slots_ref.shape[1]
    hd = slots_ref.shape[2] // 2
    for m in range(micro):
        for j in range(groups * heads_dev):
            piece = d_attn[m * 2 * half : (m + 1) * 2 * half, j * hd : (j + 1) * hd]
            piece = jnp.concatenate([piece[:half], piece[half:]], axis=1)
            first = ((j // heads_dev) * micro + m) * halves
            slots_ref[first + j % heads_dev] = piece
            if j % heads_dev == heads_dev - 1:
                for b in range(heads_dev, halves):
                    slots_ref[first + b] = piece


def tokens_kernel(slots_ref, w_ref, first_ref, out_ref, d_ref, *, layout):
    piece_rows = slots_ref.shape[1] // 3
    total = first_ref[...]
    for c in range(3):
        unpack_heads(slots_ref, d_ref.at[c], layout, piece_rows, c)
        total = total + dot(d_ref[c], w_ref[c], NT)
    out_ref[...] = total.astype(BF)


def normalise(hidden):
    center = hidden - jnp.mean(hidden, axis=-1, keepdims=True)
    spread = jnp.mean(center * center, axis=-1, keepdims=True)
    inverse = lax.rsqrt(spread + norm_eps)
    return center * inverse, inverse


def norm_back(grad, normed, inverse, gain):
    e = grad * gain
    return inverse * (
        e
        - jnp.mean(e, axis=-1, keepdims=True)
        - normed * jnp.mean(e * normed, axis=-1, keepdims=True)
    )


def after(value, *others):
    return lax.optimization_barrier((value, *others))[0]


def by_core(value):
    return lax.ppermute(value, "head", [(0, 1), (1, 0), (2, 3), (3, 2)])


def by_x(value):
    return lax.ppermute(value, "head", [(0, 2), (2, 0), (1, 3), (3, 1)])


def swap(value, axes, groups=None):
    return lax.all_to_all(
        value, axes, split_axis=0, concat_axis=0, tiled=True, axis_index_groups=groups
    )


def spread_over(value, axes, count, groups=None):
    return swap(jnp.broadcast_to(value[None], (count, *value.shape)), axes, groups)


def gather_group(rows):
    across_x = by_x(rows)
    return rows, across_x, by_core(rows), by_core(across_x)


def reduce_group(keep, send):
    count, depth = keep.shape[0] // 2, keep.shape[1]
    shape = (count, depth)
    own, send = call(add_kernel, ((shape, F32), (shape, BF)), (keep, by_core(send)), "add", 1e6)
    return own, by_x(send)


def stack_rows(*values):
    blank = jnp.zeros_like(values[0])
    return jnp.stack([*values, *[blank] * (8 - len(values))])


def in_order(blocks):
    index = lax.axis_index("head")
    own, across_x, across_core, across = blocks
    odd, far = index % 2 == 1, index // 2 == 1
    near = [jnp.where(odd, q, p) for p, q in ((own, across_core), (across_core, own))]
    wide = [jnp.where(odd, q, p) for p, q in ((across_x, across), (across, across_x))]
    return jnp.stack(
        [jnp.where(far, q, p) for p, q in zip(near + wide, wide + near)]
    )


def to_group(blocks):
    index = lax.axis_index("head")

    def block(offset):
        return lax.dynamic_index_in_dim(blocks, index ^ offset, 0, keepdims=False)

    across = lax.ppermute(block(3), "head", [(i, i ^ 3) for i in range(4)])
    return in_order((block(0), by_x(block(2)), by_core(block(1)), across))


def key_ranges(spans, bq, bk):
    return spans[0, ::bq] // bk, cdiv(spans[1, bq - 1 :: bq], bk)


def local(
    inputs,
    doc_lengths,
    grad_out,
    qkv_weight,
    out_weight,
    inner_weight,
    outer_weight,
    bias_rows,
    inner_bias,
    norm_gains,
    norm_shifts,
):
    micro, tokens, depth = inputs.shape
    groups, cycle = lax.axis_size("head"), lax.axis_size("blk")
    halves = cycle // 2
    devices = groups * cycle
    length = devices * tokens
    hd = depth // HEADS
    heads_dev = HEADS // groups
    rows_dev = qkv_weight.shape[1]
    ff_dev = outer_weight.shape[0]
    ff_part = cycle * ff_dev
    half_tokens = tokens // 2
    head_index = lax.axis_index("head")
    blk_index = lax.axis_index("blk")
    half = blk_index // halves
    unit_head = head_index * heads_dev + jnp.minimum(blk_index % halves, heads_dev - 1)
    unit_of = [min(i, heads_dev - 1) for i in range(halves)]

    own_x = lax.dynamic_index_in_dim(inputs, half, 0, keepdims=False)
    other_x = lax.dynamic_index_in_dim(inputs, 1 - half, 0, keepdims=False)
    got_x = lax.ppermute(other_x, "blk", [(i, (i + halves) % cycle) for i in range(cycle)])
    pair_x = jnp.concatenate([own_x, got_x], axis=0)
    cube = [
        [h * cycle + b for h in (c, c + 2) for b in range(s * halves, (s + 1) * halves)]
        for c in range(2)
        for s in range(2)
    ]
    inner_own = after(inner_weight, pair_x).reshape(rows_dev, groups, ff_part)
    inner_own = to_group(inner_own.transpose(1, 0, 2)).reshape(groups * rows_dev, ff_part)
    ffn = jnp.concatenate([inner_own, outer_weight, out_weight])

    units = tuple(h * heads_dev + u for h in range(groups) for u in unit_of * 2)
    (slots,) = call(
        functools.partial(head_slots_kernel, units=units),
        (((devices, 2, rows_dev, 2 * hd), BF),),
        (qkv_weight, bias_rows, norm_gains, norm_shifts, inner_bias.reshape(rows_dev, -1)),
        "head_slots",
        1e6,
        params=LARGE,
    )
    slots = swap(slots, BOTH)
    qk_weight = slots[:, 0].reshape(depth, 2 * hd)
    v_weight = slots[:, 1].reshape(depth, 2 * hd)
    small = slots[:, 1, :, hd : hd + 12].astype(F32).reshape(depth, 12).T

    bias, gains, shifts = small[0:4], small[4:6], small[6:8]
    inner_bias_all = small[8:12].T.reshape(groups, ff_part)
    inner_bias_part = lax.dynamic_index_in_dim(inner_bias_all, head_index, 0, keepdims=False)
    unit_bias = lax.dynamic_slice(bias[0:2], (0, unit_head * hd), (2, hd))
    unit_bias = jnp.pad(unit_bias, ((0, 0), (0, hd)))

    qkv_all = lax.all_gather(after(qkv_weight, ffn), BOTH, axis=0, tiled=False)
    ffn_all = lax.all_gather(after(ffn, slots), "blk", axis=0, tiled=False)
    lengths = lax.dynamic_index_in_dim(doc_lengths, half, 0, keepdims=False)
    order = jnp.arange(lengths.shape[0], dtype=jnp.int32)
    bounds = jnp.sum(jnp.where(order[None, :] <= order[:, None], lengths[None, :], 0), axis=1)
    positions = jnp.arange(length, dtype=jnp.int32)[None, :]
    starts = (bounds - lengths)[:, None]
    own = (positions >= starts) & (positions < bounds[:, None])
    spans = jnp.stack(
        [
            jnp.sum(jnp.where(own, starts, 0), axis=0),
            jnp.sum(jnp.where(own, bounds[:, None], 0), axis=0),
        ]
    )

    place = jnp.stack([head_index % 2, half]).astype(jnp.int32)
    block = 512 if length <= 4096 else 256
    ranges = key_ranges(spans, block, 512), key_ranges(spans, 512, 256)
    small_rows = (
        stack_rows(bias[2], gains[0], shifts[0]),
        stack_rows(gains[0], shifts[0], bias[3], gains[1], shifts[1]),
        stack_rows(gains[0]),
        inner_bias_part[None],
    )
    tokens_a = spread_over(pair_x, BOTH, cycle, cube)
    prepared = (qk_weight, v_weight, unit_bias, small_rows, spans, place, ranges)
    tokens_a, prepared = lax.optimization_barrier((tokens_a, prepared))
    qk_weight, v_weight, unit_bias, small_rows, spans, place, ranges = prepared
    tokens_b = by_core(tokens_a)

    per = max(1, 256 // tokens)
    q, k, v, kt, vt = project(
        place, tokens_a, tokens_b, qk_weight, v_weight, unit_bias, halves, per
    )
    lo, hi = ranges[0]
    attn_out, attn_t, lse = attend(lo, hi, q, k, vt, spans, tokens, block, 512)

    ffn = after(ffn_all, attn_out)
    inner_part = (
        ffn[:, : groups * rows_dev]
        .reshape(cycle, groups, rows_dev, ff_part)
        .transpose(1, 0, 2, 3)
        .reshape(depth, ff_part)
    )
    last = groups * rows_dev + ff_dev
    outer_part = ffn[:, groups * rows_dev : last].reshape(ff_part, depth)
    out_part = ffn[:, last:].reshape(depth // groups, depth)
    attn_slots = swap(attn_out, BOTH)
    out_x, attn_slots, inner_part, outer_part = lax.optimization_barrier(
        (by_x(out_part), attn_slots, inner_part, outer_part)
    )
    out_all = in_order((out_part, out_x, by_core(out_part), by_core(out_x))).reshape(depth, depth)

    rows = micro * tokens
    layout = (groups, micro, halves, heads_dev)
    flat, group = (rows, depth), (groups * rows, ff_part)
    attn, normed_low, normed_one, inverse_one = call(
        functools.partial(branch_kernel, layout=layout),
        ((flat, BF), (flat, BF), (flat, F32), ((rows, 1), F32)),
        (attn_slots, inputs.reshape(flat), out_all, small_rows[0]),
        "branch",
        1e6,
    )
    act_low, slope, normed_group, keep, send = call(
        inner_kernel,
        ((group, BF), (group, F32), ((groups * rows, depth), BF), ((2 * rows, depth), F32), ((2 * rows, depth), BF)),
        (*gather_group(normed_low), inner_part, outer_part, small_rows[3]),
        "inner",
        1e6,
    )
    output, d_second, d_ffn, sums_two = call(
        output_kernel,
        ((flat, BF), (flat, F32), (flat, BF), ((8, depth), F32)),
        (
            *reduce_group(keep, send),
            normed_one,
            grad_out.reshape(flat),
            small_rows[1],
        ),
        "output",
        1e6,
    )
    output = output.reshape(inputs.shape)
    d_inner, d_ffn_group, inner_sums, keep, send = call(
        inner_back_kernel,
        ((group, BF), ((groups * rows, depth), BF), ((1, ff_part), F32), ((2 * rows, depth), F32), ((2 * rows, depth), BF)),
        (*gather_group(d_ffn), inner_part, outer_part, slope),
        "inner_back",
        1e6,
    )
    own, got = reduce_group(keep, send)
    (ffn_grad,) = call(
        feed_grad_kernel,
        (((cycle, 2 * groups, rows_dev, depth), BF),),
        (normed_group, d_inner, act_low, d_ffn_group),
        "feed_grad",
        1e6,
        [pltpu.VMEM((depth, depth), F32)],
    )
    got, ffn_grad = lax.optimization_barrier((got, ffn_grad))
    d_first, d_branch, sums_one, d_heads = call(
        functools.partial(branch_back_kernel, layout=layout),
        ((flat, F32), (flat, BF), ((8, depth), F32), ((devices, half_tokens, 2 * hd), BF)),
        (
            own,
            got,
            d_second,
            normed_one,
            inverse_one,
            out_all,
            small_rows[2],
        ),
        "branch_back",
        1e6,
    )
    d_heads = swap(d_heads, BOTH)

    ffn_grad = lax.psum_scatter(ffn_grad, "blk", scatter_dimension=0, tiled=False)
    outer_grad = ffn_grad[groups:].reshape(ff_dev, depth).astype(F32)
    inner_grad = to_group(ffn_grad[:groups])
    inner_grad = inner_grad.transpose(1, 0, 2).reshape(rows_dev, groups * ff_part).astype(F32)
    out_grad = dot(attn, d_branch, TN).reshape(groups, depth // groups, depth)

    def out_block(offset):
        return lax.dynamic_index_in_dim(out_grad, head_index ^ offset, 0, keepdims=False)

    from_core = by_core(jnp.stack([out_block(1), out_block(3)]).astype(BF)).astype(F32)
    from_x = by_x((out_block(2) + from_core[1]).astype(BF)).astype(F32)
    out_grad = (out_block(0) + from_core[0] + from_x).astype(BF)
    out_terms = swap(out_grad.reshape(cycle, rows_dev, depth), "blk")
    out_grad = jnp.sum(
        out_terms.astype(F32), axis=0
    )

    lo, hi = ranges[1]
    qkv_out, qkv_t, qv_sums = attend_back(
        lo, hi, q, k, v, kt, attn_t, lse, d_heads, spans, tokens, 512, 256
    )
    qkv_home = swap(after(qkv_out, out_terms), BOTH)
    qkv_all = qkv_all.transpose(1, 0, 2, 3).reshape(3, depth, depth)
    (grad_inputs,) = call(
        functools.partial(tokens_kernel, layout=layout),
        ((flat, BF),),
        (qkv_home, qkv_all, d_first),
        "tokens",
        1e6,
        [pltpu.VMEM((3, rows, depth), BF)],
    )
    grad_inputs = grad_inputs.reshape(inputs.shape)

    unit_grad = weight_grad(place, tokens_a, tokens_b, qkv_t, halves, per)
    wide = jnp.zeros((2, HEADS, hd), F32)
    wide = lax.dynamic_update_slice(wide, qv_sums.reshape(2, 1, hd), (0, unit_head, 0))
    wide = jnp.where((blk_index % halves < heads_dev), wide, 0.0)
    sums = jnp.stack(
        [wide[0].reshape(depth), wide[1].reshape(depth), sums_one[2], sums_two[2]]
        + [sums_one[0], sums_two[0], sums_one[1], sums_two[1]]
    ).T
    inner_sums = inner_sums.reshape(1, cycle, rows_dev, ff_dev // rows_dev)
    inner_sums = jnp.broadcast_to(inner_sums, (groups, *inner_sums.shape[1:]))
    extra = jnp.concatenate(
        [
            sums.reshape(devices, rows_dev, 8),
            inner_sums.reshape(devices, rows_dev, -1),
        ],
        axis=2,
    ).astype(BF)
    extra = jnp.pad(extra, ((0, 0), (0, 0), (0, hd - extra.shape[2])))
    final = jnp.concatenate([unit_grad.reshape(devices, rows_dev, 3 * hd), extra], axis=2)
    final = after(swap(after(final, qkv_home), BOTH), grad_inputs)
    qkv_grad, bias_grad, gains_grad, shifts_grad, inner_bias_grad = call(
        functools.partial(collect_kernel, layout=layout),
        (
            ((3, rows_dev, depth), F32),
            ((4, rows_dev), F32),
            ((2, rows_dev), F32),
            ((2, rows_dev), F32),
            ((rows_dev, hd), F32),
        ),
        (head_index[None], final),
        "collect",
        1e6,
    )
    return (
        output,
        grad_inputs,
        qkv_grad,
        out_grad,
        inner_grad,
        outer_grad,
        bias_grad,
        inner_bias_grad[:, 8 : 8 + ff_dev // rows_dev].reshape(ff_dev),
        gains_grad,
        shifts_grad,
    )


def solution(mesh):
    tokens = P(None, BOTH, None)
    rows = P(BOTH, None)
    columns = P(None, BOTH)
    return jax.shard_map(
        local,
        mesh=mesh,
        in_specs=(tokens, P(), tokens, tokens, rows, rows, rows, columns, P(BOTH), columns, columns),
        out_specs=(tokens, tokens, tokens, rows, rows, rows, columns, P(BOTH), columns, columns),
        check_vma=False,
    )
```

```python
import functools
import math

import jax
import jax.numpy as jnp
from jax import lax
from jax.experimental import pallas as pl
from jax.experimental.pallas import tpu as pltpu
from jax.sharding import PartitionSpec as P

HEADS = 12
F32 = jnp.float32
BF = jnp.bfloat16
NT = (((1,), (1,)), ((), ()))
NN = (((1,), (0,)), ((), ()))
TN = (((0,), (0,)), ((), ()))
LOG2E = math.log2(math.e)
BOTH = ("head", "blk")
norm_eps = 1e-12
masked_score = -1e30
VMEM = pl.BlockSpec(memory_space=pltpu.VMEM)
SMEM = pl.BlockSpec(memory_space=pltpu.SMEM)
SMALL = pltpu.CompilerParams(vmem_limit_bytes=20 << 20)
LARGE = pltpu.CompilerParams(vmem_limit_bytes=56 << 20)


def dot(a, b, dims):
    return lax.dot_general(a, b, dims, preferred_element_type=F32)


def cdiv(a, b):
    return -(-a // b)


def chunk_walk(place_ref, blocks, halves, per, tokens, visit):
    core, half = place_ref[0], place_ref[1]
    runs = halves // per
    for source in range(2):

        def one(n, carry, source=source):
            xh = n // (2 * runs)
            rel = n // runs % 2
            run = n % runs
            head = xh * 2 + (core if source == 0 else 1 - core)
            position = ((head * 2 + (rel ^ half)) * halves + run * per) * tokens
            rows = pl.ds(pl.multiple_of(rel * tokens, tokens), tokens)

            def load(ref):
                return jnp.concatenate(
                    [ref[xh * halves + run * per + k, rows, :] for k in range(per)], axis=0
                )

            visit(source, load, pl.multiple_of(position, per * tokens))
            return carry

        lax.fori_loop(0, 4 * runs, one, 0, unroll=4 * runs <= 4)


def project_kernel(
    place_ref, a_ref, b_ref, qk_ref, v_w_ref, bias_ref, q_ref, k_ref, v_ref, kt_ref, vt_ref, *, halves, per
):
    tokens = a_ref.shape[1] // 2
    hd = q_ref.shape[1]

    def visit(source, load, position):
        x = load((a_ref, b_ref)[source])
        rows = pl.ds(position, per * tokens)
        qk = dot(x, qk_ref[...], NN) + bias_ref[0:1]
        v = (dot(x, v_w_ref[...], NN) + bias_ref[1:2])[:, :hd]
        k = qk[:, hd:]
        q_ref[rows, :] = qk[:, :hd].astype(BF)
        k_ref[rows, :] = k.astype(BF)
        v_ref[rows, :] = v.astype(BF)
        kt_ref[:, rows] = k.T.astype(BF)
        vt_ref[:, rows] = v.T.astype(BF)

    chunk_walk(place_ref, a_ref.shape[0], halves, per, tokens, visit)


def project(place, a, b, qk, v, bias, halves, per):
    length = 2 * a.shape[0] * a.shape[1]
    hd = qk.shape[1] // 2
    rows = jax.ShapeDtypeStruct((length, hd), BF)
    columns = jax.ShapeDtypeStruct((hd, length), BF)
    return pl.pallas_call(
        functools.partial(project_kernel, halves=halves, per=per),
        out_shape=(rows, rows, rows, columns, columns),
        in_specs=[SMEM] + [VMEM] * 5,
        out_specs=(VMEM,) * 5,
        compiler_params=LARGE,
        cost_estimate=pl.CostEstimate(flops=1000000, bytes_accessed=1 << 10, transcendentals=0),
        name="project",
    )(place, a, b, qk, v, bias)


def head_slots_kernel(w_ref, bias_ref, gains_ref, shifts_ref, inner_ref, out_ref, *, units):
    hd = w_ref.shape[2] // HEADS
    rows = [ref[...].astype(F32) for ref in (bias_ref, gains_ref, shifts_ref)]
    inner = inner_ref[...].astype(F32)
    blank = jnp.zeros((inner.shape[0], hd - 8 - inner.shape[1]), F32)
    small = jnp.concatenate([jnp.concatenate(rows, axis=0).T, inner, blank], axis=1).astype(BF)
    done = {}
    for d, j in enumerate(units):
        if j not in done:
            part = [w_ref[c][:, j * hd : (j + 1) * hd] for c in range(3)]
            done[j] = [
                jnp.concatenate(part[:2], axis=1),
                jnp.concatenate([part[2], small], axis=1),
            ]
        out_ref[d, 0] = done[j][0]
        out_ref[d, 1] = done[j][1]


def weight_grad_kernel(place_ref, a_ref, b_ref, gt_ref, out_ref, acc_ref, *, halves, per):
    tokens = a_ref.shape[1] // 2
    acc_ref[...] = jnp.zeros_like(acc_ref)

    def visit(source, load, position):
        x = load((a_ref, b_ref)[source])
        acc_ref[...] += dot(gt_ref[:, pl.ds(position, per * tokens)], x, NN)

    chunk_walk(place_ref, a_ref.shape[0], halves, per, tokens, visit)
    out_ref[...] = acc_ref[...].T.astype(BF)


def weight_grad(place, a, b, gt, halves, per):
    depth = a.shape[2]
    length = gt.shape[1]
    return pl.pallas_call(
        functools.partial(weight_grad_kernel, halves=halves, per=per),
        out_shape=jax.ShapeDtypeStruct((depth, gt.shape[0]), BF),
        in_specs=[SMEM] + [VMEM] * 3,
        out_specs=VMEM,
        scratch_shapes=[pltpu.VMEM((gt.shape[0], depth), F32)],
        compiler_params=SMALL if length <= 4096 else LARGE,
        cost_estimate=pl.CostEstimate(flops=1000000, bytes_accessed=1 << 10, transcendentals=0),
        name="weight_grad",
    )(place, a, b, gt)


def inside(first, start, stop, bk):
    key = first + lax.broadcasted_iota(jnp.int32, (bk, start.shape[1]), 0)
    return (key >= start) & (key < stop)


def attend_kernel(
    lo_ref, hi_ref, q_ref, k_ref, vt_ref, span_ref, out_ref, ot_ref, lse_ref, s_ref,
    *, bq, bk, pack
):
    length, hd = q_ref.shape
    factor = LOG2E / math.sqrt(hd)
    half = pack // 2

    def q_step(i, carry):
        qs = pl.ds(pl.multiple_of(i * bq, bq), bq)
        q = q_ref[qs, :]
        start, stop = span_ref[0:1, qs], span_ref[1:2, qs]
        lo, hi = lo_ref[i], hi_ref[i]

        def first(j, top):
            ks = pl.ds(pl.multiple_of(j * bk, bk), bk)
            s = dot(k_ref[ks, :], q, NT) * factor
            s = jnp.where(inside(j * bk, start, stop, bk), s, masked_score)
            s_ref[ks, :] = s
            return jnp.maximum(top, jnp.max(s.reshape(bk // 8, 8, bq), axis=0))

        top = lax.fori_loop(lo, hi, first, jnp.full((8, bq), masked_score, F32))
        peak = jnp.max(top, axis=0, keepdims=True)

        def second(j, state):
            total, acc = state
            ks = pl.ds(pl.multiple_of(j * bk, bk), bk)
            p = jnp.exp2(s_ref[ks, :] - peak)
            total = total + jnp.sum(p.reshape(bk // 8, 8, bq), axis=0)
            return total, acc + dot(vt_ref[:, ks], p.astype(BF), NN)

        total, acc = lax.fori_loop(
            lo, hi, second, (jnp.zeros((8, bq), F32), jnp.zeros((hd, bq), F32))
        )
        total = jnp.sum(total, axis=0, keepdims=True)
        out = acc / total
        ot_ref[:, qs] = out
        lse_ref[:, qs] = peak + jnp.log2(total)
        rows = out.T.astype(BF)
        for c in range(bq // pack):
            piece = rows[c * pack : (c + 1) * pack]
            out_ref[i * (bq // pack) + c] = jnp.concatenate([piece[:half], piece[half:]], axis=1)
        return carry

    lax.fori_loop(0, length // bq, q_step, 0)


def attend(lo, hi, q, k, vt, spans, pack, bq, bk):
    length, hd = q.shape
    return pl.pallas_call(
        functools.partial(attend_kernel, bq=bq, bk=bk, pack=pack),
        out_shape=(
            jax.ShapeDtypeStruct((length // pack, pack // 2, 2 * hd), BF),
            jax.ShapeDtypeStruct((hd, length), F32),
            jax.ShapeDtypeStruct((1, length), F32),
        ),
        in_specs=[SMEM, SMEM] + [VMEM] * 4,
        out_specs=(VMEM,) * 3,
        scratch_shapes=[pltpu.VMEM((length, bq), F32)],
        compiler_params=LARGE,
        cost_estimate=pl.CostEstimate(flops=1000000, bytes_accessed=1 << 10, transcendentals=0),
        name="attend",
    )(lo, hi, q, k, vt, spans)


def attend_back_kernel(
    lo_ref, hi_ref, q_ref, k_ref, v_ref, kt_ref, ot_ref, lse_ref, do_ref, span_ref,
    out_ref, gt_ref, sums_ref, dq_ref, dk_ref, dv_ref, *, bq, bk, pack
):
    length, hd = q_ref.shape
    scale = 1.0 / math.sqrt(hd)
    factor = LOG2E * scale
    half = pack // 2
    dk_ref[...] = jnp.zeros_like(dk_ref)
    dv_ref[...] = jnp.zeros_like(dv_ref)

    def q_step(i, carry):
        qs = pl.ds(pl.multiple_of(i * bq, bq), bq)
        q = q_ref[qs, :]
        start, stop = span_ref[0:1, qs], span_ref[1:2, qs]
        pieces = []
        for c in range(bq // pack):
            piece = do_ref[i * (bq // pack) + c]
            pieces += [piece[:, :hd], piece[:, hd:]]
        do = jnp.concatenate(pieces, axis=0)
        delta = jnp.sum(do.astype(F32).T * ot_ref[:, qs], axis=0, keepdims=True)
        lse = lse_ref[:, qs]

        def step(j, acc):
            ks = pl.ds(pl.multiple_of(j * bk, bk), bk)
            s = dot(k_ref[ks, :], q, NT) * factor - lse
            p = jnp.where(inside(j * bk, start, stop, bk), jnp.exp2(s), 0.0)
            dp = dot(v_ref[ks, :], do, NT)
            ds = (p * (dp - delta)).astype(BF)
            dv_ref[ks, :] += dot(p.astype(BF), do, NN)
            dk_ref[ks, :] += dot(ds, q, NN)
            return acc + dot(kt_ref[:, ks], ds, NN)

        acc = lax.fori_loop(lo_ref[i], hi_ref[i], step, jnp.zeros((hd, bq), F32))
        dq_ref[:, qs] = acc
        return carry

    lax.fori_loop(0, length // bq, q_step, 0)

    def emit(i, sums):
        rows = pl.ds(pl.multiple_of(i * bq, bq), bq)
        dqt = (dq_ref[:, rows] * scale).astype(BF)
        dk = (dk_ref[rows, :] * scale).astype(BF)
        dv = dv_ref[rows, :].astype(BF)
        dq = dqt.astype(F32).T.astype(BF)
        gt_ref[0:hd, rows] = dqt
        gt_ref[hd : 2 * hd, rows] = dk.astype(F32).T.astype(BF)
        gt_ref[2 * hd : 3 * hd, rows] = dv.astype(F32).T.astype(BF)
        for c in range(bq // pack):
            for n, value in enumerate((dq, dk, dv)):
                piece = value[c * pack : (c + 1) * pack]
                out_ref[i * (bq // pack) + c, n * half : (n + 1) * half, :] = jnp.concatenate(
                    [piece[:half], piece[half:]], axis=1
                )
        both = jnp.concatenate([dq.astype(F32), dv.astype(F32)], axis=1)
        return sums + jnp.sum(both, axis=0, keepdims=True)

    sums_ref[...] = lax.fori_loop(0, length // bq, emit, jnp.zeros((1, 2 * hd), F32))


def attend_back(lo, hi, q, k, v, kt, ot, lse, do, spans, pack, bq, bk):
    length, hd = q.shape
    return pl.pallas_call(
        functools.partial(attend_back_kernel, bq=bq, bk=bk, pack=pack),
        out_shape=(
            jax.ShapeDtypeStruct((length // pack, 3 * pack // 2, 2 * hd), BF),
            jax.ShapeDtypeStruct((3 * hd, length), BF),
            jax.ShapeDtypeStruct((1, 2 * hd), F32),
        ),
        in_specs=[SMEM, SMEM] + [VMEM] * 8,
        out_specs=(VMEM,) * 3,
        scratch_shapes=[
            pltpu.VMEM((hd, length), F32),
            pltpu.VMEM((length, hd), F32),
            pltpu.VMEM((length, hd), F32),
        ],
        compiler_params=LARGE,
        cost_estimate=pl.CostEstimate(flops=1000000, bytes_accessed=1 << 10, transcendentals=0),
        name="attend_back",
    )(lo, hi, q, k, v, kt, ot, lse, do, spans)


def call(kernel, outs, ins, name, flops, scratch=(), params=SMALL):
    return pl.pallas_call(
        kernel,
        out_shape=tuple(jax.ShapeDtypeStruct(shape, kind) for shape, kind in outs),
        in_specs=[SMEM if v.dtype == jnp.int32 else VMEM for v in ins],
        out_specs=(VMEM,) * len(outs),
        scratch_shapes=list(scratch),
        compiler_params=params,
        cost_estimate=pl.CostEstimate(
            flops=int(flops), bytes_accessed=1 << 10, transcendentals=0
        ),
        name=name,
    )(*ins)


def column_sums(*values):
    sums = [jnp.sum(v, axis=0, keepdims=True) for v in values]
    return jnp.concatenate(sums + [jnp.zeros_like(sums[0])] * (8 - len(sums)), axis=0)


def unpack_heads(slots_ref, out_ref, layout, piece_rows, which):
    groups, micro, halves, heads_dev = layout
    hd = slots_ref.shape[2] // 2
    part = slice(which * piece_rows, (which + 1) * piece_rows)
    for m in range(micro):
        rows = slice(m * 2 * piece_rows, (m + 1) * 2 * piece_rows)
        pieces = []
        for j in range(groups * heads_dev):
            piece = slots_ref[((j // heads_dev) * micro + m) * halves + j % heads_dev, part, :]
            pieces.append(jnp.concatenate([piece[:, :hd], piece[:, hd:]], axis=0))
        for j in range(0, groups * heads_dev, 2):
            out_ref[rows, j * hd : (j + 2) * hd] = jnp.concatenate(pieces[j : j + 2], axis=1)


def branch_kernel(slots_ref, x_ref, w_ref, vec_ref, attn_ref, low_ref, normed_ref, inv_ref, *, layout):
    unpack_heads(slots_ref, attn_ref, layout, slots_ref.shape[1], 0)
    first_sum = x_ref[...].astype(F32) + dot(attn_ref[...], w_ref[...], NN) + vec_ref[0:1]
    normed, inverse = normalise(first_sum)
    normed_ref[...] = normed
    inv_ref[...] = inverse
    low_ref[...] = (normed * vec_ref[1:2] + vec_ref[2:3]).astype(BF)


def normal_cdf(v):
    bell = jnp.exp(-0.5 * v * v)
    t = 1.0 / (1.0 + (0.3275911 * math.sqrt(0.5)) * jnp.abs(v))
    tail = 0.5 * 1.061405429
    for c in (-1.453152027, 1.421413741, -0.284496736, 0.254829592):
        tail = tail * t + 0.5 * c
    tail = tail * t * bell
    return jnp.where(v < 0.0, tail, 1.0 - tail), bell * (1.0 / math.sqrt(2.0 * math.pi))


def inner_kernel(a_ref, b_ref, c_ref, d_ref, wi_ref, wo_ref, bias_ref, act_ref, slope_ref, low_ref, keep_ref, send_ref):
    count = a_ref.shape[0]
    for n, ref in enumerate((a_ref, b_ref, c_ref, d_ref)):
        rows = slice(n * count, (n + 1) * count)
        x = ref[...]
        low_ref[rows, :] = x
        pre = dot(x, wi_ref[...], NN) + bias_ref[...]
        cdf, bell = normal_cdf(pre)
        slope_ref[rows, :] = cdf + pre * bell
        act = (pre * cdf).astype(BF)
        act_ref[rows, :] = act
        partial = dot(act, wo_ref[...], NN)
        if n < 2:
            keep_ref[rows, :] = partial
        else:
            send_ref[(n - 2) * count : (n - 1) * count, :] = partial.astype(BF)


def inner_back_kernel(a_ref, b_ref, c_ref, d_ref, wi_ref, wo_ref, slope_ref, inner_ref, low_ref, sums_ref, keep_ref, send_ref):
    count = a_ref.shape[0]
    sums = 0.0
    for n, ref in enumerate((a_ref, b_ref, c_ref, d_ref)):
        rows = slice(n * count, (n + 1) * count)
        x = ref[...]
        low_ref[rows, :] = x
        inner = (dot(x, wo_ref[...], NT) * slope_ref[rows, :]).astype(BF)
        inner_ref[rows, :] = inner
        sums = sums + jnp.sum(inner.astype(F32), axis=0, keepdims=True)
        partial = dot(inner, wi_ref[...], NT)
        if n < 2:
            keep_ref[rows, :] = partial
        else:
            send_ref[(n - 2) * count : (n - 1) * count, :] = partial.astype(BF)
    sums_ref[...] = sums


def feed_grad_kernel(low_ref, inner_ref, act_ref, ffn_ref, out_ref, acc_ref):
    cycle, blocks, rows = out_ref.shape[:3]
    half = blocks // 2
    acc_ref[...] = dot(low_ref[...], inner_ref[...], TN)
    for b in range(cycle):
        for h in range(half):
            first = (h * cycle + b) * rows
            out_ref[b, h] = acc_ref[first : first + rows, :].astype(BF)
    acc_ref[...] = dot(act_ref[...], ffn_ref[...], TN)
    for b in range(cycle):
        for h in range(half):
            first = (b * half + h) * rows
            out_ref[b, half + h] = acc_ref[first : first + rows, :].astype(BF)


def collect_kernel(head_ref, slots_ref, qkv_ref, bias_ref, gains_ref, shifts_ref, inner_ref, *, layout):
    groups, micro, halves, heads_dev = layout
    hd = slots_ref.shape[2] // 4
    cycle = micro * halves
    pieces = []
    for j in range(groups * heads_dev):
        first = (j // heads_dev) * cycle + j % heads_dev
        piece = slots_ref[first, :, : 3 * hd].astype(F32)
        for m in range(1, micro):
            piece = piece + slots_ref[first + m * halves, :, : 3 * hd].astype(F32)
        pieces.append(piece)
    for c in range(3):
        for j in range(0, groups * heads_dev, 2):
            pair = [p[:, c * hd : (c + 1) * hd] for p in pieces[j : j + 2]]
            qkv_ref[c, :, j * hd : (j + 2) * hd] = jnp.concatenate(pair, axis=1)
    own = slots_ref[pl.ds(head_ref[0] * cycle, cycle), :, 3 * hd :].astype(F32)
    inner_ref[...] = jnp.sum(own, axis=0)
    sums = jnp.sum(slots_ref[:, :, 3 * hd :].astype(F32), axis=0).T
    bias_ref[...] = sums[0:4]
    gains_ref[...] = sums[4:6]
    shifts_ref[...] = sums[6:8]


def add_kernel(keep_ref, got_ref, own_ref, send_ref):
    count = own_ref.shape[0]
    own_ref[...] = keep_ref[:count] + got_ref[:count].astype(F32)
    send_ref[...] = (keep_ref[count:] + got_ref[count:].astype(F32)).astype(BF)


def output_kernel(own_ref, got_ref, normed_ref, grad_ref, vec_ref, out_ref, second_ref, low_ref, sums_ref):
    first_normed = normed_ref[...] * vec_ref[0:1] + vec_ref[1:2]
    second_sum = first_normed + own_ref[...] + got_ref[...].astype(F32) + vec_ref[2:3]
    normed, inverse = normalise(second_sum)
    out_ref[...] = (normed * vec_ref[3:4] + vec_ref[4:5]).astype(BF)
    grad = grad_ref[...].astype(F32)
    d_second = norm_back(grad, normed, inverse, vec_ref[3:4])
    low = d_second.astype(BF)
    second_ref[...] = d_second
    low_ref[...] = low
    sums_ref[...] = column_sums(grad * normed, grad, low.astype(F32))


def branch_back_kernel(own_ref, got_ref, second_ref, normed_ref, inv_ref, w_ref, vec_ref, first_ref, low_ref, sums_ref, slots_ref, *, layout):
    groups, micro, halves, heads_dev = layout
    grad = own_ref[...] + got_ref[...].astype(F32) + second_ref[...]
    normed = normed_ref[...]
    d_first = norm_back(grad, normed, inv_ref[...], vec_ref[0:1])
    low = d_first.astype(BF)
    first_ref[...] = d_first
    low_ref[...] = low
    sums_ref[...] = column_sums(grad * normed, grad, low.astype(F32))
    d_attn = dot(low, w_ref[...], NT).astype(BF)
    half = slots_ref.shape[1]
    hd = slots_ref.shape[2] // 2
    for m in range(micro):
        for j in range(groups * heads_dev):
            piece = d_attn[m * 2 * half : (m + 1) * 2 * half, j * hd : (j + 1) * hd]
            piece = jnp.concatenate([piece[:half], piece[half:]], axis=1)
            first = ((j // heads_dev) * micro + m) * halves
            slots_ref[first + j % heads_dev] = piece
            if j % heads_dev == heads_dev - 1:
                for b in range(heads_dev, halves):
                    slots_ref[first + b] = piece


def tokens_kernel(slots_ref, w_ref, first_ref, out_ref, d_ref, *, layout):
    piece_rows = slots_ref.shape[1] // 3
    total = first_ref[...]
    for c in range(3):
        unpack_heads(slots_ref, d_ref.at[c], layout, piece_rows, c)
        total = total + dot(d_ref[c], w_ref[c], NT)
    out_ref[...] = total.astype(BF)


def normalise(hidden):
    center = hidden - jnp.mean(hidden, axis=-1, keepdims=True)
    spread = jnp.mean(center * center, axis=-1, keepdims=True)
    inverse = lax.rsqrt(spread + norm_eps)
    return center * inverse, inverse


def norm_back(grad, normed, inverse, gain):
    e = grad * gain
    return inverse * (
        e
        - jnp.mean(e, axis=-1, keepdims=True)
        - normed * jnp.mean(e * normed, axis=-1, keepdims=True)
    )


def after(value, *others):
    return lax.optimization_barrier((value, *others))[0]


def by_core(value):
    return lax.ppermute(value, "head", [(0, 1), (1, 0), (2, 3), (3, 2)])


def by_x(value):
    return lax.ppermute(value, "head", [(0, 2), (2, 0), (1, 3), (3, 1)])


def swap(value, axes, groups=None):
    return lax.all_to_all(
        value, axes, split_axis=0, concat_axis=0, tiled=True, axis_index_groups=groups
    )


def spread_over(value, axes, count, groups=None):
    return swap(jnp.broadcast_to(value[None], (count, *value.shape)), axes, groups)


def gather_group(rows):
    across_x = by_x(rows)
    return rows, across_x, by_core(rows), by_core(across_x)


def reduce_group(keep, send):
    count, depth = keep.shape[0] // 2, keep.shape[1]
    shape = (count, depth)
    own, send = call(add_kernel, ((shape, F32), (shape, BF)), (keep, by_core(send)), "add", 1e6)
    return own, by_x(send)


def stack_rows(*values):
    blank = jnp.zeros_like(values[0])
    return jnp.stack([*values, *[blank] * (8 - len(values))])


def in_order(blocks):
    index = lax.axis_index("head")
    own, across_x, across_core, across = blocks
    odd, far = index % 2 == 1, index // 2 == 1
    near = [jnp.where(odd, q, p) for p, q in ((own, across_core), (across_core, own))]
    wide = [jnp.where(odd, q, p) for p, q in ((across_x, across), (across, across_x))]
    return jnp.stack(
        [jnp.where(far, q, p) for p, q in zip(near + wide, wide + near)]
    )


def to_group(blocks):
    index = lax.axis_index("head")

    def block(offset):
        return lax.dynamic_index_in_dim(blocks, index ^ offset, 0, keepdims=False)

    across = lax.ppermute(block(3), "head", [(i, i ^ 3) for i in range(4)])
    return in_order((block(0), by_x(block(2)), by_core(block(1)), across))


def key_ranges(spans, bq, bk):
    return spans[0, ::bq] // bk, cdiv(spans[1, bq - 1 :: bq], bk)


def local(
    inputs,
    doc_lengths,
    grad_out,
    qkv_weight,
    out_weight,
    inner_weight,
    outer_weight,
    bias_rows,
    inner_bias,
    norm_gains,
    norm_shifts,
):
    micro, tokens, depth = inputs.shape
    groups, cycle = lax.axis_size("head"), lax.axis_size("blk")
    halves = cycle // 2
    devices = groups * cycle
    length = devices * tokens
    hd = depth // HEADS
    heads_dev = HEADS // groups
    rows_dev = qkv_weight.shape[1]
    ff_dev = outer_weight.shape[0]
    ff_part = cycle * ff_dev
    half_tokens = tokens // 2
    head_index = lax.axis_index("head")
    blk_index = lax.axis_index("blk")
    half = blk_index // halves
    unit_head = head_index * heads_dev + jnp.minimum(blk_index % halves, heads_dev - 1)
    unit_of = [min(i, heads_dev - 1) for i in range(halves)]

    own_x = lax.dynamic_index_in_dim(inputs, half, 0, keepdims=False)
    other_x = lax.dynamic_index_in_dim(inputs, 1 - half, 0, keepdims=False)
    got_x = lax.ppermute(other_x, "blk", [(i, (i + halves) % cycle) for i in range(cycle)])
    pair_x = jnp.concatenate([own_x, got_x], axis=0)
    cube = [
        [h * cycle + b for h in (c, c + 2) for b in range(s * halves, (s + 1) * halves)]
        for c in range(2)
        for s in range(2)
    ]
    inner_own = inner_weight.reshape(rows_dev, groups, ff_part)
    inner_own = to_group(inner_own.transpose(1, 0, 2)).reshape(groups * rows_dev, ff_part)
    ffn = jnp.concatenate([inner_own, outer_weight, out_weight])

    units = tuple(h * heads_dev + u for h in range(groups) for u in unit_of)
    (slots,) = call(
        functools.partial(head_slots_kernel, units=units),
        (((groups * halves, 2, rows_dev, 2 * hd), BF),),
        (qkv_weight, bias_rows, norm_gains, norm_shifts, inner_bias.reshape(rows_dev, -1)),
        "head_slots",
        1e6,
        params=LARGE,
    )
    half_groups = [
        [h * cycle + b for h in range(groups) for b in range(n * halves, (n + 1) * halves)]
        for n in range(2)
    ]
    slots, pair_x = lax.optimization_barrier((swap(slots, BOTH, half_groups), pair_x))
    far_slots = lax.ppermute(slots, "blk", [(i, (i + halves) % cycle) for i in range(cycle)])
    near, far = [v.reshape(groups, halves, 2, rows_dev, 2 * hd) for v in (slots, far_slots)]
    both = jnp.stack([jnp.where(half == 0, near, far), jnp.where(half == 0, far, near)], axis=1)
    qk_weight = both[:, :, :, 0].reshape(depth, 2 * hd)
    v_weight = both[:, :, :, 1].reshape(depth, 2 * hd)
    small = both[:, :, :, 1, :, hd : hd + 12].astype(F32).reshape(depth, 12).T

    bias, gains, shifts = small[0:4], small[4:6], small[6:8]
    inner_bias_all = small[8:12].T.reshape(groups, ff_part)
    inner_bias_part = lax.dynamic_index_in_dim(inner_bias_all, head_index, 0, keepdims=False)
    unit_bias = lax.dynamic_slice(bias[0:2], (0, unit_head * hd), (2, hd))
    unit_bias = jnp.pad(unit_bias, ((0, 0), (0, hd)))

    qkv_all = lax.all_gather(after(qkv_weight, ffn), BOTH, axis=0, tiled=False)
    ffn_all = lax.all_gather(after(ffn, slots), "blk", axis=0, tiled=False)
    lengths = lax.dynamic_index_in_dim(doc_lengths, half, 0, keepdims=False)
    order = jnp.arange(lengths.shape[0], dtype=jnp.int32)
    bounds = jnp.sum(jnp.where(order[None, :] <= order[:, None], lengths[None, :], 0), axis=1)
    positions = jnp.arange(length, dtype=jnp.int32)[None, :]
    starts = (bounds - lengths)[:, None]
    own = (positions >= starts) & (positions < bounds[:, None])
    spans = jnp.stack(
        [
            jnp.sum(jnp.where(own, starts, 0), axis=0),
            jnp.sum(jnp.where(own, bounds[:, None], 0), axis=0),
        ]
    )

    place = jnp.stack([head_index % 2, half]).astype(jnp.int32)
    block = 512 if length <= 4096 else 256
    ranges = key_ranges(spans, block, 512), key_ranges(spans, 512, 256)
    small_rows = (
        stack_rows(bias[2], gains[0], shifts[0]),
        stack_rows(gains[0], shifts[0], bias[3], gains[1], shifts[1]),
        stack_rows(gains[0]),
        inner_bias_part[None],
    )
    tokens_a = spread_over(pair_x, BOTH, cycle, cube)
    prepared = (qk_weight, v_weight, unit_bias, small_rows, spans, place, ranges)
    tokens_a, prepared = lax.optimization_barrier((tokens_a, prepared))
    qk_weight, v_weight, unit_bias, small_rows, spans, place, ranges = prepared
    tokens_b = by_core(tokens_a)

    per = max(1, 256 // tokens)
    q, k, v, kt, vt = project(
        place, tokens_a, tokens_b, qk_weight, v_weight, unit_bias, halves, per
    )
    lo, hi = ranges[0]
    attn_out, attn_t, lse = attend(lo, hi, q, k, vt, spans, tokens, block, 512)

    ffn = after(ffn_all, attn_out)
    inner_part = (
        ffn[:, : groups * rows_dev]
        .reshape(cycle, groups, rows_dev, ff_part)
        .transpose(1, 0, 2, 3)
        .reshape(depth, ff_part)
    )
    last = groups * rows_dev + ff_dev
    outer_part = ffn[:, groups * rows_dev : last].reshape(ff_part, depth)
    out_part = ffn[:, last:].reshape(depth // groups, depth)
    attn_slots = swap(attn_out, BOTH)
    out_x, attn_slots, inner_part, outer_part = lax.optimization_barrier(
        (by_x(out_part), attn_slots, inner_part, outer_part)
    )
    out_all = in_order((out_part, out_x, by_core(out_part), by_core(out_x))).reshape(depth, depth)

    rows = micro * tokens
    layout = (groups, micro, halves, heads_dev)
    flat, group = (rows, depth), (groups * rows, ff_part)
    attn, normed_low, normed_one, inverse_one = call(
        functools.partial(branch_kernel, layout=layout),
        ((flat, BF), (flat, BF), (flat, F32), ((rows, 1), F32)),
        (attn_slots, inputs.reshape(flat), out_all, small_rows[0]),
        "branch",
        1e6,
    )
    act_low, slope, normed_group, keep, send = call(
        inner_kernel,
        ((group, BF), (group, F32), ((groups * rows, depth), BF), ((2 * rows, depth), F32), ((2 * rows, depth), BF)),
        (*gather_group(normed_low), inner_part, outer_part, small_rows[3]),
        "inner",
        1e6,
    )
    output, d_second, d_ffn, sums_two = call(
        output_kernel,
        ((flat, BF), (flat, F32), (flat, BF), ((8, depth), F32)),
        (
            *reduce_group(keep, send),
            normed_one,
            grad_out.reshape(flat),
            small_rows[1],
        ),
        "output",
        1e6,
    )
    output = output.reshape(inputs.shape)
    d_inner, d_ffn_group, inner_sums, keep, send = call(
        inner_back_kernel,
        ((group, BF), ((groups * rows, depth), BF), ((1, ff_part), F32), ((2 * rows, depth), F32), ((2 * rows, depth), BF)),
        (*gather_group(d_ffn), inner_part, outer_part, slope),
        "inner_back",
        1e6,
    )
    own, got = reduce_group(keep, send)
    (ffn_grad,) = call(
        feed_grad_kernel,
        (((cycle, 2 * groups, rows_dev, depth), BF),),
        (normed_group, d_inner, act_low, d_ffn_group),
        "feed_grad",
        1e6,
        [pltpu.VMEM((depth, depth), F32)],
    )
    got, ffn_grad = lax.optimization_barrier((got, ffn_grad))
    d_first, d_branch, sums_one, d_heads = call(
        functools.partial(branch_back_kernel, layout=layout),
        ((flat, F32), (flat, BF), ((8, depth), F32), ((devices, half_tokens, 2 * hd), BF)),
        (
            own,
            got,
            d_second,
            normed_one,
            inverse_one,
            out_all,
            small_rows[2],
        ),
        "branch_back",
        1e6,
    )
    d_heads = swap(d_heads, BOTH)

    ffn_grad = lax.psum_scatter(ffn_grad, "blk", scatter_dimension=0, tiled=False)
    outer_grad = ffn_grad[groups:].reshape(ff_dev, depth).astype(F32)
    inner_grad = to_group(ffn_grad[:groups])
    inner_grad = inner_grad.transpose(1, 0, 2).reshape(rows_dev, groups * ff_part).astype(F32)
    out_grad = dot(attn, d_branch, TN).reshape(groups, depth // groups, depth)

    def out_block(offset):
        return lax.dynamic_index_in_dim(out_grad, head_index ^ offset, 0, keepdims=False)

    from_core = by_core(jnp.stack([out_block(1), out_block(3)]).astype(BF)).astype(F32)
    from_x = by_x((out_block(2) + from_core[1]).astype(BF)).astype(F32)
    out_grad = (out_block(0) + from_core[0] + from_x).astype(BF)
    out_terms = swap(out_grad.reshape(cycle, rows_dev, depth), "blk")
    out_grad = jnp.sum(
        out_terms.astype(F32), axis=0
    )

    lo, hi = ranges[1]
    qkv_out, qkv_t, qv_sums = attend_back(
        lo, hi, q, k, v, kt, attn_t, lse, d_heads, spans, tokens, 512, 256
    )
    qkv_home = swap(after(qkv_out, out_terms), BOTH)
    qkv_all = qkv_all.transpose(1, 0, 2, 3).reshape(3, depth, depth)
    (grad_inputs,) = call(
        functools.partial(tokens_kernel, layout=layout),
        ((flat, BF),),
        (qkv_home, qkv_all, d_first),
        "tokens",
        1e6,
        [pltpu.VMEM((3, rows, depth), BF)],
    )
    grad_inputs = grad_inputs.reshape(inputs.shape)

    unit_grad = weight_grad(place, tokens_a, tokens_b, qkv_t, halves, per)
    wide = jnp.zeros((2, HEADS, hd), F32)
    wide = lax.dynamic_update_slice(wide, qv_sums.reshape(2, 1, hd), (0, unit_head, 0))
    wide = jnp.where((blk_index % halves < heads_dev), wide, 0.0)
    sums = jnp.stack(
        [wide[0].reshape(depth), wide[1].reshape(depth), sums_one[2], sums_two[2]]
        + [sums_one[0], sums_two[0], sums_one[1], sums_two[1]]
    ).T
    inner_sums = inner_sums.reshape(1, cycle, rows_dev, ff_dev // rows_dev)
    inner_sums = jnp.broadcast_to(inner_sums, (groups, *inner_sums.shape[1:]))
    extra = jnp.concatenate(
        [
            sums.reshape(devices, rows_dev, 8),
            inner_sums.reshape(devices, rows_dev, -1),
        ],
        axis=2,
    ).astype(BF)
    extra = jnp.pad(extra, ((0, 0), (0, 0), (0, hd - extra.shape[2])))
    final = jnp.concatenate([unit_grad.reshape(devices, rows_dev, 3 * hd), extra], axis=2)
    final = after(swap(after(final, qkv_home), BOTH), grad_inputs)
    qkv_grad, bias_grad, gains_grad, shifts_grad, inner_bias_grad = call(
        functools.partial(collect_kernel, layout=layout),
        (
            ((3, rows_dev, depth), F32),
            ((4, rows_dev), F32),
            ((2, rows_dev), F32),
            ((2, rows_dev), F32),
            ((rows_dev, hd), F32),
        ),
        (head_index[None], final),
        "collect",
        1e6,
    )
    return (
        output,
        grad_inputs,
        qkv_grad,
        out_grad,
        inner_grad,
        outer_grad,
        bias_grad,
        inner_bias_grad[:, 8 : 8 + ff_dev // rows_dev].reshape(ff_dev),
        gains_grad,
        shifts_grad,
    )


def solution(mesh):
    tokens = P(None, BOTH, None)
    rows = P(BOTH, None)
    columns = P(None, BOTH)
    return jax.shard_map(
        local,
        mesh=mesh,
        in_specs=(tokens, P(), tokens, tokens, rows, rows, rows, columns, P(BOTH), columns, columns),
        out_specs=(tokens, tokens, tokens, rows, rows, rows, columns, P(BOTH), columns, columns),
        check_vma=False,
    )
```

```python
import functools
import math

import jax
import jax.numpy as jnp
from jax import lax
from jax.experimental import pallas as pl
from jax.experimental.pallas import tpu as pltpu
from jax.sharding import PartitionSpec as P

HEADS = 12
F32 = jnp.float32
BF = jnp.bfloat16
NT = (((1,), (1,)), ((), ()))
NN = (((1,), (0,)), ((), ()))
TN = (((0,), (0,)), ((), ()))
LOG2E = math.log2(math.e)
BOTH = ("head", "blk")
norm_eps = 1e-12
masked_score = -1e30
VMEM = pl.BlockSpec(memory_space=pltpu.VMEM)
SMEM = pl.BlockSpec(memory_space=pltpu.SMEM)
SMALL = pltpu.CompilerParams(vmem_limit_bytes=20 << 20)
LARGE = pltpu.CompilerParams(vmem_limit_bytes=56 << 20)


def dot(a, b, dims):
    return lax.dot_general(a, b, dims, preferred_element_type=F32)


def cdiv(a, b):
    return -(-a // b)


def chunk_walk(place_ref, blocks, halves, per, tokens, visit):
    core, half = place_ref[0], place_ref[1]
    runs = halves // per
    for source in range(2):

        def one(n, carry, source=source):
            xh = n // (2 * runs)
            rel = n // runs % 2
            run = n % runs
            head = xh * 2 + (core if source == 0 else 1 - core)
            position = ((head * 2 + (rel ^ half)) * halves + run * per) * tokens
            rows = pl.ds(pl.multiple_of(rel * tokens, tokens), tokens)

            def load(ref):
                return jnp.concatenate(
                    [ref[xh * halves + run * per + k, rows, :] for k in range(per)], axis=0
                )

            visit(source, load, pl.multiple_of(position, per * tokens))
            return carry

        lax.fori_loop(0, 4 * runs, one, 0, unroll=4 * runs <= 4)


def project_kernel(
    place_ref, a_ref, b_ref, qk_ref, v_w_ref, bias_ref, q_ref, k_ref, v_ref, kt_ref, vt_ref, *, halves, per
):
    tokens = a_ref.shape[1] // 2
    hd = q_ref.shape[1]

    def visit(source, load, position):
        x = load((a_ref, b_ref)[source])
        rows = pl.ds(position, per * tokens)
        qk = dot(x, qk_ref[...], NN) + bias_ref[0:1]
        v = (dot(x, v_w_ref[...], NN) + bias_ref[1:2])[:, :hd]
        k = qk[:, hd:]
        q_ref[rows, :] = qk[:, :hd].astype(BF)
        k_ref[rows, :] = k.astype(BF)
        v_ref[rows, :] = v.astype(BF)
        kt_ref[:, rows] = k.T.astype(BF)
        vt_ref[:, rows] = v.T.astype(BF)

    chunk_walk(place_ref, a_ref.shape[0], halves, per, tokens, visit)


def project(place, a, b, qk, v, bias, halves, per):
    length = 2 * a.shape[0] * a.shape[1]
    hd = qk.shape[1] // 2
    rows = jax.ShapeDtypeStruct((length, hd), BF)
    columns = jax.ShapeDtypeStruct((hd, length), BF)
    return pl.pallas_call(
        functools.partial(project_kernel, halves=halves, per=per),
        out_shape=(rows, rows, rows, columns, columns),
        in_specs=[SMEM] + [VMEM] * 5,
        out_specs=(VMEM,) * 5,
        compiler_params=LARGE,
        cost_estimate=pl.CostEstimate(flops=1000000, bytes_accessed=1 << 10, transcendentals=0),
        name="project",
    )(place, a, b, qk, v, bias)


def head_slots_kernel(w_ref, bias_ref, gains_ref, shifts_ref, inner_ref, out_ref, *, units):
    hd = w_ref.shape[2] // HEADS
    rows = [ref[...].astype(F32) for ref in (bias_ref, gains_ref, shifts_ref)]
    inner = inner_ref[...].astype(F32)
    blank = jnp.zeros((inner.shape[0], hd - 8 - inner.shape[1]), F32)
    small = jnp.concatenate([jnp.concatenate(rows, axis=0).T, inner, blank], axis=1).astype(BF)
    done = {}
    for d, j in enumerate(units):
        if j not in done:
            part = [w_ref[c][:, j * hd : (j + 1) * hd] for c in range(3)]
            done[j] = [
                jnp.concatenate(part[:2], axis=1),
                jnp.concatenate([part[2], small], axis=1),
            ]
        out_ref[d, 0] = done[j][0]
        out_ref[d, 1] = done[j][1]


def weight_grad_kernel(place_ref, a_ref, b_ref, gt_ref, out_ref, acc_ref, *, halves, per):
    tokens = a_ref.shape[1] // 2
    acc_ref[...] = jnp.zeros_like(acc_ref)

    def visit(source, load, position):
        x = load((a_ref, b_ref)[source])
        acc_ref[...] += dot(gt_ref[:, pl.ds(position, per * tokens)], x, NN)

    chunk_walk(place_ref, a_ref.shape[0], halves, per, tokens, visit)
    out_ref[...] = acc_ref[...].T.astype(BF)


def weight_grad(place, a, b, gt, halves, per):
    depth = a.shape[2]
    length = gt.shape[1]
    return pl.pallas_call(
        functools.partial(weight_grad_kernel, halves=halves, per=per),
        out_shape=jax.ShapeDtypeStruct((depth, gt.shape[0]), BF),
        in_specs=[SMEM] + [VMEM] * 3,
        out_specs=VMEM,
        scratch_shapes=[pltpu.VMEM((gt.shape[0], depth), F32)],
        compiler_params=SMALL if length <= 4096 else LARGE,
        cost_estimate=pl.CostEstimate(flops=1000000, bytes_accessed=1 << 10, transcendentals=0),
        name="weight_grad",
    )(place, a, b, gt)


def inside(first, start, stop, bk):
    key = first + lax.broadcasted_iota(jnp.int32, (bk, start.shape[1]), 0)
    return (key >= start) & (key < stop)


def attend_kernel(
    lo_ref, hi_ref, q_ref, k_ref, vt_ref, span_ref, out_ref, ot_ref, lse_ref, s_ref,
    *, bq, bk, pack
):
    length, hd = q_ref.shape
    factor = LOG2E / math.sqrt(hd)
    half = pack // 2

    def q_step(i, carry):
        qs = pl.ds(pl.multiple_of(i * bq, bq), bq)
        q = q_ref[qs, :]
        start, stop = span_ref[0:1, qs], span_ref[1:2, qs]
        lo, hi = lo_ref[i], hi_ref[i]

        def first(j, top):
            ks = pl.ds(pl.multiple_of(j * bk, bk), bk)
            s = dot(k_ref[ks, :], q, NT) * factor
            s = jnp.where(inside(j * bk, start, stop, bk), s, masked_score)
            s_ref[ks, :] = s
            return jnp.maximum(top, jnp.max(s.reshape(bk // 8, 8, bq), axis=0))

        top = lax.fori_loop(lo, hi, first, jnp.full((8, bq), masked_score, F32))
        peak = jnp.max(top, axis=0, keepdims=True)

        def second(j, state):
            total, acc = state
            ks = pl.ds(pl.multiple_of(j * bk, bk), bk)
            p = jnp.exp2(s_ref[ks, :] - peak)
            total = total + jnp.sum(p.reshape(bk // 8, 8, bq), axis=0)
            return total, acc + dot(vt_ref[:, ks], p.astype(BF), NN)

        total, acc = lax.fori_loop(
            lo, hi, second, (jnp.zeros((8, bq), F32), jnp.zeros((hd, bq), F32))
        )
        total = jnp.sum(total, axis=0, keepdims=True)
        out = acc / total
        ot_ref[:, qs] = out
        lse_ref[:, qs] = peak + jnp.log2(total)
        rows = out.T.astype(BF)
        for c in range(bq // pack):
            piece = rows[c * pack : (c + 1) * pack]
            out_ref[i * (bq // pack) + c] = jnp.concatenate([piece[:half], piece[half:]], axis=1)
        return carry

    lax.fori_loop(0, length // bq, q_step, 0)


def attend(lo, hi, q, k, vt, spans, pack, bq, bk):
    length, hd = q.shape
    return pl.pallas_call(
        functools.partial(attend_kernel, bq=bq, bk=bk, pack=pack),
        out_shape=(
            jax.ShapeDtypeStruct((length // pack, pack // 2, 2 * hd), BF),
            jax.ShapeDtypeStruct((hd, length), F32),
            jax.ShapeDtypeStruct((1, length), F32),
        ),
        in_specs=[SMEM, SMEM] + [VMEM] * 4,
        out_specs=(VMEM,) * 3,
        scratch_shapes=[pltpu.VMEM((length, bq), F32)],
        compiler_params=LARGE,
        cost_estimate=pl.CostEstimate(flops=1000000, bytes_accessed=1 << 10, transcendentals=0),
        name="attend",
    )(lo, hi, q, k, vt, spans)


def attend_back_kernel(
    lo_ref, hi_ref, q_ref, k_ref, v_ref, kt_ref, ot_ref, lse_ref, do_ref, span_ref,
    out_ref, gt_ref, sums_ref, dq_ref, dk_ref, dv_ref, *, bq, bk, pack
):
    length, hd = q_ref.shape
    scale = 1.0 / math.sqrt(hd)
    factor = LOG2E * scale
    half = pack // 2
    dk_ref[...] = jnp.zeros_like(dk_ref)
    dv_ref[...] = jnp.zeros_like(dv_ref)

    def q_step(i, carry):
        qs = pl.ds(pl.multiple_of(i * bq, bq), bq)
        q = q_ref[qs, :]
        start, stop = span_ref[0:1, qs], span_ref[1:2, qs]
        pieces = []
        for c in range(bq // pack):
            piece = do_ref[i * (bq // pack) + c]
            pieces += [piece[:, :hd], piece[:, hd:]]
        do = jnp.concatenate(pieces, axis=0)
        delta = jnp.sum(do.astype(F32).T * ot_ref[:, qs], axis=0, keepdims=True)
        lse = lse_ref[:, qs]

        def step(j, acc):
            ks = pl.ds(pl.multiple_of(j * bk, bk), bk)
            s = dot(k_ref[ks, :], q, NT) * factor - lse
            p = jnp.where(inside(j * bk, start, stop, bk), jnp.exp2(s), 0.0)
            dp = dot(v_ref[ks, :], do, NT)
            ds = (p * (dp - delta)).astype(BF)
            dv_ref[ks, :] += dot(p.astype(BF), do, NN)
            dk_ref[ks, :] += dot(ds, q, NN)
            return acc + dot(kt_ref[:, ks], ds, NN)

        acc = lax.fori_loop(lo_ref[i], hi_ref[i], step, jnp.zeros((hd, bq), F32))
        dq_ref[:, qs] = acc
        return carry

    lax.fori_loop(0, length // bq, q_step, 0)

    def emit(i, sums):
        rows = pl.ds(pl.multiple_of(i * bq, bq), bq)
        dqt = (dq_ref[:, rows] * scale).astype(BF)
        dk = (dk_ref[rows, :] * scale).astype(BF)
        dv = dv_ref[rows, :].astype(BF)
        dq = dqt.astype(F32).T.astype(BF)
        gt_ref[0:hd, rows] = dqt
        gt_ref[hd : 2 * hd, rows] = dk.astype(F32).T.astype(BF)
        gt_ref[2 * hd : 3 * hd, rows] = dv.astype(F32).T.astype(BF)
        for c in range(bq // pack):
            for n, value in enumerate((dq, dk, dv)):
                piece = value[c * pack : (c + 1) * pack]
                out_ref[i * (bq // pack) + c, n * half : (n + 1) * half, :] = jnp.concatenate(
                    [piece[:half], piece[half:]], axis=1
                )
        both = jnp.concatenate([dq.astype(F32), dv.astype(F32)], axis=1)
        return sums + jnp.sum(both, axis=0, keepdims=True)

    sums_ref[...] = lax.fori_loop(0, length // bq, emit, jnp.zeros((1, 2 * hd), F32))


def attend_back(lo, hi, q, k, v, kt, ot, lse, do, spans, pack, bq, bk):
    length, hd = q.shape
    return pl.pallas_call(
        functools.partial(attend_back_kernel, bq=bq, bk=bk, pack=pack),
        out_shape=(
            jax.ShapeDtypeStruct((length // pack, 3 * pack // 2, 2 * hd), BF),
            jax.ShapeDtypeStruct((3 * hd, length), BF),
            jax.ShapeDtypeStruct((1, 2 * hd), F32),
        ),
        in_specs=[SMEM, SMEM] + [VMEM] * 8,
        out_specs=(VMEM,) * 3,
        scratch_shapes=[
            pltpu.VMEM((hd, length), F32),
            pltpu.VMEM((length, hd), F32),
            pltpu.VMEM((length, hd), F32),
        ],
        compiler_params=LARGE,
        cost_estimate=pl.CostEstimate(flops=1000000, bytes_accessed=1 << 10, transcendentals=0),
        name="attend_back",
    )(lo, hi, q, k, v, kt, ot, lse, do, spans)


def call(kernel, outs, ins, name, flops, scratch=(), params=SMALL):
    return pl.pallas_call(
        kernel,
        out_shape=tuple(jax.ShapeDtypeStruct(shape, kind) for shape, kind in outs),
        in_specs=[SMEM if v.dtype == jnp.int32 else VMEM for v in ins],
        out_specs=(VMEM,) * len(outs),
        scratch_shapes=list(scratch),
        compiler_params=params,
        cost_estimate=pl.CostEstimate(
            flops=int(flops), bytes_accessed=1 << 10, transcendentals=0
        ),
        name=name,
    )(*ins)


def column_sums(*values):
    sums = [jnp.sum(v, axis=0, keepdims=True) for v in values]
    return jnp.concatenate(sums + [jnp.zeros_like(sums[0])] * (8 - len(sums)), axis=0)


def unpack_heads(slots_ref, out_ref, layout, piece_rows, which):
    groups, micro, halves, heads_dev = layout
    hd = slots_ref.shape[2] // 2
    part = slice(which * piece_rows, (which + 1) * piece_rows)
    for m in range(micro):
        rows = slice(m * 2 * piece_rows, (m + 1) * 2 * piece_rows)
        pieces = []
        for j in range(groups * heads_dev):
            piece = slots_ref[((j // heads_dev) * micro + m) * halves + j % heads_dev, part, :]
            pieces.append(jnp.concatenate([piece[:, :hd], piece[:, hd:]], axis=0))
        for j in range(0, groups * heads_dev, 2):
            out_ref[rows, j * hd : (j + 2) * hd] = jnp.concatenate(pieces[j : j + 2], axis=1)


def branch_kernel(slots_ref, x_ref, w_ref, vec_ref, attn_ref, low_ref, normed_ref, inv_ref, *, layout):
    unpack_heads(slots_ref, attn_ref, layout, slots_ref.shape[1], 0)
    first_sum = x_ref[...].astype(F32) + dot(attn_ref[...], w_ref[...], NN) + vec_ref[0:1]
    normed, inverse = normalise(first_sum)
    normed_ref[...] = normed
    inv_ref[...] = inverse
    low_ref[...] = (normed * vec_ref[1:2] + vec_ref[2:3]).astype(BF)


def normal_cdf(v):
    bell = jnp.exp(-0.5 * v * v) * (1.0 / math.sqrt(2.0 * math.pi))
    return 0.5 * (1.0 + lax.erf(v * (1.0 / math.sqrt(2.0)))), bell


def inner_kernel(a_ref, b_ref, c_ref, d_ref, wi_ref, wo_ref, bias_ref, act_ref, slope_ref, low_ref, keep_ref, send_ref):
    count = a_ref.shape[0]
    for n, ref in enumerate((a_ref, b_ref, c_ref, d_ref)):
        rows = slice(n * count, (n + 1) * count)
        x = ref[...]
        low_ref[rows, :] = x
        pre = dot(x, wi_ref[...], NN) + bias_ref[...]
        cdf, bell = normal_cdf(pre)
        slope_ref[rows, :] = cdf + pre * bell
        act = (pre * cdf).astype(BF)
        act_ref[rows, :] = act
        partial = dot(act, wo_ref[...], NN)
        if n < 2:
            keep_ref[rows, :] = partial
        else:
            send_ref[(n - 2) * count : (n - 1) * count, :] = partial.astype(BF)


def inner_back_kernel(a_ref, b_ref, c_ref, d_ref, wi_ref, wo_ref, slope_ref, inner_ref, low_ref, sums_ref, keep_ref, send_ref):
    count = a_ref.shape[0]
    sums = 0.0
    for n, ref in enumerate((a_ref, b_ref, c_ref, d_ref)):
        rows = slice(n * count, (n + 1) * count)
        x = ref[...]
        low_ref[rows, :] = x
        inner = (dot(x, wo_ref[...], NT) * slope_ref[rows, :]).astype(BF)
        inner_ref[rows, :] = inner
        sums = sums + jnp.sum(inner.astype(F32), axis=0, keepdims=True)
        partial = dot(inner, wi_ref[...], NT)
        if n < 2:
            keep_ref[rows, :] = partial
        else:
            send_ref[(n - 2) * count : (n - 1) * count, :] = partial.astype(BF)
    sums_ref[...] = sums


def feed_grad_kernel(low_ref, inner_ref, act_ref, ffn_ref, out_ref, acc_ref):
    cycle, blocks, rows = out_ref.shape[:3]
    half = blocks // 2
    acc_ref[...] = dot(low_ref[...], inner_ref[...], TN)
    for b in range(cycle):
        for h in range(half):
            first = (h * cycle + b) * rows
            out_ref[b, h] = acc_ref[first : first + rows, :].astype(BF)
    acc_ref[...] = dot(act_ref[...], ffn_ref[...], TN)
    for b in range(cycle):
        for h in range(half):
            first = (b * half + h) * rows
            out_ref[b, half + h] = acc_ref[first : first + rows, :].astype(BF)


def collect_kernel(head_ref, slots_ref, qkv_ref, bias_ref, gains_ref, shifts_ref, inner_ref, *, layout):
    groups, micro, halves, heads_dev = layout
    hd = slots_ref.shape[2] // 4
    cycle = micro * halves
    pieces = []
    for j in range(groups * heads_dev):
        first = (j // heads_dev) * cycle + j % heads_dev
        piece = slots_ref[first, :, : 3 * hd].astype(F32)
        for m in range(1, micro):
            piece = piece + slots_ref[first + m * halves, :, : 3 * hd].astype(F32)
        pieces.append(piece)
    for c in range(3):
        for j in range(0, groups * heads_dev, 2):
            pair = [p[:, c * hd : (c + 1) * hd] for p in pieces[j : j + 2]]
            qkv_ref[c, :, j * hd : (j + 2) * hd] = jnp.concatenate(pair, axis=1)
    own = slots_ref[pl.ds(head_ref[0] * cycle, cycle), :, 3 * hd :].astype(F32)
    inner_ref[...] = jnp.sum(own, axis=0)
    sums = jnp.sum(slots_ref[:, :, 3 * hd :].astype(F32), axis=0).T
    bias_ref[...] = sums[0:4]
    gains_ref[...] = sums[4:6]
    shifts_ref[...] = sums[6:8]


def add_kernel(keep_ref, got_ref, own_ref, send_ref):
    count = own_ref.shape[0]
    own_ref[...] = keep_ref[:count] + got_ref[:count].astype(F32)
    send_ref[...] = (keep_ref[count:] + got_ref[count:].astype(F32)).astype(BF)


def output_kernel(own_ref, got_ref, normed_ref, grad_ref, vec_ref, out_ref, second_ref, low_ref, sums_ref):
    first_normed = normed_ref[...] * vec_ref[0:1] + vec_ref[1:2]
    second_sum = first_normed + own_ref[...] + got_ref[...].astype(F32) + vec_ref[2:3]
    normed, inverse = normalise(second_sum)
    out_ref[...] = (normed * vec_ref[3:4] + vec_ref[4:5]).astype(BF)
    grad = grad_ref[...].astype(F32)
    d_second = norm_back(grad, normed, inverse, vec_ref[3:4])
    low = d_second.astype(BF)
    second_ref[...] = d_second
    low_ref[...] = low
    sums_ref[...] = column_sums(grad * normed, grad, low.astype(F32))


def branch_back_kernel(own_ref, got_ref, second_ref, normed_ref, inv_ref, w_ref, vec_ref, first_ref, low_ref, sums_ref, slots_ref, *, layout):
    groups, micro, halves, heads_dev = layout
    grad = own_ref[...] + got_ref[...].astype(F32) + second_ref[...]
    normed = normed_ref[...]
    d_first = norm_back(grad, normed, inv_ref[...], vec_ref[0:1])
    low = d_first.astype(BF)
    first_ref[...] = d_first
    low_ref[...] = low
    sums_ref[...] = column_sums(grad * normed, grad, low.astype(F32))
    d_attn = dot(low, w_ref[...], NT).astype(BF)
    half = slots_ref.shape[1]
    hd = slots_ref.shape[2] // 2
    for m in range(micro):
        for j in range(groups * heads_dev):
            piece = d_attn[m * 2 * half : (m + 1) * 2 * half, j * hd : (j + 1) * hd]
            piece = jnp.concatenate([piece[:half], piece[half:]], axis=1)
            first = ((j // heads_dev) * micro + m) * halves
            slots_ref[first + j % heads_dev] = piece
            if j % heads_dev == heads_dev - 1:
                for b in range(heads_dev, halves):
                    slots_ref[first + b] = piece


def tokens_kernel(slots_ref, w_ref, first_ref, out_ref, d_ref, *, layout):
    piece_rows = slots_ref.shape[1] // 3
    total = first_ref[...]
    for c in range(3):
        unpack_heads(slots_ref, d_ref.at[c], layout, piece_rows, c)
        total = total + dot(d_ref[c], w_ref[c], NT)
    out_ref[...] = total.astype(BF)


def normalise(hidden):
    center = hidden - jnp.mean(hidden, axis=-1, keepdims=True)
    spread = jnp.mean(center * center, axis=-1, keepdims=True)
    inverse = lax.rsqrt(spread + norm_eps)
    return center * inverse, inverse


def norm_back(grad, normed, inverse, gain):
    e = grad * gain
    return inverse * (
        e
        - jnp.mean(e, axis=-1, keepdims=True)
        - normed * jnp.mean(e * normed, axis=-1, keepdims=True)
    )


def after(value, *others):
    return lax.optimization_barrier((value, *others))[0]


def by_core(value):
    return lax.ppermute(value, "head", [(0, 1), (1, 0), (2, 3), (3, 2)])


def by_x(value):
    return lax.ppermute(value, "head", [(0, 2), (2, 0), (1, 3), (3, 1)])


def swap(value, axes, groups=None):
    return lax.all_to_all(
        value, axes, split_axis=0, concat_axis=0, tiled=True, axis_index_groups=groups
    )


def spread_over(value, axes, count, groups=None):
    return swap(jnp.broadcast_to(value[None], (count, *value.shape)), axes, groups)


def gather_group(rows):
    across_x = by_x(rows)
    return rows, across_x, by_core(rows), by_core(across_x)


def reduce_group(keep, send):
    count, depth = keep.shape[0] // 2, keep.shape[1]
    shape = (count, depth)
    own, send = call(add_kernel, ((shape, F32), (shape, BF)), (keep, by_core(send)), "add", 1e6)
    return own, by_x(send)


def stack_rows(*values):
    blank = jnp.zeros_like(values[0])
    return jnp.stack([*values, *[blank] * (8 - len(values))])


def in_order(blocks):
    index = lax.axis_index("head")
    own, across_x, across_core, across = blocks
    odd, far = index % 2 == 1, index // 2 == 1
    near = [jnp.where(odd, q, p) for p, q in ((own, across_core), (across_core, own))]
    wide = [jnp.where(odd, q, p) for p, q in ((across_x, across), (across, across_x))]
    return jnp.stack(
        [jnp.where(far, q, p) for p, q in zip(near + wide, wide + near)]
    )


def to_group(blocks):
    index = lax.axis_index("head")

    def block(offset):
        return lax.dynamic_index_in_dim(blocks, index ^ offset, 0, keepdims=False)

    across = lax.ppermute(block(3), "head", [(i, i ^ 3) for i in range(4)])
    return in_order((block(0), by_x(block(2)), by_core(block(1)), across))


def key_ranges(spans, bq, bk):
    return spans[0, ::bq] // bk, cdiv(spans[1, bq - 1 :: bq], bk)


def local(
    inputs,
    doc_lengths,
    grad_out,
    qkv_weight,
    out_weight,
    inner_weight,
    outer_weight,
    bias_rows,
    inner_bias,
    norm_gains,
    norm_shifts,
):
    micro, tokens, depth = inputs.shape
    groups, cycle = lax.axis_size("head"), lax.axis_size("blk")
    halves = cycle // 2
    devices = groups * cycle
    length = devices * tokens
    hd = depth // HEADS
    heads_dev = HEADS // groups
    rows_dev = qkv_weight.shape[1]
    ff_dev = outer_weight.shape[0]
    ff_part = cycle * ff_dev
    half_tokens = tokens // 2
    head_index = lax.axis_index("head")
    blk_index = lax.axis_index("blk")
    half = blk_index // halves
    unit_head = head_index * heads_dev + jnp.minimum(blk_index % halves, heads_dev - 1)
    unit_of = [min(i, heads_dev - 1) for i in range(halves)]

    own_x = lax.dynamic_index_in_dim(inputs, half, 0, keepdims=False)
    other_x = lax.dynamic_index_in_dim(inputs, 1 - half, 0, keepdims=False)
    got_x = lax.ppermute(other_x, "blk", [(i, (i + halves) % cycle) for i in range(cycle)])
    pair_x = jnp.concatenate([own_x, got_x], axis=0)
    cube = [
        [h * cycle + b for h in (c, c + 2) for b in range(s * halves, (s + 1) * halves)]
        for c in range(2)
        for s in range(2)
    ]
    inner_own = inner_weight.reshape(rows_dev, groups, ff_part)
    inner_own = to_group(inner_own.transpose(1, 0, 2)).reshape(groups * rows_dev, ff_part)
    ffn = jnp.concatenate([inner_own, outer_weight, out_weight])

    units = tuple(h * heads_dev + u for h in range(groups) for u in unit_of)
    (slots,) = call(
        functools.partial(head_slots_kernel, units=units),
        (((groups * halves, 2, rows_dev, 2 * hd), BF),),
        (qkv_weight, bias_rows, norm_gains, norm_shifts, inner_bias.reshape(rows_dev, -1)),
        "head_slots",
        1e6,
        params=LARGE,
    )
    half_groups = [
        [h * cycle + b for h in range(groups) for b in range(n * halves, (n + 1) * halves)]
        for n in range(2)
    ]
    slots, pair_x = lax.optimization_barrier((swap(slots, BOTH, half_groups), pair_x))
    far_slots = lax.ppermute(slots, "blk", [(i, (i + halves) % cycle) for i in range(cycle)])
    near, far = [v.reshape(groups, halves, 2, rows_dev, 2 * hd) for v in (slots, far_slots)]
    both = jnp.stack([jnp.where(half == 0, near, far), jnp.where(half == 0, far, near)], axis=1)
    qk_weight = both[:, :, :, 0].reshape(depth, 2 * hd)
    v_weight = both[:, :, :, 1].reshape(depth, 2 * hd)
    small = both[:, :, :, 1, :, hd : hd + 12].astype(F32).reshape(depth, 12).T

    bias, gains, shifts = small[0:4], small[4:6], small[6:8]
    inner_bias_all = small[8:12].T.reshape(groups, ff_part)
    inner_bias_part = lax.dynamic_index_in_dim(inner_bias_all, head_index, 0, keepdims=False)
    unit_bias = lax.dynamic_slice(bias[0:2], (0, unit_head * hd), (2, hd))
    unit_bias = jnp.pad(unit_bias, ((0, 0), (0, hd)))

    qkv_all = lax.all_gather(after(qkv_weight, ffn), BOTH, axis=0, tiled=False)
    ffn_all = lax.all_gather(after(ffn, slots), "blk", axis=0, tiled=False)
    lengths = lax.dynamic_index_in_dim(doc_lengths, half, 0, keepdims=False)
    order = jnp.arange(lengths.shape[0], dtype=jnp.int32)
    bounds = jnp.sum(jnp.where(order[None, :] <= order[:, None], lengths[None, :], 0), axis=1)
    positions = jnp.arange(length, dtype=jnp.int32)[None, :]
    starts = (bounds - lengths)[:, None]
    own = (positions >= starts) & (positions < bounds[:, None])
    spans = jnp.stack(
        [
            jnp.sum(jnp.where(own, starts, 0), axis=0),
            jnp.sum(jnp.where(own, bounds[:, None], 0), axis=0),
        ]
    )

    place = jnp.stack([head_index % 2, half]).astype(jnp.int32)
    block = 512 if length <= 4096 else 256
    ranges = key_ranges(spans, block, 512), key_ranges(spans, 512, 256)
    small_rows = (
        stack_rows(bias[2], gains[0], shifts[0]),
        stack_rows(gains[0], shifts[0], bias[3], gains[1], shifts[1]),
        stack_rows(gains[0]),
        inner_bias_part[None],
    )
    tokens_a = spread_over(pair_x, BOTH, cycle, cube)
    prepared = (qk_weight, v_weight, unit_bias, small_rows, spans, place, ranges)
    tokens_a, prepared = lax.optimization_barrier((tokens_a, prepared))
    qk_weight, v_weight, unit_bias, small_rows, spans, place, ranges = prepared
    tokens_b = by_core(tokens_a)

    per = max(1, 256 // tokens)
    q, k, v, kt, vt = project(
        place, tokens_a, tokens_b, qk_weight, v_weight, unit_bias, halves, per
    )
    lo, hi = ranges[0]
    attn_out, attn_t, lse = attend(lo, hi, q, k, vt, spans, tokens, block, 512)

    ffn = after(ffn_all, attn_out)
    inner_part = (
        ffn[:, : groups * rows_dev]
        .reshape(cycle, groups, rows_dev, ff_part)
        .transpose(1, 0, 2, 3)
        .reshape(depth, ff_part)
    )
    last = groups * rows_dev + ff_dev
    outer_part = ffn[:, groups * rows_dev : last].reshape(ff_part, depth)
    out_part = ffn[:, last:].reshape(depth // groups, depth)
    attn_slots = swap(attn_out, BOTH)
    out_x, attn_slots, inner_part, outer_part = lax.optimization_barrier(
        (by_x(out_part), attn_slots, inner_part, outer_part)
    )
    out_all = in_order((out_part, out_x, by_core(out_part), by_core(out_x))).reshape(depth, depth)

    rows = micro * tokens
    layout = (groups, micro, halves, heads_dev)
    flat, group = (rows, depth), (groups * rows, ff_part)
    attn, normed_low, normed_one, inverse_one = call(
        functools.partial(branch_kernel, layout=layout),
        ((flat, BF), (flat, BF), (flat, F32), ((rows, 1), F32)),
        (attn_slots, inputs.reshape(flat), out_all, small_rows[0]),
        "branch",
        1e6,
    )
    act_low, slope, normed_group, keep, send = call(
        inner_kernel,
        ((group, BF), (group, F32), ((groups * rows, depth), BF), ((2 * rows, depth), F32), ((2 * rows, depth), BF)),
        (*gather_group(normed_low), inner_part, outer_part, small_rows[3]),
        "inner",
        1e6,
    )
    output, d_second, d_ffn, sums_two = call(
        output_kernel,
        ((flat, BF), (flat, F32), (flat, BF), ((8, depth), F32)),
        (
            *reduce_group(keep, send),
            normed_one,
            grad_out.reshape(flat),
            small_rows[1],
        ),
        "output",
        1e6,
    )
    output = output.reshape(inputs.shape)
    d_inner, d_ffn_group, inner_sums, keep, send = call(
        inner_back_kernel,
        ((group, BF), ((groups * rows, depth), BF), ((1, ff_part), F32), ((2 * rows, depth), F32), ((2 * rows, depth), BF)),
        (*gather_group(d_ffn), inner_part, outer_part, slope),
        "inner_back",
        1e6,
    )
    own, got = reduce_group(keep, send)
    (ffn_grad,) = call(
        feed_grad_kernel,
        (((cycle, 2 * groups, rows_dev, depth), BF),),
        (normed_group, d_inner, act_low, d_ffn_group),
        "feed_grad",
        1e6,
        [pltpu.VMEM((depth, depth), F32)],
    )
    got, ffn_grad = lax.optimization_barrier((got, ffn_grad))
    d_first, d_branch, sums_one, d_heads = call(
        functools.partial(branch_back_kernel, layout=layout),
        ((flat, F32), (flat, BF), ((8, depth), F32), ((devices, half_tokens, 2 * hd), BF)),
        (
            own,
            got,
            d_second,
            normed_one,
            inverse_one,
            out_all,
            small_rows[2],
        ),
        "branch_back",
        1e6,
    )
    d_heads = swap(d_heads, BOTH)

    ffn_grad = lax.psum_scatter(ffn_grad, "blk", scatter_dimension=0, tiled=False)
    outer_grad = ffn_grad[groups:].reshape(ff_dev, depth).astype(F32)
    inner_grad = to_group(ffn_grad[:groups])
    inner_grad = inner_grad.transpose(1, 0, 2).reshape(rows_dev, groups * ff_part).astype(F32)
    out_grad = dot(attn, d_branch, TN).reshape(groups, depth // groups, depth)

    def out_block(offset):
        return lax.dynamic_index_in_dim(out_grad, head_index ^ offset, 0, keepdims=False)

    from_core = by_core(jnp.stack([out_block(1), out_block(3)]).astype(BF)).astype(F32)
    from_x = by_x((out_block(2) + from_core[1]).astype(BF)).astype(F32)
    out_grad = (out_block(0) + from_core[0] + from_x).astype(BF)
    out_terms = swap(out_grad.reshape(cycle, rows_dev, depth), "blk")
    out_grad = jnp.sum(
        out_terms.astype(F32), axis=0
    )

    lo, hi = ranges[1]
    qkv_out, qkv_t, qv_sums = attend_back(
        lo, hi, q, k, v, kt, attn_t, lse, d_heads, spans, tokens, 512, 256
    )
    qkv_home = swap(after(qkv_out, out_terms), BOTH)
    qkv_all = qkv_all.transpose(1, 0, 2, 3).reshape(3, depth, depth)
    (grad_inputs,) = call(
        functools.partial(tokens_kernel, layout=layout),
        ((flat, BF),),
        (qkv_home, qkv_all, d_first),
        "tokens",
        1e6,
        [pltpu.VMEM((3, rows, depth), BF)],
    )
    grad_inputs = grad_inputs.reshape(inputs.shape)

    unit_grad = weight_grad(place, tokens_a, tokens_b, qkv_t, halves, per)
    wide = jnp.zeros((2, HEADS, hd), F32)
    wide = lax.dynamic_update_slice(wide, qv_sums.reshape(2, 1, hd), (0, unit_head, 0))
    wide = jnp.where((blk_index % halves < heads_dev), wide, 0.0)
    sums = jnp.stack(
        [wide[0].reshape(depth), wide[1].reshape(depth), sums_one[2], sums_two[2]]
        + [sums_one[0], sums_two[0], sums_one[1], sums_two[1]]
    ).T
    inner_sums = inner_sums.reshape(1, cycle, rows_dev, ff_dev // rows_dev)
    inner_sums = jnp.broadcast_to(inner_sums, (groups, *inner_sums.shape[1:]))
    extra = jnp.concatenate(
        [
            sums.reshape(devices, rows_dev, 8),
            inner_sums.reshape(devices, rows_dev, -1),
        ],
        axis=2,
    ).astype(BF)
    extra = jnp.pad(extra, ((0, 0), (0, 0), (0, hd - extra.shape[2])))
    final = jnp.concatenate([unit_grad.reshape(devices, rows_dev, 3 * hd), extra], axis=2)
    final = after(swap(after(final, qkv_home), BOTH), grad_inputs)
    qkv_grad, bias_grad, gains_grad, shifts_grad, inner_bias_grad = call(
        functools.partial(collect_kernel, layout=layout),
        (
            ((3, rows_dev, depth), F32),
            ((4, rows_dev), F32),
            ((2, rows_dev), F32),
            ((2, rows_dev), F32),
            ((rows_dev, hd), F32),
        ),
        (head_index[None], final),
        "collect",
        1e6,
    )
    return (
        output,
        grad_inputs,
        qkv_grad,
        out_grad,
        inner_grad,
        outer_grad,
        bias_grad,
        inner_bias_grad[:, 8 : 8 + ff_dev // rows_dev].reshape(ff_dev),
        gains_grad,
        shifts_grad,
    )


def solution(mesh):
    tokens = P(None, BOTH, None)
    rows = P(BOTH, None)
    columns = P(None, BOTH)
    return jax.shard_map(
        local,
        mesh=mesh,
        in_specs=(tokens, P(), tokens, tokens, rows, rows, rows, columns, P(BOTH), columns, columns),
        out_specs=(tokens, tokens, tokens, rows, rows, rows, columns, P(BOTH), columns, columns),
        check_vma=False,
    )
```

```python
import functools
import math

import jax
import jax.numpy as jnp
from jax import lax
from jax.experimental import pallas as pl
from jax.experimental.pallas import tpu as pltpu
from jax.sharding import PartitionSpec as P

HEADS = 12
F32 = jnp.float32
BF = jnp.bfloat16
NT = (((1,), (1,)), ((), ()))
NN = (((1,), (0,)), ((), ()))
TN = (((0,), (0,)), ((), ()))
LOG2E = math.log2(math.e)
BOTH = ("head", "blk")
norm_eps = 1e-12
masked_score = -1e30
VMEM = pl.BlockSpec(memory_space=pltpu.VMEM)
SMEM = pl.BlockSpec(memory_space=pltpu.SMEM)
SMALL = pltpu.CompilerParams(vmem_limit_bytes=14 << 20)
LARGE = pltpu.CompilerParams(vmem_limit_bytes=56 << 20)


def dot(a, b, dims):
    return lax.dot_general(a, b, dims, preferred_element_type=F32)


def cdiv(a, b):
    return -(-a // b)


def chunk_walk(place_ref, blocks, halves, per, tokens, visit):
    core, half = place_ref[0], place_ref[1]
    runs = halves // per
    for source in range(2):

        def one(n, carry, source=source):
            xh = n // (2 * runs)
            rel = n // runs % 2
            run = n % runs
            head = xh * 2 + (core if source == 0 else 1 - core)
            position = ((head * 2 + (rel ^ half)) * halves + run * per) * tokens
            rows = pl.ds(pl.multiple_of(rel * tokens, tokens), tokens)

            def load(ref):
                return jnp.concatenate(
                    [ref[xh * halves + run * per + k, rows, :] for k in range(per)], axis=0
                )

            visit(source, load, pl.multiple_of(position, per * tokens))
            return carry

        lax.fori_loop(0, 4 * runs, one, 0, unroll=4 * runs <= 4)


def project_kernel(
    place_ref, a_ref, b_ref, qk_ref, v_w_ref, bias_ref, q_ref, k_ref, v_ref, kt_ref, vt_ref, *, halves, per
):
    tokens = a_ref.shape[1] // 2
    hd = q_ref.shape[1]

    def visit(source, load, position):
        x = load((a_ref, b_ref)[source])
        rows = pl.ds(position, per * tokens)
        qk = dot(x, qk_ref[...], NN) + bias_ref[0:1]
        v = (dot(x, v_w_ref[...], NN) + bias_ref[1:2])[:, :hd]
        k = qk[:, hd:]
        q_ref[rows, :] = qk[:, :hd].astype(BF)
        k_ref[rows, :] = k.astype(BF)
        v_ref[rows, :] = v.astype(BF)
        kt_ref[:, rows] = k.T.astype(BF)
        vt_ref[:, rows] = v.T.astype(BF)

    chunk_walk(place_ref, a_ref.shape[0], halves, per, tokens, visit)


def project(place, a, b, qk, v, bias, halves, per):
    length = 2 * a.shape[0] * a.shape[1]
    hd = qk.shape[1] // 2
    rows = jax.ShapeDtypeStruct((length, hd), BF)
    columns = jax.ShapeDtypeStruct((hd, length), BF)
    return pl.pallas_call(
        functools.partial(project_kernel, halves=halves, per=per),
        out_shape=(rows, rows, rows, columns, columns),
        in_specs=[SMEM] + [VMEM] * 5,
        out_specs=(VMEM,) * 5,
        compiler_params=LARGE,
        cost_estimate=pl.CostEstimate(flops=1000000, bytes_accessed=1 << 10, transcendentals=0),
        name="project",
    )(place, a, b, qk, v, bias)


def head_slots_kernel(w_ref, bias_ref, gains_ref, shifts_ref, inner_ref, out_ref, *, units):
    hd = w_ref.shape[2] // HEADS
    rows = [ref[...].astype(F32) for ref in (bias_ref, gains_ref, shifts_ref)]
    inner = inner_ref[...].astype(F32)
    blank = jnp.zeros((inner.shape[0], hd - 8 - inner.shape[1]), F32)
    small = jnp.concatenate([jnp.concatenate(rows, axis=0).T, inner, blank], axis=1).astype(BF)
    done = {}
    for d, j in enumerate(units):
        if j not in done:
            part = [w_ref[c][:, j * hd : (j + 1) * hd] for c in range(3)]
            done[j] = [
                jnp.concatenate(part[:2], axis=1),
                jnp.concatenate([part[2], small], axis=1),
            ]
        out_ref[d, 0] = done[j][0]
        out_ref[d, 1] = done[j][1]


def weight_grad_kernel(place_ref, a_ref, b_ref, gt_ref, out_ref, acc_ref, *, halves, per):
    tokens = a_ref.shape[1] // 2
    acc_ref[...] = jnp.zeros_like(acc_ref)

    def visit(source, load, position):
        x = load((a_ref, b_ref)[source])
        acc_ref[...] += dot(gt_ref[:, pl.ds(position, per * tokens)], x, NN)

    chunk_walk(place_ref, a_ref.shape[0], halves, per, tokens, visit)
    out_ref[...] = acc_ref[...].T.astype(BF)


def weight_grad(place, a, b, gt, halves, per):
    depth = a.shape[2]
    length = gt.shape[1]
    return pl.pallas_call(
        functools.partial(weight_grad_kernel, halves=halves, per=per),
        out_shape=jax.ShapeDtypeStruct((depth, gt.shape[0]), BF),
        in_specs=[SMEM] + [VMEM] * 3,
        out_specs=VMEM,
        scratch_shapes=[pltpu.VMEM((gt.shape[0], depth), F32)],
        compiler_params=SMALL if length <= 4096 else LARGE,
        cost_estimate=pl.CostEstimate(flops=1000000, bytes_accessed=1 << 10, transcendentals=0),
        name="weight_grad",
    )(place, a, b, gt)


def inside(first, start, stop, bk):
    key = first + lax.broadcasted_iota(jnp.int32, (bk, start.shape[1]), 0)
    return (key >= start) & (key < stop)


def attend_kernel(
    lo_ref, hi_ref, q_ref, k_ref, vt_ref, span_ref, out_ref, ot_ref, lse_ref, s_ref,
    *, bq, bk, pack
):
    length, hd = q_ref.shape
    factor = LOG2E / math.sqrt(hd)
    half = pack // 2

    def q_step(i, carry):
        qs = pl.ds(pl.multiple_of(i * bq, bq), bq)
        q = q_ref[qs, :]
        start, stop = span_ref[0:1, qs], span_ref[1:2, qs]
        lo, hi = lo_ref[i], hi_ref[i]

        def first(j, top):
            ks = pl.ds(pl.multiple_of(j * bk, bk), bk)
            s = dot(k_ref[ks, :], q, NT) * factor
            s = jnp.where(inside(j * bk, start, stop, bk), s, masked_score)
            s_ref[ks, :] = s
            return jnp.maximum(top, jnp.max(s.reshape(bk // 8, 8, bq), axis=0))

        top = lax.fori_loop(lo, hi, first, jnp.full((8, bq), masked_score, F32))
        peak = jnp.max(top, axis=0, keepdims=True)

        def second(j, state):
            total, acc = state
            ks = pl.ds(pl.multiple_of(j * bk, bk), bk)
            p = jnp.exp2(s_ref[ks, :] - peak)
            total = total + jnp.sum(p.reshape(bk // 8, 8, bq), axis=0)
            return total, acc + dot(vt_ref[:, ks], p.astype(BF), NN)

        total, acc = lax.fori_loop(
            lo, hi, second, (jnp.zeros((8, bq), F32), jnp.zeros((hd, bq), F32))
        )
        total = jnp.sum(total, axis=0, keepdims=True)
        out = acc / total
        ot_ref[:, qs] = out
        lse_ref[:, qs] = peak + jnp.log2(total)
        rows = out.T.astype(BF)
        for c in range(bq // pack):
            piece = rows[c * pack : (c + 1) * pack]
            out_ref[i * (bq // pack) + c] = jnp.concatenate([piece[:half], piece[half:]], axis=1)
        return carry

    lax.fori_loop(0, length // bq, q_step, 0)


def attend(lo, hi, q, k, vt, spans, pack, bq, bk):
    length, hd = q.shape
    return pl.pallas_call(
        functools.partial(attend_kernel, bq=bq, bk=bk, pack=pack),
        out_shape=(
            jax.ShapeDtypeStruct((length // pack, pack // 2, 2 * hd), BF),
            jax.ShapeDtypeStruct((hd, length), F32),
            jax.ShapeDtypeStruct((1, length), F32),
        ),
        in_specs=[SMEM, SMEM] + [VMEM] * 4,
        out_specs=(VMEM,) * 3,
        scratch_shapes=[pltpu.VMEM((length, bq), F32)],
        compiler_params=LARGE,
        cost_estimate=pl.CostEstimate(flops=1000000, bytes_accessed=1 << 10, transcendentals=0),
        name="attend",
    )(lo, hi, q, k, vt, spans)


def attend_back_kernel(
    lo_ref, hi_ref, q_ref, k_ref, v_ref, kt_ref, ot_ref, lse_ref, do_ref, span_ref,
    out_ref, gt_ref, sums_ref, dq_ref, dk_ref, dv_ref, *, bq, bk, pack
):
    length, hd = q_ref.shape
    scale = 1.0 / math.sqrt(hd)
    factor = LOG2E * scale
    half = pack // 2
    dk_ref[...] = jnp.zeros_like(dk_ref)
    dv_ref[...] = jnp.zeros_like(dv_ref)

    def q_step(i, carry):
        qs = pl.ds(pl.multiple_of(i * bq, bq), bq)
        q = q_ref[qs, :]
        start, stop = span_ref[0:1, qs], span_ref[1:2, qs]
        pieces = []
        for c in range(bq // pack):
            piece = do_ref[i * (bq // pack) + c]
            pieces += [piece[:, :hd], piece[:, hd:]]
        do = jnp.concatenate(pieces, axis=0)
        delta = jnp.sum(do.astype(F32).T * ot_ref[:, qs], axis=0, keepdims=True)
        lse = lse_ref[:, qs]

        def step(j, acc):
            ks = pl.ds(pl.multiple_of(j * bk, bk), bk)
            s = dot(k_ref[ks, :], q, NT) * factor - lse
            p = jnp.where(inside(j * bk, start, stop, bk), jnp.exp2(s), 0.0)
            dp = dot(v_ref[ks, :], do, NT)
            ds = (p * (dp - delta)).astype(BF)
            dv_ref[ks, :] += dot(p.astype(BF), do, NN)
            dk_ref[ks, :] += dot(ds, q, NN)
            return acc + dot(kt_ref[:, ks], ds, NN)

        acc = lax.fori_loop(lo_ref[i], hi_ref[i], step, jnp.zeros((hd, bq), F32))
        dq_ref[:, qs] = acc
        return carry

    lax.fori_loop(0, length // bq, q_step, 0)

    def emit(i, sums):
        rows = pl.ds(pl.multiple_of(i * bq, bq), bq)
        dqt = (dq_ref[:, rows] * scale).astype(BF)
        dk = (dk_ref[rows, :] * scale).astype(BF)
        dv = dv_ref[rows, :].astype(BF)
        dq = dqt.astype(F32).T.astype(BF)
        gt_ref[0:hd, rows] = dqt
        gt_ref[hd : 2 * hd, rows] = dk.astype(F32).T.astype(BF)
        gt_ref[2 * hd : 3 * hd, rows] = dv.astype(F32).T.astype(BF)
        for c in range(bq // pack):
            for n, value in enumerate((dq, dk, dv)):
                piece = value[c * pack : (c + 1) * pack]
                out_ref[i * (bq // pack) + c, n * half : (n + 1) * half, :] = jnp.concatenate(
                    [piece[:half], piece[half:]], axis=1
                )
        both = jnp.concatenate([dq.astype(F32), dv.astype(F32)], axis=1)
        return sums + jnp.sum(both, axis=0, keepdims=True)

    sums_ref[...] = lax.fori_loop(0, length // bq, emit, jnp.zeros((1, 2 * hd), F32))


def attend_back(lo, hi, q, k, v, kt, ot, lse, do, spans, pack, bq, bk):
    length, hd = q.shape
    return pl.pallas_call(
        functools.partial(attend_back_kernel, bq=bq, bk=bk, pack=pack),
        out_shape=(
            jax.ShapeDtypeStruct((length // pack, 3 * pack // 2, 2 * hd), BF),
            jax.ShapeDtypeStruct((3 * hd, length), BF),
            jax.ShapeDtypeStruct((1, 2 * hd), F32),
        ),
        in_specs=[SMEM, SMEM] + [VMEM] * 8,
        out_specs=(VMEM,) * 3,
        scratch_shapes=[
            pltpu.VMEM((hd, length), F32),
            pltpu.VMEM((length, hd), F32),
            pltpu.VMEM((length, hd), F32),
        ],
        compiler_params=LARGE,
        cost_estimate=pl.CostEstimate(flops=1000000, bytes_accessed=1 << 10, transcendentals=0),
        name="attend_back",
    )(lo, hi, q, k, v, kt, ot, lse, do, spans)


def call(kernel, outs, ins, name, flops, scratch=(), params=SMALL):
    return pl.pallas_call(
        kernel,
        out_shape=tuple(jax.ShapeDtypeStruct(shape, kind) for shape, kind in outs),
        in_specs=[SMEM if v.dtype == jnp.int32 else VMEM for v in ins],
        out_specs=(VMEM,) * len(outs),
        scratch_shapes=list(scratch),
        compiler_params=params,
        cost_estimate=pl.CostEstimate(
            flops=int(flops), bytes_accessed=1 << 10, transcendentals=0
        ),
        name=name,
    )(*ins)


def column_sums(*values):
    sums = [jnp.sum(v, axis=0, keepdims=True) for v in values]
    return jnp.concatenate(sums + [jnp.zeros_like(sums[0])] * (8 - len(sums)), axis=0)


def unpack_heads(slots_ref, out_ref, layout, piece_rows, which):
    groups, micro, halves, heads_dev = layout
    hd = slots_ref.shape[2] // 2
    part = slice(which * piece_rows, (which + 1) * piece_rows)
    for m in range(micro):
        rows = slice(m * 2 * piece_rows, (m + 1) * 2 * piece_rows)
        pieces = []
        for j in range(groups * heads_dev):
            piece = slots_ref[((j // heads_dev) * micro + m) * halves + j % heads_dev, part, :]
            pieces.append(jnp.concatenate([piece[:, :hd], piece[:, hd:]], axis=0))
        for j in range(0, groups * heads_dev, 2):
            out_ref[rows, j * hd : (j + 2) * hd] = jnp.concatenate(pieces[j : j + 2], axis=1)


def branch_kernel(slots_ref, x_ref, w_ref, vec_ref, attn_ref, low_ref, normed_ref, inv_ref, *, layout):
    unpack_heads(slots_ref, attn_ref, layout, slots_ref.shape[1], 0)
    first_sum = x_ref[...].astype(F32) + dot(attn_ref[...], w_ref[...], NN) + vec_ref[0:1]
    normed, inverse = normalise(first_sum)
    normed_ref[...] = normed
    inv_ref[...] = inverse
    low_ref[...] = (normed * vec_ref[1:2] + vec_ref[2:3]).astype(BF)


def normal_cdf(v):
    bell = jnp.exp(-0.5 * v * v) * (1.0 / math.sqrt(2.0 * math.pi))
    return 0.5 * (1.0 + lax.erf(v * (1.0 / math.sqrt(2.0)))), bell


def inner_kernel(a_ref, b_ref, c_ref, d_ref, wi_ref, wo_ref, bias_ref, act_ref, slope_ref, low_ref, keep_ref, send_ref):
    count = a_ref.shape[0]
    for n, ref in enumerate((a_ref, b_ref, c_ref, d_ref)):
        rows = slice(n * count, (n + 1) * count)
        x = ref[...]
        low_ref[rows, :] = x
        pre = dot(x, wi_ref[...], NN) + bias_ref[...]
        cdf, bell = normal_cdf(pre)
        slope_ref[rows, :] = cdf + pre * bell
        act = (pre * cdf).astype(BF)
        act_ref[rows, :] = act
        partial = dot(act, wo_ref[...], NN)
        if n < 2:
            keep_ref[rows, :] = partial
        else:
            send_ref[(n - 2) * count : (n - 1) * count, :] = partial.astype(BF)


def inner_back_kernel(a_ref, b_ref, c_ref, d_ref, wi_ref, wo_ref, slope_ref, inner_ref, low_ref, sums_ref, keep_ref, send_ref):
    count = a_ref.shape[0]
    sums = 0.0
    for n, ref in enumerate((a_ref, b_ref, c_ref, d_ref)):
        rows = slice(n * count, (n + 1) * count)
        x = ref[...]
        low_ref[rows, :] = x
        inner = (dot(x, wo_ref[...], NT) * slope_ref[rows, :]).astype(BF)
        inner_ref[rows, :] = inner
        sums = sums + jnp.sum(inner.astype(F32), axis=0, keepdims=True)
        partial = dot(inner, wi_ref[...], NT)
        if n < 2:
            keep_ref[rows, :] = partial
        else:
            send_ref[(n - 2) * count : (n - 1) * count, :] = partial.astype(BF)
    sums_ref[...] = sums


def feed_grad_kernel(low_ref, inner_ref, act_ref, ffn_ref, out_ref, acc_ref):
    cycle, blocks, rows = out_ref.shape[:3]
    half = blocks // 2
    acc_ref[...] = dot(low_ref[...], inner_ref[...], TN)
    for b in range(cycle):
        for h in range(half):
            first = (h * cycle + b) * rows
            out_ref[b, h] = acc_ref[first : first + rows, :].astype(BF)
    acc_ref[...] = dot(act_ref[...], ffn_ref[...], TN)
    for b in range(cycle):
        for h in range(half):
            first = (b * half + h) * rows
            out_ref[b, half + h] = acc_ref[first : first + rows, :].astype(BF)


def collect_kernel(head_ref, slots_ref, qkv_ref, bias_ref, gains_ref, shifts_ref, inner_ref, *, layout):
    groups, micro, halves, heads_dev = layout
    hd = slots_ref.shape[2] // 4
    cycle = micro * halves
    pieces = []
    for j in range(groups * heads_dev):
        first = (j // heads_dev) * cycle + j % heads_dev
        piece = slots_ref[first, :, : 3 * hd].astype(F32)
        for m in range(1, micro):
            piece = piece + slots_ref[first + m * halves, :, : 3 * hd].astype(F32)
        pieces.append(piece)
    for c in range(3):
        for j in range(0, groups * heads_dev, 2):
            pair = [p[:, c * hd : (c + 1) * hd] for p in pieces[j : j + 2]]
            qkv_ref[c, :, j * hd : (j + 2) * hd] = jnp.concatenate(pair, axis=1)
    own = slots_ref[pl.ds(head_ref[0] * cycle, cycle), :, 3 * hd :].astype(F32)
    inner_ref[...] = jnp.sum(own, axis=0)
    sums = jnp.sum(slots_ref[:, :, 3 * hd :].astype(F32), axis=0).T
    bias_ref[...] = sums[0:4]
    gains_ref[...] = sums[4:6]
    shifts_ref[...] = sums[6:8]


def add_kernel(keep_ref, got_ref, own_ref, send_ref):
    count = own_ref.shape[0]
    own_ref[...] = keep_ref[:count] + got_ref[:count].astype(F32)
    send_ref[...] = (keep_ref[count:] + got_ref[count:].astype(F32)).astype(BF)


def output_kernel(own_ref, got_ref, normed_ref, grad_ref, vec_ref, out_ref, second_ref, low_ref, sums_ref):
    first_normed = normed_ref[...] * vec_ref[0:1] + vec_ref[1:2]
    second_sum = first_normed + own_ref[...] + got_ref[...].astype(F32) + vec_ref[2:3]
    normed, inverse = normalise(second_sum)
    out_ref[...] = (normed * vec_ref[3:4] + vec_ref[4:5]).astype(BF)
    grad = grad_ref[...].astype(F32)
    d_second = norm_back(grad, normed, inverse, vec_ref[3:4])
    low = d_second.astype(BF)
    second_ref[...] = d_second
    low_ref[...] = low
    sums_ref[...] = column_sums(grad * normed, grad, low.astype(F32))


def branch_back_kernel(own_ref, got_ref, second_ref, normed_ref, inv_ref, w_ref, vec_ref, first_ref, low_ref, sums_ref, slots_ref, *, layout):
    groups, micro, halves, heads_dev = layout
    grad = own_ref[...] + got_ref[...].astype(F32) + second_ref[...]
    normed = normed_ref[...]
    d_first = norm_back(grad, normed, inv_ref[...], vec_ref[0:1])
    low = d_first.astype(BF)
    first_ref[...] = d_first
    low_ref[...] = low
    sums_ref[...] = column_sums(grad * normed, grad, low.astype(F32))
    d_attn = dot(low, w_ref[...], NT).astype(BF)
    half = slots_ref.shape[1]
    hd = slots_ref.shape[2] // 2
    for m in range(micro):
        for j in range(groups * heads_dev):
            piece = d_attn[m * 2 * half : (m + 1) * 2 * half, j * hd : (j + 1) * hd]
            piece = jnp.concatenate([piece[:half], piece[half:]], axis=1)
            first = ((j // heads_dev) * micro + m) * halves
            slots_ref[first + j % heads_dev] = piece
            if j % heads_dev == heads_dev - 1:
                for b in range(heads_dev, halves):
                    slots_ref[first + b] = piece


def tokens_kernel(slots_ref, w_ref, first_ref, out_ref, d_ref, *, layout):
    piece_rows = slots_ref.shape[1] // 3
    total = first_ref[...]
    for c in range(3):
        unpack_heads(slots_ref, d_ref.at[c], layout, piece_rows, c)
        total = total + dot(d_ref[c], w_ref[c], NT)
    out_ref[...] = total.astype(BF)


def normalise(hidden):
    center = hidden - jnp.mean(hidden, axis=-1, keepdims=True)
    spread = jnp.mean(center * center, axis=-1, keepdims=True)
    inverse = lax.rsqrt(spread + norm_eps)
    return center * inverse, inverse


def norm_back(grad, normed, inverse, gain):
    e = grad * gain
    return inverse * (
        e
        - jnp.mean(e, axis=-1, keepdims=True)
        - normed * jnp.mean(e * normed, axis=-1, keepdims=True)
    )


def after(value, *others):
    return lax.optimization_barrier((value, *others))[0]


def by_core(value):
    return lax.ppermute(value, "head", [(0, 1), (1, 0), (2, 3), (3, 2)])


def by_x(value):
    return lax.ppermute(value, "head", [(0, 2), (2, 0), (1, 3), (3, 1)])


def swap(value, axes, groups=None):
    return lax.all_to_all(
        value, axes, split_axis=0, concat_axis=0, tiled=True, axis_index_groups=groups
    )


def spread_over(value, axes, count, groups=None):
    return swap(jnp.broadcast_to(value[None], (count, *value.shape)), axes, groups)


def gather_group(rows):
    across_x = by_x(rows)
    return rows, across_x, by_core(rows), by_core(across_x)


def reduce_group(keep, send):
    count, depth = keep.shape[0] // 2, keep.shape[1]
    shape = (count, depth)
    own, send = call(add_kernel, ((shape, F32), (shape, BF)), (keep, by_core(send)), "add", 1e6)
    return own, by_x(send)


def stack_rows(*values):
    blank = jnp.zeros_like(values[0])
    return jnp.stack([*values, *[blank] * (8 - len(values))])


def in_order(blocks):
    index = lax.axis_index("head")
    own, across_x, across_core, across = blocks
    odd, far = index % 2 == 1, index // 2 == 1
    near = [jnp.where(odd, q, p) for p, q in ((own, across_core), (across_core, own))]
    wide = [jnp.where(odd, q, p) for p, q in ((across_x, across), (across, across_x))]
    return jnp.stack(
        [jnp.where(far, q, p) for p, q in zip(near + wide, wide + near)]
    )


def to_group(blocks):
    index = lax.axis_index("head")

    def block(offset):
        return lax.dynamic_index_in_dim(blocks, index ^ offset, 0, keepdims=False)

    across = lax.ppermute(block(3), "head", [(i, i ^ 3) for i in range(4)])
    return in_order((block(0), by_x(block(2)), by_core(block(1)), across))


def key_ranges(spans, bq, bk):
    return spans[0, ::bq] // bk, cdiv(spans[1, bq - 1 :: bq], bk)


def local(
    inputs,
    doc_lengths,
    grad_out,
    qkv_weight,
    out_weight,
    inner_weight,
    outer_weight,
    bias_rows,
    inner_bias,
    norm_gains,
    norm_shifts,
):
    micro, tokens, depth = inputs.shape
    groups, cycle = lax.axis_size("head"), lax.axis_size("blk")
    halves = cycle // 2
    devices = groups * cycle
    length = devices * tokens
    hd = depth // HEADS
    heads_dev = HEADS // groups
    rows_dev = qkv_weight.shape[1]
    ff_dev = outer_weight.shape[0]
    ff_part = cycle * ff_dev
    half_tokens = tokens // 2
    head_index = lax.axis_index("head")
    blk_index = lax.axis_index("blk")
    half = blk_index // halves
    unit_head = head_index * heads_dev + jnp.minimum(blk_index % halves, heads_dev - 1)
    unit_of = [min(i, heads_dev - 1) for i in range(halves)]

    own_x = lax.dynamic_index_in_dim(inputs, half, 0, keepdims=False)
    other_x = lax.dynamic_index_in_dim(inputs, 1 - half, 0, keepdims=False)
    got_x = lax.ppermute(other_x, "blk", [(i, (i + halves) % cycle) for i in range(cycle)])
    pair_x = jnp.concatenate([own_x, got_x], axis=0)
    cube = [
        [h * cycle + b for h in (c, c + 2) for b in range(s * halves, (s + 1) * halves)]
        for c in range(2)
        for s in range(2)
    ]
    inner_own = inner_weight.reshape(rows_dev, groups, ff_part)
    inner_own = to_group(inner_own.transpose(1, 0, 2)).reshape(groups * rows_dev, ff_part)
    ffn = jnp.concatenate([inner_own, outer_weight, out_weight])

    units = tuple(h * heads_dev + u for h in range(groups) for u in unit_of)
    (slots,) = call(
        functools.partial(head_slots_kernel, units=units),
        (((groups * halves, 2, rows_dev, 2 * hd), BF),),
        (qkv_weight, bias_rows, norm_gains, norm_shifts, inner_bias.reshape(rows_dev, -1)),
        "head_slots",
        1e6,
        params=LARGE,
    )
    half_groups = [
        [h * cycle + b for h in range(groups) for b in range(n * halves, (n + 1) * halves)]
        for n in range(2)
    ]
    slots, pair_x = lax.optimization_barrier((swap(slots, BOTH, half_groups), pair_x))
    far_slots = lax.ppermute(slots, "blk", [(i, (i + halves) % cycle) for i in range(cycle)])
    near, far = [v.reshape(groups, halves, 2, rows_dev, 2 * hd) for v in (slots, far_slots)]
    both = jnp.stack([jnp.where(half == 0, near, far), jnp.where(half == 0, far, near)], axis=1)
    qk_weight = both[:, :, :, 0].reshape(depth, 2 * hd)
    v_weight = both[:, :, :, 1].reshape(depth, 2 * hd)
    small = both[:, :, :, 1, :, hd : hd + 12].astype(F32).reshape(depth, 12).T

    bias, gains, shifts = small[0:4], small[4:6], small[6:8]
    inner_bias_all = small[8:12].T.reshape(groups, ff_part)
    inner_bias_part = lax.dynamic_index_in_dim(inner_bias_all, head_index, 0, keepdims=False)
    unit_bias = lax.dynamic_slice(bias[0:2], (0, unit_head * hd), (2, hd))
    unit_bias = jnp.pad(unit_bias, ((0, 0), (0, hd)))

    qkv_all = lax.all_gather(after(qkv_weight, ffn), BOTH, axis=0, tiled=False)
    ffn_all = lax.all_gather(after(ffn, slots), "blk", axis=0, tiled=False)
    lengths = lax.dynamic_index_in_dim(doc_lengths, half, 0, keepdims=False)
    order = jnp.arange(lengths.shape[0], dtype=jnp.int32)
    bounds = jnp.sum(jnp.where(order[None, :] <= order[:, None], lengths[None, :], 0), axis=1)
    positions = jnp.arange(length, dtype=jnp.int32)[None, :]
    starts = (bounds - lengths)[:, None]
    own = (positions >= starts) & (positions < bounds[:, None])
    spans = jnp.stack(
        [
            jnp.sum(jnp.where(own, starts, 0), axis=0),
            jnp.sum(jnp.where(own, bounds[:, None], 0), axis=0),
        ]
    )

    place = jnp.stack([head_index % 2, half]).astype(jnp.int32)
    block = 512 if length <= 4096 else 256
    ranges = key_ranges(spans, block, 512), key_ranges(spans, 512, 256)
    small_rows = (
        stack_rows(bias[2], gains[0], shifts[0]),
        stack_rows(gains[0], shifts[0], bias[3], gains[1], shifts[1]),
        stack_rows(gains[0]),
        inner_bias_part[None],
    )
    tokens_a = spread_over(pair_x, BOTH, cycle, cube)
    prepared = (qk_weight, v_weight, unit_bias, spans, place, ranges)
    tokens_a, prepared = lax.optimization_barrier((tokens_a, prepared))
    qk_weight, v_weight, unit_bias, spans, place, ranges = prepared
    tokens_b = by_core(tokens_a)

    per = max(1, 256 // tokens)
    q, k, v, kt, vt = project(
        place, tokens_a, tokens_b, qk_weight, v_weight, unit_bias, halves, per
    )
    lo, hi = ranges[0]
    attn_out, attn_t, lse = attend(lo, hi, q, k, vt, spans, tokens, block, 512)

    ffn = after(ffn_all, attn_out)
    inner_part = (
        ffn[:, : groups * rows_dev]
        .reshape(cycle, groups, rows_dev, ff_part)
        .transpose(1, 0, 2, 3)
        .reshape(depth, ff_part)
    )
    last = groups * rows_dev + ff_dev
    outer_part = ffn[:, groups * rows_dev : last].reshape(ff_part, depth)
    out_part = ffn[:, last:].reshape(depth // groups, depth)
    attn_slots = swap(attn_out, BOTH)
    out_x, attn_slots, inner_part, outer_part, small_rows = lax.optimization_barrier(
        (by_x(out_part), attn_slots, inner_part, outer_part, small_rows)
    )
    out_all = in_order((out_part, out_x, by_core(out_part), by_core(out_x))).reshape(depth, depth)

    rows = micro * tokens
    layout = (groups, micro, halves, heads_dev)
    flat, group = (rows, depth), (groups * rows, ff_part)
    attn, normed_low, normed_one, inverse_one = call(
        functools.partial(branch_kernel, layout=layout),
        ((flat, BF), (flat, BF), (flat, F32), ((rows, 1), F32)),
        (attn_slots, inputs.reshape(flat), out_all, small_rows[0]),
        "branch",
        1e6,
    )
    act_low, slope, normed_group, keep, send = call(
        inner_kernel,
        ((group, BF), (group, F32), ((groups * rows, depth), BF), ((2 * rows, depth), F32), ((2 * rows, depth), BF)),
        (*gather_group(normed_low), inner_part, outer_part, small_rows[3]),
        "inner",
        1e6,
    )
    output, d_second, d_ffn, sums_two = call(
        output_kernel,
        ((flat, BF), (flat, F32), (flat, BF), ((8, depth), F32)),
        (
            *reduce_group(keep, send),
            normed_one,
            grad_out.reshape(flat),
            small_rows[1],
        ),
        "output",
        1e6,
    )
    output = output.reshape(inputs.shape)
    d_inner, d_ffn_group, inner_sums, keep, send = call(
        inner_back_kernel,
        ((group, BF), ((groups * rows, depth), BF), ((1, ff_part), F32), ((2 * rows, depth), F32), ((2 * rows, depth), BF)),
        (*gather_group(d_ffn), inner_part, outer_part, slope),
        "inner_back",
        1e6,
    )
    own, got = reduce_group(keep, send)
    (ffn_grad,) = call(
        feed_grad_kernel,
        (((cycle, 2 * groups, rows_dev, depth), BF),),
        (normed_group, d_inner, act_low, d_ffn_group),
        "feed_grad",
        1e6,
        [pltpu.VMEM((depth, depth), F32)],
    )
    got, ffn_grad = lax.optimization_barrier((got, ffn_grad))
    d_first, d_branch, sums_one, d_heads = call(
        functools.partial(branch_back_kernel, layout=layout),
        ((flat, F32), (flat, BF), ((8, depth), F32), ((devices, half_tokens, 2 * hd), BF)),
        (
            own,
            got,
            d_second,
            normed_one,
            inverse_one,
            out_all,
            small_rows[2],
        ),
        "branch_back",
        1e6,
    )
    d_heads = swap(d_heads, BOTH)

    ffn_grad = lax.psum_scatter(ffn_grad, "blk", scatter_dimension=0, tiled=False)
    outer_grad = ffn_grad[groups:].reshape(ff_dev, depth).astype(F32)
    inner_grad = to_group(ffn_grad[:groups])
    inner_grad = inner_grad.transpose(1, 0, 2).reshape(rows_dev, groups * ff_part).astype(F32)
    out_grad = dot(attn, d_branch, TN).reshape(groups, depth // groups, depth)

    def out_block(offset):
        return lax.dynamic_index_in_dim(out_grad, head_index ^ offset, 0, keepdims=False)

    from_core = by_core(jnp.stack([out_block(1), out_block(3)]).astype(BF)).astype(F32)
    from_x = by_x((out_block(2) + from_core[1]).astype(BF)).astype(F32)
    out_grad = (out_block(0) + from_core[0] + from_x).astype(BF)
    out_terms = swap(out_grad.reshape(cycle, rows_dev, depth), "blk")
    out_grad = jnp.sum(
        out_terms.astype(F32), axis=0
    )

    lo, hi = ranges[1]
    qkv_out, qkv_t, qv_sums = attend_back(
        lo, hi, q, k, v, kt, attn_t, lse, d_heads, spans, tokens, 512, 256
    )
    qkv_home = swap(after(qkv_out, out_terms), BOTH)
    qkv_all = qkv_all.transpose(1, 0, 2, 3).reshape(3, depth, depth)
    (grad_inputs,) = call(
        functools.partial(tokens_kernel, layout=layout),
        ((flat, BF),),
        (qkv_home, qkv_all, d_first),
        "tokens",
        1e6,
        [pltpu.VMEM((3, rows, depth), BF)],
    )
    grad_inputs = grad_inputs.reshape(inputs.shape)

    unit_grad = weight_grad(place, tokens_a, tokens_b, qkv_t, halves, per)
    wide = jnp.zeros((2, HEADS, hd), F32)
    wide = lax.dynamic_update_slice(wide, qv_sums.reshape(2, 1, hd), (0, unit_head, 0))
    wide = jnp.where((blk_index % halves < heads_dev), wide, 0.0)
    sums = jnp.stack(
        [wide[0].reshape(depth), wide[1].reshape(depth), sums_one[2], sums_two[2]]
        + [sums_one[0], sums_two[0], sums_one[1], sums_two[1]]
    ).T
    inner_sums = inner_sums.reshape(1, cycle, rows_dev, ff_dev // rows_dev)
    inner_sums = jnp.broadcast_to(inner_sums, (groups, *inner_sums.shape[1:]))
    extra = jnp.concatenate(
        [
            sums.reshape(devices, rows_dev, 8),
            inner_sums.reshape(devices, rows_dev, -1),
        ],
        axis=2,
    ).astype(BF)
    extra = jnp.pad(extra, ((0, 0), (0, 0), (0, hd - extra.shape[2])))
    final = jnp.concatenate([unit_grad.reshape(devices, rows_dev, 3 * hd), extra], axis=2)
    final = after(swap(after(final, qkv_home), BOTH), grad_inputs)
    qkv_grad, bias_grad, gains_grad, shifts_grad, inner_bias_grad = call(
        functools.partial(collect_kernel, layout=layout),
        (
            ((3, rows_dev, depth), F32),
            ((4, rows_dev), F32),
            ((2, rows_dev), F32),
            ((2, rows_dev), F32),
            ((rows_dev, hd), F32),
        ),
        (head_index[None], final),
        "collect",
        1e6,
    )
    return (
        output,
        grad_inputs,
        qkv_grad,
        out_grad,
        inner_grad,
        outer_grad,
        bias_grad,
        inner_bias_grad[:, 8 : 8 + ff_dev // rows_dev].reshape(ff_dev),
        gains_grad,
        shifts_grad,
    )


def solution(mesh):
    tokens = P(None, BOTH, None)
    rows = P(BOTH, None)
    columns = P(None, BOTH)
    return jax.shard_map(
        local,
        mesh=mesh,
        in_specs=(tokens, P(), tokens, tokens, rows, rows, rows, columns, P(BOTH), columns, columns),
        out_specs=(tokens, tokens, tokens, rows, rows, rows, columns, P(BOTH), columns, columns),
        check_vma=False,
    )
```
